128 devices in a mesh: dp: 32 (over y, z, core), tensor: 4 (over x).
Axes of the slice: x: 4, y: 4, z: 4, core: 2. Of those that a mesh axis runs over, the one named last changes fastest.
Arguments:
- tokens: bfloat16 [32768, 768], P('dp'), may hold values from -6 to 6
- cotangent: bfloat16 [32768, 768], P('dp'), may hold values from -6 to 6
- seq_len: int32 [64], replicated, may hold values from 1 to 512
- seq_slot: int32 [64], replicated, may hold values from 0 to 63, as said below
- attn_gain: float32 [768], replicated, may hold values from 0.25 to 1.75
- w_query: bfloat16 [768, 768], P(None, 'tensor'), may hold values from -0.21875 to 0.21875
- w_key: bfloat16 [768, 768], P(None, 'tensor'), may hold values from -0.21875 to 0.21875
- w_value: bfloat16 [768, 768], P(None, 'tensor'), may hold values from -0.21875 to 0.21875
- w_attn_out: bfloat16 [768, 768], P('tensor'), may hold values from -1.5 to 1.5
- mlp_gain: float32 [768], replicated, may hold values from 0.25 to 1.75
- w_in: bfloat16 [768, 1152], P(None, 'tensor'), may hold values from -0.21875 to 0.21875
- w_gate: bfloat16 [768, 1152], P(None, 'tensor'), may hold values from -0.21875 to 0.21875
- w_down: bfloat16 [1152, 768], P('tensor'), may hold values from -0.25 to 0.25
Outputs:
- mixed_out: bfloat16 [32768, 768], P('dp')
- grad_tokens: float32 [32768, 768], P('dp')
- grad_attn_gain: float32 [768], replicated
- grad_query: float32 [768, 768], P(None, 'tensor')
- grad_key: float32 [768, 768], P(None, 'tensor')
- grad_value: float32 [768, 768], P(None, 'tensor')
- grad_attn_out: float32 [768, 768], P('tensor')
- grad_mlp_gain: float32 [768], replicated
- grad_in: float32 [768, 1152], P(None, 'tensor')
- grad_gate: float32 [768, 1152], P(None, 'tensor')
- grad_down: float32 [1152, 768], P('tensor')
The draws below stay inside these ranges and needn't reach their ends.
Inputs may be any that keep to these rules, and one draw needn't show every extreme that they name: seq_slot is a permutation: sequence i sits in data group seq_slot[i] // 2, in place seq_slot[i] % 2. Every data group's lengths sum to at most 1024, and some group's sequences all have length 512.
All inputs are finite; a program needn't handle non-finite values.
Results may differ from the reference program's by a relative error of at most 0.015.
The reference program's roundings to bfloat16 on the way count: a program that leaves them out, or rounds other values in their place, can miss the bound.
Values sent between devices are 32-bit elements; how exact they have to be, the bound alone decides.
No kernel may reach another device: no remote copies, remote signals or barrier semaphores. Data moves between devices by JAX's collectives and lax.ppermute only.
A program may use at most 128 MiB of HBM per device.

```python
import jax
import jax.numpy as jnp
from jax import lax

D = 768
HEADS = 12
HEAD_DIM = 64
FF = 1152
HALF = 64
TOK_DEV = 1024
SEQ_GRP = 2
MAXLEN = 512
SEQS = 64
TOKENS = 32768
N_DP = 32


def layout_draw(key):
    key_len, key_full, key_perm = jax.random.split(key, 3)
    slot_len = jax.random.randint(key_len, (SEQS,), 1, MAXLEN + 1)
    full_group = jax.random.randint(key_full, (), 0, N_DP)
    group_of = jnp.arange(SEQS) // SEQ_GRP
    slot_len = jnp.where(group_of == full_group, MAXLEN, slot_len)
    slot_of = jax.random.permutation(key_perm, SEQS)
    return (slot_len[slot_of].astype(jnp.int32), slot_of.astype(jnp.int32))


def draw_seq_len(key, part):
    return layout_draw(key)[0]


def draw_seq_slot(key, part):
    return layout_draw(key)[1]


def block_levels(stream_key, extent, shards, smallest, high):
    loudness, own = 1.0, jax.random.fold_in(stream_key, 6)
    for axis_at, shards_of in shards:
        draws = jnp.exp(jax.random.uniform(jax.random.fold_in(own, axis_at), (shards_of,), jnp.float32, smallest / len(shards), high / len(shards)))
        loudness = loudness * jnp.repeat(draws, extent[axis_at] // shards_of).reshape([-1 if axis == axis_at else 1 for axis in range(len(extent))])
    return loudness


def noise(own_key, shape, scale, bound, shards=(), kind=jnp.bfloat16):
    values = scale * jax.random.normal(own_key, shape, jnp.float32)
    if shards:
        values = values * block_levels(own_key, shape, shards, -0.22, 0.18)
    return jnp.clip(values, -bound, bound).astype(kind)


def setup_inputs(seed: int = 0) -> dict:
    key_of = jax.random.split(jax.random.key(seed), 14)
    return {
        "tokens": noise(key_of[0], (TOKENS, D), 1.0, 6.0, ((0, 32),)),
        "cotangent": noise(key_of[1], (TOKENS, D), 1.0, 6.0, ((0, 32),)),
        "seq_len": draw_seq_len(jax.random.fold_in(key_of[13], 71), 0),
        "seq_slot": draw_seq_slot(jax.random.fold_in(key_of[13], 71), 0),
        "attn_gain": jnp.clip(1.0 + 0.15 * jax.random.normal(key_of[4], (D,), jnp.float32), 0.25, 1.75),
        "w_query": noise(key_of[5], (D, D), D ** -0.5, 0.21875, ((1, 4),)),
        "w_key": noise(key_of[6], (D, D), D ** -0.5, 0.21875, ((1, 4),)),
        "w_value": noise(key_of[7], (D, D), D ** -0.5, 0.21875, ((1, 4),)),
        "w_attn_out": noise(key_of[8], (D, D), (D // 48) ** -0.5, 1.5, ((0, 4),)),
        "mlp_gain": jnp.clip(1.0 + 0.15 * jax.random.normal(key_of[9], (D,), jnp.float32), 0.25, 1.75),
        "w_in": noise(key_of[10], (D, FF), D ** -0.5, 0.21875, ((1, 4),)),
        "w_gate": noise(key_of[11], (D, FF), D ** -0.5, 0.21875, ((1, 4),)),
        "w_down": noise(key_of[12], (FF, D), (FF // 2) ** -0.5, 0.25, ((0, 4),)),
    }


@jax.custom_vjp
def low(v):
    return lax.optimization_barrier(v.astype(jnp.bfloat16)).astype(jnp.float32)

@jax.custom_vjp
def low_back(v):
    return v

def low_keep(v):
    return (low(v), None)

def low_pass(kept, grad):
    return (grad,)

def back_keep(v):
    return (v, None)

def back_low(kept, grad):
    return (low(grad),)
low.defvjp(low_keep, low_pass)
low_back.defvjp(back_keep, back_low)

def arrange(lengths, row_count):
    ends = jnp.cumsum(lengths).astype(jnp.int32)
    index = jnp.arange(row_count, dtype=jnp.int32)
    segment = lax.optimization_barrier(jnp.sum((index[:, None] >= ends[None, :]).astype(jnp.int32), axis=1))
    starts = jnp.concatenate([jnp.zeros((1,), jnp.int32), ends])
    labels = jnp.arange(starts.shape[0], dtype=jnp.int32)
    picked = lax.optimization_barrier(jnp.sum(jnp.where(segment[:, None] == labels[None, :], starts[None, :], 0), axis=1))
    return (segment, index - picked)

def normed(values, gain):
    centre = lax.optimization_barrier(jnp.mean(values, axis=-1, keepdims=True))
    centred = values - centre
    spread = lax.optimization_barrier(jnp.mean(centred * centred, axis=-1, keepdims=True))
    return centred * lax.rsqrt(spread + 1e-05) * gain

def angles_of(position, head_dim):
    width = head_dim // 2
    frequency = 10000.0 ** (-(jnp.arange(width, dtype=jnp.float32) * 2.0 / head_dim))
    phase = position.astype(jnp.float32)[:, None] * frequency[None, :]
    return (jnp.cos(phase)[:, None, :], jnp.sin(phase)[:, None, :])

def rotate(vector, cosine, sine):
    width = vector.shape[-1] // 2
    first = vector[..., :width]
    second = vector[..., width:]
    return jnp.concatenate([first * cosine - second * sine, second * cosine + first * sine], axis=-1)

def matmul(left, right):
    return jnp.dot(left, right, precision=lax.Precision.HIGHEST, preferred_element_type=jnp.float32)

def layer_rows(inputs, segment, position, params):
    attn_gain, w_query, w_key, w_value, w_attn_out, mlp_gain, w_in, w_gate, w_down = params
    row_count = inputs.shape[0]
    normed1 = low(normed(inputs, attn_gain))
    query_pre = low_back(matmul(normed1, w_query)).reshape(row_count, HEADS, HEAD_DIM)
    key_pre = low_back(matmul(normed1, w_key)).reshape(row_count, HEADS, HEAD_DIM)
    value_pre = low_back(matmul(normed1, w_value)).reshape(row_count, HEADS, HEAD_DIM)
    cosine, sine = angles_of(position, HEAD_DIM)
    query = low(rotate(query_pre, cosine, sine))
    keys = low(rotate(key_pre, cosine, sine))
    values = low(value_pre)
    scale = 1.0 / HEAD_DIM ** 0.5
    scores = jnp.einsum('qhd,khd->hqk', query, keys, precision=lax.Precision.HIGHEST) * scale
    scores = low_back(scores)
    index = jnp.arange(row_count, dtype=jnp.int32)
    allowed = (segment[:, None] == segment[None, :]) & (jnp.abs(index[:, None] - index[None, :]) <= HALF)
    scores = jnp.where(allowed[None], scores, -1e+30)
    row_max = lax.optimization_barrier(jnp.max(scores, axis=-1, keepdims=True))
    expo = jnp.exp(scores - row_max)
    prob = expo / lax.optimization_barrier(jnp.sum(expo, axis=-1, keepdims=True))
    mixed = jnp.einsum('hqk,khd->qhd', low(prob), values, precision=lax.Precision.HIGHEST)
    attn_mix = low(low_back(mixed.reshape(row_count, HEADS * HEAD_DIM)))
    resid = inputs + low_back(matmul(attn_mix, w_attn_out))
    normed2 = low(normed(resid, mlp_gain))
    up_part = low_back(matmul(normed2, w_in))
    gate_part = low_back(matmul(normed2, w_gate))
    hidden = low(jax.nn.gelu(up_part, approximate=False) * gate_part)
    return resid + low_back(matmul(hidden, w_down))

def reference(tokens, cotangent, seq_len, seq_slot, attn_gain, w_query, w_key, w_value, w_attn_out, mlp_gain, w_in, w_gate, w_down):
    slots = jnp.arange(SEQS, dtype=jnp.int32).reshape(N_DP, SEQ_GRP)
    lengths = lax.optimization_barrier(jnp.sum(jnp.where(seq_slot[None, None, :] == slots[:, :, None], seq_len[None, None, :], 0), axis=-1)).astype(jnp.int32)
    segment, position = jax.vmap(lambda group_len: arrange(group_len, TOK_DEV))(lengths)
    live = (segment < SEQ_GRP).astype(jnp.float32).reshape(TOKENS, 1)
    inputs = tokens.astype(jnp.float32)
    weights = (attn_gain.astype(jnp.float32), w_query.astype(jnp.float32), w_key.astype(jnp.float32), w_value.astype(jnp.float32), w_attn_out.astype(jnp.float32), mlp_gain.astype(jnp.float32), w_in.astype(jnp.float32), w_gate.astype(jnp.float32), w_down.astype(jnp.float32))

    def forward(rows_all, *params):
        grouped = rows_all.reshape(N_DP, TOK_DEV, D)
        step = jax.checkpoint(lambda item: layer_rows(item[0], item[1], item[2], params))
        result = lax.map(step, (grouped, segment, position))
        return result.reshape(TOKENS, D)
    output, pullback = jax.vjp(forward, inputs, *weights)
    grads = pullback(cotangent.astype(jnp.float32) * live)
    return (output.astype(jnp.bfloat16), grads[0], grads[1], grads[2], grads[3], grads[4], grads[5], grads[6], grads[7], grads[8], grads[9])
```

```python
import jax
import jax.numpy as jnp
from jax import lax
from jax.experimental import pallas as pl
from jax.experimental.pallas import tpu as pltpu
from jax.sharding import PartitionSpec as P

HEAD_DIM = 64
HALF = 64
QB = 128
KB = QB + 2 * HALF
PAIR = 2 * HEAD_DIM
F32 = jnp.float32
BF16 = jnp.bfloat16
VMEM_LIMIT = 48 * 1024 * 1024


def dot(a, b):
    return jnp.dot(a, b, preferred_element_type=F32)


def inner_rows(left, right):
    return lax.dot_general(left, right, (((0,), (0,)), ((), ())), preferred_element_type=F32)


def outer_cols(left, right):
    return lax.dot_general(left, right, (((1,), (1,)), ((), ())), preferred_element_type=F32)


def normed(values, gain):
    centre = jnp.mean(values, axis=-1, keepdims=True)
    centred = values - centre
    spread = jnp.mean(centred * centred, axis=-1, keepdims=True)
    return centred * lax.rsqrt(spread + 1e-05) * gain


def norm_back(values, gain, grad):
    centre = jnp.mean(values, axis=-1, keepdims=True)
    centred = values - centre
    spread = jnp.mean(centred * centred, axis=-1, keepdims=True)
    inv = lax.rsqrt(spread + 1e-05)
    unit = centred * inv
    scaled = grad * gain
    first = jnp.mean(scaled, axis=-1, keepdims=True)
    second = jnp.mean(scaled * unit, axis=-1, keepdims=True)
    return inv * (scaled - first - unit * second), grad * unit


def swap_halves(v):
    lane = lax.broadcasted_iota(jnp.int32, v.shape, 1)
    low_half = lax.rem(lane, HEAD_DIM) < HEAD_DIM // 2
    return jnp.where(low_half, pltpu.roll(v, PAIR - HEAD_DIM // 2, 1), pltpu.roll(v, HEAD_DIM // 2, 1))


def rope(v, cos, sin):
    return v * cos + swap_halves(v) * sin


def write_qkv(n, w_ref, cos_ref, sin_ref, q_ref, k_ref, v_ref):
    count = w_ref.shape[1] // 3

    def weight(part):
        return jnp.concatenate([w_ref[r, part * count : (part + 1) * count, :] for r in range(w_ref.shape[0])], axis=0)

    cos, sin = cos_ref[...], sin_ref[...]
    q = outer_cols(n, weight(0))
    k = outer_cols(n, weight(1))
    for j in range(q.shape[1] // PAIR):
        cols = slice(j * PAIR, (j + 1) * PAIR)
        q_ref[:, cols] = (rope(q[:, cols], cos, sin) * (1.0 / HEAD_DIM**0.5)).astype(BF16)
        k_ref[:, cols] = rope(k[:, cols], cos, sin).astype(BF16)
    v_ref[...] = outer_cols(n, weight(2)).astype(BF16)


def norm_qkv_kernel(x_ref, gain_ref, w_ref, cos_ref, sin_ref, n_ref, q_ref, k_ref, v_ref):
    n = normed(x_ref[...].astype(F32), gain_ref[...]).astype(BF16)
    n_ref[...] = n
    write_qkv(n, w_ref, cos_ref, sin_ref, q_ref, k_ref, v_ref)


def only_qkv_kernel(n_ref, w_ref, cos_ref, sin_ref, q_ref, k_ref, v_ref):
    write_qkv(n_ref[...], w_ref, cos_ref, sin_ref, q_ref, k_ref, v_ref)


def project_qkv(rows_in, gain, pack, cos, sin):
    rows, width = rows_in.shape
    cols = pack.shape[0] * pack.shape[1] // 3
    block = 256
    row_spec = pl.BlockSpec((block, width), lambda i: (i, 0))
    out_spec = pl.BlockSpec((block, cols), lambda i: (i, 0))
    gain_spec = pl.BlockSpec((1, width), lambda i: (0, 0))
    w_spec = pl.BlockSpec(pack.shape, lambda i: (0, 0, 0))
    tab_spec = pl.BlockSpec((block, PAIR), lambda i: (i, 0))
    first = gain is not None
    return pl.pallas_call(
        norm_qkv_kernel if first else only_qkv_kernel,
        grid=(rows // block,),
        in_specs=[row_spec] + [gain_spec] * first + [w_spec, tab_spec, tab_spec],
        out_specs=[row_spec] * first + [out_spec] * 3,
        out_shape=[jax.ShapeDtypeStruct((rows, width), BF16)] * first + [jax.ShapeDtypeStruct((rows, cols), BF16)] * 3,
        compiler_params=pltpu.CompilerParams(vmem_limit_bytes=VMEM_LIMIT),
        cost_estimate=pl.CostEstimate(
            flops=8 * rows * width * cols, bytes_accessed=8 * rows * width + 6 * width * cols, transcendentals=0
        ),
        name="norm_qkv" if first else "qkv",
    )(*([rows_in] + [gain] * first + [pack, cos, sin]))


def pad_rows(dst, src):
    rows = src.shape[0]
    edge = jnp.zeros((HALF, PAIR), dst.dtype)
    dst[0:HALF, :] = edge
    dst[HALF : HALF + rows, :] = src
    dst[HALF + rows : rows + 2 * HALF, :] = edge


def split_lanes(src, first, second):
    lane = lax.broadcasted_iota(jnp.int32, src.shape, 1)
    zero = jnp.zeros_like(src)
    first[...] = jnp.where(lane < HEAD_DIM, src, zero)
    second[...] = jnp.where(lane < HEAD_DIM, zero, src)


def split_sublanes(src, first, second):
    zero = jnp.zeros((HEAD_DIM, src.shape[1]), src.dtype)
    first[0:HEAD_DIM, :] = src[0:HEAD_DIM, :]
    first[HEAD_DIM:PAIR, :] = zero
    second[0:HEAD_DIM, :] = zero
    second[HEAD_DIM:PAIR, :] = src[HEAD_DIM:PAIR, :]


def attend_kernel(q_ref, k_ref, v_ref, bias_ref, o_ref, p_ref, pad, kt0, kt1, v0, v1):
    rows = q_ref.shape[0]
    pad_rows(pad, k_ref[...])
    split_sublanes(pad[...].T, kt0, kt1)
    pad_rows(pad, v_ref[...])
    split_lanes(pad[...], v0, v1)
    for i in range(rows // QB):
        win = slice(i * QB, i * QB + KB)
        q = q_ref[i * QB : (i + 1) * QB, :]
        out = None
        for h, (kt, v) in enumerate(((kt0, v0), (kt1, v1))):
            s = dot(q, kt[:, win]) + bias_ref[i]
            e = jnp.exp(s - jnp.max(s, axis=-1, keepdims=True))
            p = (e * (1.0 / jnp.sum(e, axis=-1, keepdims=True))).astype(BF16)
            p_ref[0, i, h] = p
            part = dot(p, v[win, :])
            out = part if out is None else out + part
        o_ref[i * QB : (i + 1) * QB, :] = out.astype(BF16)


def attend(q, k, v, bias):
    rows, width = q.shape
    pairs, blocks = width // PAIR, rows // QB
    spec = pl.BlockSpec((rows, PAIR), lambda j: (0, j))
    padded = rows + 2 * HALF
    return pl.pallas_call(
        attend_kernel,
        grid=(pairs,),
        in_specs=[spec, spec, spec, pl.BlockSpec((blocks, QB, KB), lambda j: (0, 0, 0))],
        out_specs=[spec, pl.BlockSpec((1, blocks, 2, QB, KB), lambda j: (j, 0, 0, 0, 0))],
        out_shape=[
            jax.ShapeDtypeStruct((rows, width), BF16),
            jax.ShapeDtypeStruct((pairs, blocks, 2, QB, KB), BF16),
        ],
        scratch_shapes=[
            pltpu.VMEM((padded, PAIR), BF16),
            pltpu.VMEM((PAIR, padded), BF16),
            pltpu.VMEM((PAIR, padded), BF16),
            pltpu.VMEM((padded, PAIR), BF16),
            pltpu.VMEM((padded, PAIR), BF16),
        ],
        compiler_params=pltpu.CompilerParams(vmem_limit_bytes=VMEM_LIMIT),
        cost_estimate=pl.CostEstimate(flops=2 * 10**9 * pairs, bytes_accessed=2 * rows * width * 8, transcendentals=0),
        name="attend",
    )(q, k, v, bias)


def attend_back_kernel(
    q_ref, k_ref, v_ref, g_ref, p_ref, cos_ref, sin_ref, gq_ref, gk_ref, gv_ref, pad, vt0, vt1, k0, k1, gkt, gvt
):
    rows = q_ref.shape[0]
    scale = 1.0 / HEAD_DIM**0.5
    pad_rows(pad, v_ref[...])
    split_sublanes(pad[...].T, vt0, vt1)
    pad_rows(pad, k_ref[...])
    split_lanes(pad[...], k0, k1)
    gkt[...] = jnp.zeros_like(gkt)
    gvt[...] = jnp.zeros_like(gvt)
    for i in range(rows // QB):
        win = slice(i * QB, i * QB + KB)
        at = slice(i * QB, (i + 1) * QB)
        g = g_ref[at, :]
        g_t = g.T
        q_t = q_ref[at, :].T
        out = None
        for h, (vt, k) in enumerate(((vt0, k0), (vt1, k1))):
            head = slice(h * HEAD_DIM, (h + 1) * HEAD_DIM)
            p_low = p_ref[0, i, h]
            p = p_low.astype(F32)
            gp = dot(g, vt[:, win])
            weighted = jnp.sum(p * gp, axis=-1, keepdims=True)
            gs = (p * (gp - weighted)).astype(BF16)
            part = dot(gs, k[win, :])
            out = part if out is None else out + part
            gkt[head, win] += dot(q_t[head, :], gs)
            gvt[head, win] += dot(g_t[head, :], p_low)
        gq_ref[at, :] = rope(out * scale, cos_ref[at, :], -sin_ref[at, :]).astype(BF16)
    gk = gkt[...].T[HALF : HALF + rows, :]
    gk_ref[...] = rope(gk, cos_ref[...], -sin_ref[...]).astype(BF16)
    gv_ref[...] = gvt[...].T[HALF : HALF + rows, :].astype(BF16)


def attend_back(q, k, v, g, prob, cos, sin):
    rows, width = q.shape
    pairs, blocks = width // PAIR, rows // QB
    spec = pl.BlockSpec((rows, PAIR), lambda j: (0, j))
    tab_spec = pl.BlockSpec((rows, PAIR), lambda j: (0, 0))
    padded = rows + 2 * HALF
    return pl.pallas_call(
        attend_back_kernel,
        grid=(pairs,),
        in_specs=[spec] * 4 + [pl.BlockSpec((1, blocks, 2, QB, KB), lambda j: (j, 0, 0, 0, 0)), tab_spec, tab_spec],
        out_specs=[spec] * 3,
        out_shape=[jax.ShapeDtypeStruct((rows, width), BF16)] * 3,
        scratch_shapes=[
            pltpu.VMEM((padded, PAIR), BF16),
            pltpu.VMEM((PAIR, padded), BF16),
            pltpu.VMEM((PAIR, padded), BF16),
            pltpu.VMEM((padded, PAIR), BF16),
            pltpu.VMEM((padded, PAIR), BF16),
            pltpu.VMEM((PAIR, padded), F32),
            pltpu.VMEM((PAIR, padded), F32),
        ],
        compiler_params=pltpu.CompilerParams(vmem_limit_bytes=VMEM_LIMIT),
        cost_estimate=pl.CostEstimate(flops=3 * 10**9 * pairs, bytes_accessed=2 * rows * width * 10, transcendentals=0),
        name="attend_back",
    )(q, k, v, g, prob, cos, sin)


def ring(step):
    size = lax.axis_size("tensor")
    return [(i, (i + step) % size) for i in range(size)]


def plane(dy, dz, dc=0):
    size = lax.axis_size("dp")
    out = []
    for i in range(size):
        y, z, c = i // 8, (i // 2) % 4, i % 2
        out.append((i, (((y + dy) % 4) * 4 + (z + dz) % 4) * 2 + (c + dc) % 2))
    return out


def place_pair_kernel(core_ref, own_ref, mine_ref, other_ref, out_ref):
    half = mine_ref.shape[1]
    out_ref[0] = own_ref[...]
    core = core_ref[0]
    out_ref[1, :, pl.ds(pl.multiple_of(core * half, half), half)] = mine_ref[...].astype(BF16)
    out_ref[1, :, pl.ds(pl.multiple_of((1 - core) * half, half), half)] = other_ref[...].astype(BF16)


def place_rest_kernel(core_ref, mine_ref, other_ref, head_ref, tail_ref, other_head_ref, other_tail_ref, out_ref):
    rows, half = mine_ref.shape
    core = core_ref[0]
    mine_at = pl.ds(pl.multiple_of(core * half, half), half)
    other_at = pl.ds(pl.multiple_of((1 - core) * half, half), half)
    out_ref[0, :, mine_at] = mine_ref[...].astype(BF16)
    out_ref[0, :, other_at] = other_ref[...].astype(BF16)
    out_ref[1, 0 : rows // 2, mine_at] = head_ref[...].astype(BF16)
    out_ref[1, rows // 2 : rows, mine_at] = tail_ref[...].astype(BF16)
    out_ref[1, 0 : rows // 2, other_at] = other_head_ref[...].astype(BF16)
    out_ref[1, rows // 2 : rows, other_at] = other_tail_ref[...].astype(BF16)


def place(kernel, core, rows, lanes, args, name):
    whole = pl.BlockSpec(memory_space=pltpu.VMEM)
    return pl.pallas_call(
        kernel,
        in_specs=[pl.BlockSpec(memory_space=pltpu.SMEM)] + [whole] * len(args),
        out_specs=whole,
        out_shape=jax.ShapeDtypeStruct((2, rows, lanes), BF16),
        compiler_params=pltpu.CompilerParams(vmem_limit_bytes=VMEM_LIMIT),
        name=name,
    )(core[None].astype(jnp.int32), *args)


def gather_attn(w_query, w_key, w_value):
    core = lax.axis_index("dp") % 2
    own = jnp.concatenate([w_query.T, w_key.T, w_value.T], axis=0)
    rows, lanes = own.shape
    half = lanes // 2
    mine = lax.dynamic_slice_in_dim(own, core * half, half, 1).astype(F32)
    swap = plane(0, 0, 1)
    after = lax.ppermute(mine, "tensor", ring(-1))
    before = lax.ppermute(mine, "tensor", ring(1))
    head = lax.ppermute(after[: rows // 2], "tensor", ring(-1))
    tail = lax.ppermute(before[rows // 2 :], "tensor", ring(1))
    other_after = lax.ppermute(after, "dp", swap)
    other_before = lax.ppermute(before, "dp", swap)
    first = place(place_pair_kernel, core, rows, lanes, (own, after, other_after), "place_pair")
    other_head = lax.ppermute(head, "dp", swap)
    other_tail = lax.ppermute(tail, "dp", swap)
    rest = place(
        place_rest_kernel, core, rows, lanes, (before, other_before, head, tail, other_head, other_tail), "place_rest"
    )
    return first, rest


def gather_mlp(w_in, w_gate, w_down, w_attn_out):
    at = lax.axis_index("dp")
    core, z, y = at % 2, (at // 2) % 4, at // 8
    half = w_down.shape[1] // 2
    count = w_down.shape[0] // 4
    short = w_attn_out.shape[0] // 4
    tall_in = lax.dynamic_slice(w_in, (core * half, z * count), (half, count)).T
    tall_gate = lax.dynamic_slice(w_gate, (core * half, z * count), (half, count)).T
    down = lax.dynamic_slice(w_down, (z * count, core * half), (count, half))
    out = lax.dynamic_slice(w_attn_out, (z * short, core * half), (short, half))
    out = jnp.pad(out, ((0, count - short), (0, 0)))
    piece = jnp.where(y == 0, tall_in, jnp.where(y == 1, tall_gate, jnp.where(y == 2, down, out))).astype(F32)
    whole = lax.all_gather(piece, ("dp", "tensor"), axis=0, tiled=False)
    return whole.reshape(4, 4, 2, 4, count, half)


def mlp_kernel(
    at_ref,
    w_ref,
    x_ref,
    mix0_ref,
    mix1_ref,
    cot_ref,
    live_ref,
    gain_ref,
    out_ref,
    resid_ref,
    low_ref,
    mixg_ref,
    n_ref,
    hid_ref,
    gup_ref,
    ggt_ref,
    go_ref,
    gain_out_ref,
    up_w,
    gt_w,
    dn_w,
    o_w,
):
    step = pl.program_id(0)
    quarters, halves, count, half = w_ref.shape[1], w_ref.shape[2], w_ref.shape[4], w_ref.shape[5]
    loads = 16
    rank = step % 4

    def load(dst, rows):
        at = pl.ds(pl.multiple_of(rank * (quarters * rows), 16), quarters * rows)
        for c in range(halves):
            block = jnp.concatenate([w_ref[0, z, c, 0, 0:rows, :] for z in range(quarters)], axis=0)
            dst[at, c * half : (c + 1) * half] = block.astype(BF16)

    for kind, (dst, rows) in enumerate(((up_w, count), (gt_w, count), (dn_w, count), (o_w, o_w.shape[0] // 16))):

        @pl.when(step // 4 == kind)
        def _(dst=dst, rows=rows):
            load(dst, rows)

    @pl.when(step >= loads)
    def _():
        split = mix0_ref.shape[1]
        gain = gain_ref[...]
        resid = x_ref[...].astype(F32) + dot(mix0_ref[...], o_w[0:split, :]) + dot(mix1_ref[...], o_w[split:, :])
        centre = jnp.mean(resid, axis=-1, keepdims=True)
        centred = resid - centre
        inv = lax.rsqrt(jnp.mean(centred * centred, axis=-1, keepdims=True) + 1e-05)
        unit = centred * inv
        n = (unit * gain).astype(BF16)
        n_ref[...] = n
        up = outer_cols(n, up_w[...])
        gate = outer_cols(n, gt_w[...])
        go = cot_ref[...].astype(F32) * live_ref[...]
        go_low = go.astype(BF16)
        go_ref[...] = go_low
        gh = outer_cols(go_low, dn_w[...])
        bell = jnp.exp(up * up * -0.5)
        t = 1.0 / (1.0 + (0.3275911 * 0.7071067811865476) * jnp.abs(up))
        poly = t * (
            0.5 * 0.254829592
            + t * (0.5 * -0.284496736 + t * (0.5 * 1.421413741 + t * (0.5 * -1.453152027 + t * (0.5 * 1.061405429))))
        )
        tail = poly * bell
        cdf = jnp.where(up >= 0.0, 1.0 - tail, tail)
        act = up * cdf
        slope = cdf + up * bell * 0.3989422804014327
        hid = (act * gate).astype(BF16)
        gup = (gh * gate * slope).astype(BF16)
        ggt = (gh * act).astype(BF16)
        own = hid_ref.shape[1]
        hid_ref[...] = hid[:, :own]
        gup_ref[...] = gup[:, :own]
        ggt_ref[...] = ggt[:, :own]
        out_ref[...] = (resid + dot(hid, dn_w[...])).astype(BF16)
        gn = dot(gup, up_w[...]) + dot(ggt, gt_w[...])
        scaled = gn * gain
        first = jnp.mean(scaled, axis=-1, keepdims=True)
        second = jnp.mean(scaled * unit, axis=-1, keepdims=True)
        grad = go + inv * (scaled - first - unit * second)
        resid_ref[...] = grad
        low = grad.astype(BF16)
        low_ref[...] = low
        mixg_ref[...] = outer_cols(low, o_w[...]).astype(BF16)
        terms = jnp.sum(gn * unit, axis=0, keepdims=True)

        @pl.when(step == loads)
        def _():
            gain_out_ref[...] = terms

        @pl.when(step > loads)
        def _():
            gain_out_ref[...] += terms


def mlp(weights, tokens, mix0, mix1, cotangent, live, gain):
    rows, width = tokens.shape
    block, loads = 256, 16
    quarters, halves, count, half = weights.shape[1], weights.shape[2], weights.shape[4], weights.shape[5]
    own = quarters * count
    ff = 4 * own

    def at_row(i, _):
        return (jnp.maximum(i - loads, 0), 0)

    def at_weight(i, at):
        step = jnp.minimum(i, loads - 1)
        rank = step % 4
        return (step // 4, 0, 0, (at[0] + (rank ^ (rank >> 1))) % 4, 0, 0)

    def row(cols):
        return pl.BlockSpec((block, cols), at_row)

    def fixed(i, _):
        return (0, 0)

    def shape(cols, kind):
        return jax.ShapeDtypeStruct((rows, cols), kind)

    split = mix0.shape[1]
    return pl.pallas_call(
        mlp_kernel,
        grid_spec=pltpu.PrefetchScalarGridSpec(
            num_scalar_prefetch=1,
            grid=(loads + rows // block,),
            in_specs=[
                pl.BlockSpec((1, quarters, halves, 1, count, half), at_weight),
                row(width),
                row(split),
                row(width - split),
                row(width),
                row(1),
                pl.BlockSpec((1, width), fixed),
            ],
            out_specs=[
                row(width),
                row(width),
                row(width),
                row(width),
                row(width),
                row(own),
                row(own),
                row(own),
                row(width),
                pl.BlockSpec((1, width), fixed),
            ],
            scratch_shapes=[
                pltpu.VMEM((ff, width), BF16),
                pltpu.VMEM((ff, width), BF16),
                pltpu.VMEM((ff, width), BF16),
                pltpu.VMEM((width, width), BF16),
            ],
        ),
        out_shape=[
            shape(width, BF16),
            shape(width, F32),
            shape(width, BF16),
            shape(width, BF16),
            shape(width, BF16),
            shape(own, BF16),
            shape(own, BF16),
            shape(own, BF16),
            shape(width, BF16),
            jax.ShapeDtypeStruct((1, width), F32),
        ],
        compiler_params=pltpu.CompilerParams(vmem_limit_bytes=VMEM_LIMIT),
        cost_estimate=pl.CostEstimate(flops=12 * rows * width * ff, bytes_accessed=40 * 10**6, transcendentals=0),
        name="mlp",
    )(lax.axis_index("tensor")[None].astype(jnp.int32), weights, tokens, mix0, mix1, cotangent, live, gain)


def finish_kernel(x_ref, grad_ref, gain_ref, *refs):
    parts, weights, (out_ref, gain_out_ref) = refs[:6], refs[6:8], refs[8:]
    total = None
    for half in range(2):
        w_ref = weights[half]
        count = w_ref.shape[1] // 3
        for part in range(3):
            w = jnp.concatenate([w_ref[r, part * count : (part + 1) * count, :] for r in range(w_ref.shape[0])], axis=0)
            term = dot(parts[half * 3 + part][...], w)
            total = term if total is None else total + term
    back, terms = norm_back(x_ref[...].astype(F32), gain_ref[...], total)
    out_ref[...] = grad_ref[...] + back
    terms = jnp.sum(terms, axis=0, keepdims=True)

    @pl.when(pl.program_id(0) == 0)
    def _():
        gain_out_ref[...] = terms

    @pl.when(pl.program_id(0) > 0)
    def _():
        gain_out_ref[...] += terms


def finish(tokens, grad_resid, gain, parts, weights):
    rows, width = tokens.shape
    block = 256

    def row(cols):
        return pl.BlockSpec((block, cols), lambda i: (i, 0))

    fixed = pl.BlockSpec((1, width), lambda i: (0, 0))
    return pl.pallas_call(
        finish_kernel,
        grid=(rows // block,),
        in_specs=[row(width), row(width), fixed]
        + [row(p.shape[1]) for p in parts]
        + [pl.BlockSpec(w.shape, lambda i: (0, 0, 0)) for w in weights],
        out_specs=[row(width), fixed],
        out_shape=[jax.ShapeDtypeStruct((rows, width), F32), jax.ShapeDtypeStruct((1, width), F32)],
        compiler_params=pltpu.CompilerParams(vmem_limit_bytes=VMEM_LIMIT),
        cost_estimate=pl.CostEstimate(flops=6 * rows * width * width, bytes_accessed=20 * 10**6, transcendentals=0),
        name="finish",
    )(tokens, grad_resid, gain, *parts, *weights)


def to_peers(blocks, moves):
    return [lax.ppermute(block, "dp", plane(*move)) for block, move in zip(blocks, moves)]


def reduce_late(grads, gains):
    at = lax.axis_index("dp")
    core, z, y = at % 2, (at // 2) % 4, at // 8
    rows = grads.shape[0]
    in_y = [(d, 0) for d in (1, 2, 3)]
    in_z = [(0, d) for d in (1, 2, 3)]
    small = gains().astype(F32) if callable(gains) else gains

    def block_of(array, place, count):
        return lax.dynamic_slice_in_dim(array, place * count, count, 0)

    half = block_of(grads, core, rows // 2) + lax.ppermute(block_of(grads, 1 - core, rows // 2), "dp", plane(0, 0, 1))
    quarter = rows // 8
    got = to_peers([block_of(half, (y + d) % 4, quarter) for d in (1, 2, 3)], in_y)
    mine = block_of(half, y, quarter) + got[0] + got[1] + got[2]
    part = rows // 32
    got = to_peers([block_of(mine, (z + d) % 4, part) for d in (1, 2, 3)], in_z)
    done = block_of(mine, z, part) + got[0] + got[1] + got[2]

    def spread(block, small, moves, place):
        sent = jnp.concatenate([block, small], axis=0)
        got = to_peers([sent] * 3, moves)
        count = block.shape[0]
        small = small + got[0][count:] + got[1][count:] + got[2][count:]
        blocks = [block] + [g[:count] for g in got]
        order = [lax.rem(place - j + 4, 4) for j in range(4)]
        whole = jnp.concatenate([lax.select_n(order[j], *blocks) for j in range(4)], axis=0)
        return whole, small

    done, small = spread(done, small, in_z, z)
    done, small = spread(done, small, in_y, y)
    sent = jnp.concatenate([done, small], axis=0)
    got = lax.ppermute(sent, "dp", plane(0, 0, 1))
    count = done.shape[0]
    small = small + got[count:]
    top = jnp.where(core == 0, done, got[:count])
    low = jnp.where(core == 0, got[:count], done)
    return jnp.concatenate([top, low], axis=0), small


def body(
    tokens,
    cotangent,
    seq_len,
    seq_slot,
    attn_gain,
    w_query,
    w_key,
    w_value,
    w_attn_out,
    mlp_gain,
    w_in,
    w_gate,
    w_down,
):
    rows, width = tokens.shape
    heads_cols = w_query.shape[1]
    per_group = 2
    slots = lax.axis_index("dp") * per_group + jnp.arange(per_group, dtype=jnp.int32)
    lengths = jnp.sum(jnp.where(seq_slot[None, :] == slots[:, None], seq_len[None, :], 0), axis=1)
    end0, end1 = lengths[0], lengths[0] + lengths[1]

    def segment_of(index):
        return (index >= end0).astype(jnp.int32) + (index >= end1).astype(jnp.int32)

    index = lax.broadcasted_iota(jnp.int32, (rows, PAIR), 0)
    position = index - jnp.where(index >= end1, end1, jnp.where(index >= end0, end0, 0))
    lane = lax.broadcasted_iota(jnp.int32, (rows, PAIR), 1)
    width_half = HEAD_DIM // 2
    frequency = 10000.0 ** (-(jnp.arange(width_half, dtype=F32) * 2.0 / HEAD_DIM))
    frequency = jnp.tile(frequency, PAIR // width_half)
    phase = position.astype(F32) * frequency[None, :]
    cos = jnp.cos(phase)
    sin = jnp.where(lane % HEAD_DIM < width_half, -1.0, 1.0) * jnp.sin(phase)
    shape = (rows // QB, QB, KB)
    block_at = lax.broadcasted_iota(jnp.int32, shape, 0) * QB
    row_at = block_at + lax.broadcasted_iota(jnp.int32, shape, 1)
    col_at = block_at + lax.broadcasted_iota(jnp.int32, shape, 2) - HALF
    allowed = (
        (segment_of(row_at) == segment_of(col_at))
        & (jnp.abs(row_at - col_at) <= HALF)
        & (col_at >= 0)
        & (col_at < rows)
    )
    bias = jnp.where(allowed, 0.0, -1e30).astype(F32)
    live = (jnp.arange(rows, dtype=jnp.int32) < end1).astype(F32)

    weights_mlp = gather_mlp(w_in, w_gate, w_down, w_attn_out)
    weights_attn = gather_attn(w_query, w_key, w_value)
    gain1 = attn_gain[None, :]
    normed1, *qkv0 = project_qkv(tokens, gain1, weights_attn[0], cos, sin)
    mix0, prob0 = attend(*qkv0, bias)
    qkv1 = project_qkv(normed1, None, weights_attn[1], cos, sin)
    mix1, prob1 = attend(*qkv1, bias)
    (
        mixed_out,
        grad_resid,
        grad_resid_low,
        grad_mix,
        normed2,
        hidden,
        grad_up,
        grad_gt,
        grad_out_low,
        gain2_sum,
    ) = mlp(weights_mlp, tokens, mix0, mix1, cotangent, live[:, None], mlp_gain[None, :])
    grad_down = inner_rows(hidden, grad_out_low)
    grad_in = inner_rows(normed2, grad_up)
    grad_gate = inner_rows(normed2, grad_gt)
    grad_attn_out = inner_rows(mix0[:, :heads_cols], grad_resid_low)
    early = lax.psum((grad_attn_out, grad_in, grad_gate, grad_down), "dp")
    split = mix0.shape[1]
    back0 = attend_back(*qkv0, grad_mix[:, :split], prob0, cos, sin)
    own_grads = jnp.concatenate([g[:, :heads_cols] for g in back0], axis=1)
    late = inner_rows(normed1, own_grads)
    back1 = attend_back(*qkv1, grad_mix[:, split:], prob1, cos, sin)
    grad_tokens, gain1_sum = finish(tokens, grad_resid, gain1, [*back0, *back1], weights_attn)
    lanes = late.shape[1]
    small = jnp.concatenate([gain1_sum[0], gain2_sum[0]])
    small = jnp.pad(small, (0, 8 * lanes - small.shape[0])).reshape(8, lanes)
    late, small = reduce_late(late, small)
    small = small.reshape(-1)
    return (
        mixed_out,
        grad_tokens,
        small[:width],
        late[:, :heads_cols],
        late[:, heads_cols : 2 * heads_cols],
        late[:, 2 * heads_cols :],
        early[0],
        small[width : 2 * width],
        early[1],
        early[2],
        early[3],
    )


def solution(mesh):
    rows, cols, all_of = P("dp", None), P(None, "tensor"), P()
    tall = P("tensor", None)
    return jax.shard_map(
        body,
        mesh=mesh,
        in_specs=(rows, rows, all_of, all_of, all_of, cols, cols, cols, tall, all_of, cols, cols, tall),
        out_specs=(rows, rows, all_of, cols, cols, cols, tall, all_of, cols, cols, tall),
        check_vma=False,
    )
```

```python
import jax
import jax.numpy as jnp
from jax import lax
from jax.experimental import pallas as pl
from jax.experimental.pallas import tpu as pltpu
from jax.sharding import PartitionSpec as P

HEAD_DIM = 64
HALF = 64
QB = 128
KB = QB + 2 * HALF
PAIR = 2 * HEAD_DIM
F32 = jnp.float32
BF16 = jnp.bfloat16
VMEM_LIMIT = 48 * 1024 * 1024


def dot(a, b):
    return jnp.dot(a, b, preferred_element_type=F32)


def inner_rows(left, right):
    return lax.dot_general(left, right, (((0,), (0,)), ((), ())), preferred_element_type=F32)


def outer_cols(left, right):
    return lax.dot_general(left, right, (((1,), (1,)), ((), ())), preferred_element_type=F32)


def normed(values, gain):
    centre = jnp.mean(values, axis=-1, keepdims=True)
    centred = values - centre
    spread = jnp.mean(centred * centred, axis=-1, keepdims=True)
    return centred * lax.rsqrt(spread + 1e-05) * gain


def norm_back(values, gain, grad):
    centre = jnp.mean(values, axis=-1, keepdims=True)
    centred = values - centre
    spread = jnp.mean(centred * centred, axis=-1, keepdims=True)
    inv = lax.rsqrt(spread + 1e-05)
    unit = centred * inv
    scaled = grad * gain
    first = jnp.mean(scaled, axis=-1, keepdims=True)
    second = jnp.mean(scaled * unit, axis=-1, keepdims=True)
    return inv * (scaled - first - unit * second), grad * unit


def swap_halves(v):
    lane = lax.broadcasted_iota(jnp.int32, v.shape, 1)
    low_half = lax.rem(lane, HEAD_DIM) < HEAD_DIM // 2
    return jnp.where(low_half, pltpu.roll(v, PAIR - HEAD_DIM // 2, 1), pltpu.roll(v, HEAD_DIM // 2, 1))


def rope(v, cos, sin):
    return v * cos + swap_halves(v) * sin


def write_qkv(n, w_ref, cos_ref, sin_ref, q_ref, k_ref, v_ref):
    count = w_ref.shape[1] // 3

    def weight(part):
        return jnp.concatenate([w_ref[r, part * count : (part + 1) * count, :] for r in range(w_ref.shape[0])], axis=0)

    cos, sin = cos_ref[...], sin_ref[...]
    q = outer_cols(n, weight(0))
    k = outer_cols(n, weight(1))
    for j in range(q.shape[1] // PAIR):
        cols = slice(j * PAIR, (j + 1) * PAIR)
        q_ref[:, cols] = (rope(q[:, cols], cos, sin) * (1.0 / HEAD_DIM**0.5)).astype(BF16)
        k_ref[:, cols] = rope(k[:, cols], cos, sin).astype(BF16)
    v_ref[...] = outer_cols(n, weight(2)).astype(BF16)


def norm_qkv_kernel(x_ref, gain_ref, w_ref, cos_ref, sin_ref, n_ref, q_ref, k_ref, v_ref):
    n = normed(x_ref[...].astype(F32), gain_ref[...]).astype(BF16)
    n_ref[...] = n
    write_qkv(n, w_ref, cos_ref, sin_ref, q_ref, k_ref, v_ref)


def only_qkv_kernel(n_ref, w_ref, cos_ref, sin_ref, q_ref, k_ref, v_ref):
    write_qkv(n_ref[...], w_ref, cos_ref, sin_ref, q_ref, k_ref, v_ref)


def project_qkv(rows_in, gain, pack, cos, sin):
    rows, width = rows_in.shape
    cols = pack.shape[0] * pack.shape[1] // 3
    block = 256
    row_spec = pl.BlockSpec((block, width), lambda i: (i, 0))
    out_spec = pl.BlockSpec((block, cols), lambda i: (i, 0))
    gain_spec = pl.BlockSpec((1, width), lambda i: (0, 0))
    w_spec = pl.BlockSpec(pack.shape, lambda i: (0, 0, 0))
    tab_spec = pl.BlockSpec((block, PAIR), lambda i: (i, 0))
    first = gain is not None
    return pl.pallas_call(
        norm_qkv_kernel if first else only_qkv_kernel,
        grid=(rows // block,),
        in_specs=[row_spec] + [gain_spec] * first + [w_spec, tab_spec, tab_spec],
        out_specs=[row_spec] * first + [out_spec] * 3,
        out_shape=[jax.ShapeDtypeStruct((rows, width), BF16)] * first + [jax.ShapeDtypeStruct((rows, cols), BF16)] * 3,
        compiler_params=pltpu.CompilerParams(vmem_limit_bytes=VMEM_LIMIT),
        cost_estimate=pl.CostEstimate(
            flops=8 * rows * width * cols, bytes_accessed=8 * rows * width + 6 * width * cols, transcendentals=0
        ),
        name="norm_qkv" if first else "qkv",
    )(*([rows_in] + [gain] * first + [pack, cos, sin]))


def pad_rows(dst, src):
    rows = src.shape[0]
    edge = jnp.zeros((HALF, PAIR), dst.dtype)
    dst[0:HALF, :] = edge
    dst[HALF : HALF + rows, :] = src
    dst[HALF + rows : rows + 2 * HALF, :] = edge


def split_lanes(src, first, second):
    lane = lax.broadcasted_iota(jnp.int32, src.shape, 1)
    zero = jnp.zeros_like(src)
    first[...] = jnp.where(lane < HEAD_DIM, src, zero)
    second[...] = jnp.where(lane < HEAD_DIM, zero, src)


def attend_kernel(q_ref, k_ref, v_ref, bias_ref, o_ref, p_ref, pad, k0, k1, vt):
    rows = q_ref.shape[0]
    pad_rows(pad, v_ref[...])
    vt[...] = pad[...].T
    pad_rows(pad, k_ref[...])
    split_lanes(pad[...], k0, k1)
    for i in range(rows // QB):
        win = slice(i * QB, i * QB + KB)
        at = slice(i * QB, (i + 1) * QB)
        q_t = q_ref[at, :].T
        bias = bias_ref[i]
        outs = []
        for h, k in enumerate((k0, k1)):
            s = dot(k[win, :], q_t) + bias
            e = jnp.exp(s - jnp.max(s, axis=0, keepdims=True))
            p = (e * (1.0 / jnp.sum(e, axis=0, keepdims=True))).astype(BF16)
            p_ref[0, i, :, h * QB : (h + 1) * QB] = p
            outs.append(dot(vt[h * HEAD_DIM : (h + 1) * HEAD_DIM, win], p))
        o_ref[at, :] = jnp.concatenate(outs, axis=0).astype(BF16).T


def attend(q, k, v, bias):
    rows, width = q.shape
    pairs, blocks = width // PAIR, rows // QB
    spec = pl.BlockSpec((rows, PAIR), lambda j: (0, j))
    padded = rows + 2 * HALF
    return pl.pallas_call(
        attend_kernel,
        grid=(pairs,),
        in_specs=[spec, spec, spec, pl.BlockSpec((blocks, KB, QB), lambda j: (0, 0, 0))],
        out_specs=[spec, pl.BlockSpec((1, blocks, KB, 2 * QB), lambda j: (j, 0, 0, 0))],
        out_shape=[
            jax.ShapeDtypeStruct((rows, width), BF16),
            jax.ShapeDtypeStruct((pairs, blocks, KB, 2 * QB), BF16),
        ],
        scratch_shapes=[pltpu.VMEM((padded, PAIR), BF16)] * 3 + [pltpu.VMEM((PAIR, padded), BF16)],
        compiler_params=pltpu.CompilerParams(vmem_limit_bytes=VMEM_LIMIT),
        cost_estimate=pl.CostEstimate(flops=2 * 10**9 * pairs, bytes_accessed=2 * rows * width * 8, transcendentals=0),
        name="attend",
    )(q, k, v, bias)


def swap_rows(v):
    quarter = HEAD_DIM // 2
    part = [v[i * quarter : (i + 1) * quarter, :] for i in range(4)]
    return jnp.concatenate([part[1], part[0], part[3], part[2]], axis=0)


def both_heads(v):
    lane = lax.broadcasted_iota(jnp.int32, v.shape, 1)
    zero = jnp.zeros_like(v)
    return jnp.concatenate([jnp.where(lane < HEAD_DIM, v, zero), jnp.where(lane < HEAD_DIM, zero, v)], axis=0)


def attend_back_kernel(
    q_ref, k_ref, v_ref, g_ref, p_ref, cos_ref, sin_ref, cos_t, sin_t, gq_ref, gk_ref, gv_ref, pad, v0, v1, kt, gk, gv
):
    rows = q_ref.shape[0]
    scale = 1.0 / HEAD_DIM**0.5
    pad_rows(pad, k_ref[...])
    kt[...] = pad[...].T
    pad_rows(pad, v_ref[...])
    split_lanes(pad[...], v0, v1)
    gk[...] = jnp.zeros_like(gk)
    gv[...] = jnp.zeros_like(gv)
    for i in range(rows // QB):
        win = slice(i * QB, i * QB + KB)
        at = slice(i * QB, (i + 1) * QB)
        g = g_ref[at, :]
        g_t = g.T
        p_low = p_ref[0, i]
        outs, grads = [], []
        for h, v in enumerate((v0, v1)):
            p = p_low[:, h * QB : (h + 1) * QB].astype(F32)
            gp = dot(v[win, :], g_t)
            weighted = jnp.sum(p * gp, axis=0, keepdims=True)
            gs = (p * (gp - weighted)).astype(BF16)
            grads.append(gs)
            outs.append(dot(kt[h * HEAD_DIM : (h + 1) * HEAD_DIM, win], gs))
        gk[win, :] += dot(jnp.concatenate(grads, axis=1), both_heads(q_ref[at, :]))
        gv[win, :] += dot(p_low, both_heads(g))
        gq = jnp.concatenate(outs, axis=0) * scale
        gq_ref[at, :] = (gq * cos_t[:, at] - swap_rows(gq) * sin_t[:, at]).astype(BF16).T
    gk_ref[...] = rope(gk[HALF : HALF + rows, :], cos_ref[...], -sin_ref[...]).astype(BF16)
    gv_ref[...] = gv[HALF : HALF + rows, :].astype(BF16)


def attend_back(q, k, v, g, prob, cos, sin, cos_t, sin_t):
    rows, width = q.shape
    pairs, blocks = width // PAIR, rows // QB
    spec = pl.BlockSpec((rows, PAIR), lambda j: (0, j))
    tab_spec = pl.BlockSpec((rows, PAIR), lambda j: (0, 0))
    tab_t_spec = pl.BlockSpec((PAIR, rows), lambda j: (0, 0))
    padded = rows + 2 * HALF
    return pl.pallas_call(
        attend_back_kernel,
        grid=(pairs,),
        in_specs=[spec] * 4
        + [pl.BlockSpec((1, blocks, KB, 2 * QB), lambda j: (j, 0, 0, 0)), tab_spec, tab_spec, tab_t_spec, tab_t_spec],
        out_specs=[spec] * 3,
        out_shape=[jax.ShapeDtypeStruct((rows, width), BF16)] * 3,
        scratch_shapes=[pltpu.VMEM((padded, PAIR), BF16)] * 3
        + [pltpu.VMEM((PAIR, padded), BF16)]
        + [pltpu.VMEM((padded, PAIR), F32)] * 2,
        compiler_params=pltpu.CompilerParams(vmem_limit_bytes=VMEM_LIMIT),
        cost_estimate=pl.CostEstimate(flops=3 * 10**9 * pairs, bytes_accessed=2 * rows * width * 10, transcendentals=0),
        name="attend_back",
    )(q, k, v, g, prob, cos, sin, cos_t, sin_t)


def ring(step):
    size = lax.axis_size("tensor")
    return [(i, (i + step) % size) for i in range(size)]


def plane(dy, dz, dc=0):
    size = lax.axis_size("dp")
    out = []
    for i in range(size):
        y, z, c = i // 8, (i // 2) % 4, i % 2
        out.append((i, (((y + dy) % 4) * 4 + (z + dz) % 4) * 2 + (c + dc) % 2))
    return out


def place_pair_kernel(core_ref, own_ref, mine_ref, other_ref, out_ref):
    half = mine_ref.shape[1]
    out_ref[0] = own_ref[...]
    core = core_ref[0]
    out_ref[1, :, pl.ds(pl.multiple_of(core * half, half), half)] = mine_ref[...].astype(BF16)
    out_ref[1, :, pl.ds(pl.multiple_of((1 - core) * half, half), half)] = other_ref[...].astype(BF16)


def place_rest_kernel(core_ref, mine_ref, other_ref, head_ref, tail_ref, other_head_ref, other_tail_ref, out_ref):
    rows, half = mine_ref.shape
    core = core_ref[0]
    mine_at = pl.ds(pl.multiple_of(core * half, half), half)
    other_at = pl.ds(pl.multiple_of((1 - core) * half, half), half)
    out_ref[0, :, mine_at] = mine_ref[...].astype(BF16)
    out_ref[0, :, other_at] = other_ref[...].astype(BF16)
    out_ref[1, 0 : rows // 2, mine_at] = head_ref[...].astype(BF16)
    out_ref[1, rows // 2 : rows, mine_at] = tail_ref[...].astype(BF16)
    out_ref[1, 0 : rows // 2, other_at] = other_head_ref[...].astype(BF16)
    out_ref[1, rows // 2 : rows, other_at] = other_tail_ref[...].astype(BF16)


def place(kernel, core, rows, lanes, args, name):
    whole = pl.BlockSpec(memory_space=pltpu.VMEM)
    return pl.pallas_call(
        kernel,
        in_specs=[pl.BlockSpec(memory_space=pltpu.SMEM)] + [whole] * len(args),
        out_specs=whole,
        out_shape=jax.ShapeDtypeStruct((2, rows, lanes), BF16),
        compiler_params=pltpu.CompilerParams(vmem_limit_bytes=VMEM_LIMIT),
        name=name,
    )(core[None].astype(jnp.int32), *args)


def gather_attn(w_query, w_key, w_value, meanwhile):
    core = lax.axis_index("dp") % 2
    own = jnp.concatenate([w_query.T, w_key.T, w_value.T], axis=0)
    rows, lanes = own.shape
    half = lanes // 2
    mine = lax.dynamic_slice_in_dim(own, core * half, half, 1).astype(F32)
    swap = plane(0, 0, 1)
    after = lax.ppermute(mine, "tensor", ring(-1))
    before = lax.ppermute(mine, "tensor", ring(1))
    after, before, meanwhile = lax.optimization_barrier((after, before, meanwhile))
    head = lax.ppermute(after[: rows // 2], "tensor", ring(-1))
    tail = lax.ppermute(before[rows // 2 :], "tensor", ring(1))
    other_after = lax.ppermute(after, "dp", swap)
    other_before = lax.ppermute(before, "dp", swap)
    first = place(place_pair_kernel, core, rows, lanes, (own, after, other_after), "place_pair")

    def rest(behind):
        late_head, late_tail, behind = lax.optimization_barrier((head, tail, behind))
        other_head = lax.ppermute(late_head, "dp", swap)
        other_tail = lax.ppermute(late_tail, "dp", swap)
        args = (before, other_before, late_head, late_tail, other_head, other_tail)
        return place(place_rest_kernel, core, rows, lanes, args, "place_rest"), behind

    return first, rest, meanwhile


def gather_mlp(w_in, w_gate, w_down, w_attn_out):
    at = lax.axis_index("dp")
    core, z, y = at % 2, (at // 2) % 4, at // 8
    half = w_down.shape[1] // 2
    count = w_down.shape[0] // 4
    short = w_attn_out.shape[0] // 4
    tall_in = lax.dynamic_slice(w_in, (core * half, z * count), (half, count)).T
    tall_gate = lax.dynamic_slice(w_gate, (core * half, z * count), (half, count)).T
    down = lax.dynamic_slice(w_down, (z * count, core * half), (count, half))
    out = lax.dynamic_slice(w_attn_out, (z * short, core * half), (short, half))
    out = jnp.pad(out, ((0, count - short), (0, 0)))
    piece = jnp.where(y == 0, tall_in, jnp.where(y == 1, tall_gate, jnp.where(y == 2, down, out))).astype(F32)
    whole = lax.all_gather(piece, ("dp", "tensor"), axis=0, tiled=False)
    return whole.reshape(4, 4, 2, 4, count, half)


def mlp_kernel(
    at_ref,
    w_ref,
    x_ref,
    mix0_ref,
    mix1_ref,
    cot_ref,
    live_ref,
    gain_ref,
    out_ref,
    resid_ref,
    low_ref,
    mixg_ref,
    n_ref,
    hid_ref,
    gug_ref,
    go_ref,
    gain_out_ref,
    up_w,
    gt_w,
    dn_w,
    o_w,
):
    step = pl.program_id(0)
    quarters, halves, count, half = w_ref.shape[1], w_ref.shape[2], w_ref.shape[4], w_ref.shape[5]
    loads = 4

    def load(dst, rows):
        for r in range(4):
            rank = lax.rem(at_ref[0] + (r ^ (r >> 1)), 4)
            at = slice(r * quarters * rows, (r + 1) * quarters * rows)
            for c in range(halves):
                block = jnp.concatenate([w_ref[0, z, c, rank, 0:rows, :] for z in range(quarters)], axis=0)
                dst[at, c * half : (c + 1) * half] = block.astype(BF16)

    for kind, (dst, rows) in enumerate(((up_w, count), (gt_w, count), (dn_w, count), (o_w, o_w.shape[0] // 16))):

        @pl.when(step == kind)
        def _(dst=dst, rows=rows):
            load(dst, rows)

    @pl.when(step >= loads)
    def _():
        split = mix0_ref.shape[1]
        gain = gain_ref[...]
        resid = x_ref[...].astype(F32) + dot(mix0_ref[...], o_w[0:split, :]) + dot(mix1_ref[...], o_w[split:, :])
        centre = jnp.mean(resid, axis=-1, keepdims=True)
        centred = resid - centre
        inv = lax.rsqrt(jnp.mean(centred * centred, axis=-1, keepdims=True) + 1e-05)
        unit = centred * inv
        n = (unit * gain).astype(BF16)
        n_ref[...] = n
        up = outer_cols(n, up_w[...])
        gate = outer_cols(n, gt_w[...])
        go = cot_ref[...].astype(F32) * live_ref[...]
        go_low = go.astype(BF16)
        go_ref[...] = go_low
        gh = outer_cols(go_low, dn_w[...])
        bell = jnp.exp(up * up * -0.5)
        t = 1.0 / (1.0 + (0.3275911 * 0.7071067811865476) * jnp.abs(up))
        poly = t * (
            0.5 * 0.254829592
            + t * (0.5 * -0.284496736 + t * (0.5 * 1.421413741 + t * (0.5 * -1.453152027 + t * (0.5 * 1.061405429))))
        )
        tail = poly * bell
        cdf = jnp.where(up >= 0.0, 1.0 - tail, tail)
        act = up * cdf
        slope = cdf + up * bell * 0.3989422804014327
        hid = (act * gate).astype(BF16)
        gup = (gh * gate * slope).astype(BF16)
        ggt = (gh * act).astype(BF16)
        own = hid_ref.shape[1]
        hid_ref[...] = hid[:, :own]
        gug_ref[...] = jnp.concatenate([gup[:, :own], ggt[:, :own]], axis=1)
        out_ref[...] = (resid + dot(hid, dn_w[...])).astype(BF16)
        gn = dot(gup, up_w[...]) + dot(ggt, gt_w[...])
        scaled = gn * gain
        first = jnp.mean(scaled, axis=-1, keepdims=True)
        second = jnp.mean(scaled * unit, axis=-1, keepdims=True)
        grad = go + inv * (scaled - first - unit * second)
        resid_ref[...] = grad
        low = grad.astype(BF16)
        low_ref[...] = low
        mixg_ref[...] = outer_cols(low, o_w[...]).astype(BF16)
        terms = jnp.sum(gn * unit, axis=0, keepdims=True)

        @pl.when(step == loads)
        def _():
            gain_out_ref[...] = terms

        @pl.when(step > loads)
        def _():
            gain_out_ref[...] += terms


def mlp(weights, tokens, mix0, mix1, cotangent, live, gain):
    rows, width = tokens.shape
    block, loads = 256, 4
    quarters, halves, count, half = weights.shape[1], weights.shape[2], weights.shape[4], weights.shape[5]
    own = quarters * count
    ff = 4 * own

    def at_row(i, _):
        return (jnp.maximum(i - loads, 0), 0)

    def at_weight(i, at):
        return (jnp.minimum(i, loads - 1), 0, 0, 0, 0, 0)

    def row(cols):
        return pl.BlockSpec((block, cols), at_row)

    def fixed(i, _):
        return (0, 0)

    def shape(cols, kind):
        return jax.ShapeDtypeStruct((rows, cols), kind)

    split = mix0.shape[1]
    return pl.pallas_call(
        mlp_kernel,
        grid_spec=pltpu.PrefetchScalarGridSpec(
            num_scalar_prefetch=1,
            grid=(loads + rows // block,),
            in_specs=[
                pl.BlockSpec((1, quarters, halves, 4, count, half), at_weight),
                row(width),
                row(split),
                row(width - split),
                row(width),
                row(1),
                pl.BlockSpec((1, width), fixed),
            ],
            out_specs=[
                row(width),
                row(width),
                row(width),
                row(width),
                row(width),
                row(own),
                row(2 * own),
                row(width),
                pl.BlockSpec((1, width), fixed),
            ],
            scratch_shapes=[
                pltpu.VMEM((ff, width), BF16),
                pltpu.VMEM((ff, width), BF16),
                pltpu.VMEM((ff, width), BF16),
                pltpu.VMEM((width, width), BF16),
            ],
        ),
        out_shape=[
            shape(width, BF16),
            shape(width, F32),
            shape(width, BF16),
            shape(width, BF16),
            shape(width, BF16),
            shape(own, BF16),
            shape(2 * own, BF16),
            shape(width, BF16),
            jax.ShapeDtypeStruct((1, width), F32),
        ],
        compiler_params=pltpu.CompilerParams(vmem_limit_bytes=VMEM_LIMIT),
        cost_estimate=pl.CostEstimate(flops=12 * rows * width * ff, bytes_accessed=40 * 10**6, transcendentals=0),
        name="mlp",
    )(lax.axis_index("tensor")[None].astype(jnp.int32), weights, tokens, mix0, mix1, cotangent, live, gain)


def finish_kernel(x_ref, grad_ref, gain_ref, *refs):
    parts, weights, (out_ref, gain_out_ref) = refs[:6], refs[6:8], refs[8:]
    total = None
    for half in range(2):
        w_ref = weights[half]
        count = w_ref.shape[1] // 3
        for part in range(3):
            w = jnp.concatenate([w_ref[r, part * count : (part + 1) * count, :] for r in range(w_ref.shape[0])], axis=0)
            term = dot(parts[half * 3 + part][...], w)
            total = term if total is None else total + term
    back, terms = norm_back(x_ref[...].astype(F32), gain_ref[...], total)
    out_ref[...] = grad_ref[...] + back
    terms = jnp.sum(terms, axis=0, keepdims=True)

    @pl.when(pl.program_id(0) == 0)
    def _():
        gain_out_ref[...] = terms

    @pl.when(pl.program_id(0) > 0)
    def _():
        gain_out_ref[...] += terms


def finish(tokens, grad_resid, gain, parts, weights):
    rows, width = tokens.shape
    block = 256

    def row(cols):
        return pl.BlockSpec((block, cols), lambda i: (i, 0))

    fixed = pl.BlockSpec((1, width), lambda i: (0, 0))
    return pl.pallas_call(
        finish_kernel,
        grid=(rows // block,),
        in_specs=[row(width), row(width), fixed]
        + [row(p.shape[1]) for p in parts]
        + [pl.BlockSpec(w.shape, lambda i: (0, 0, 0)) for w in weights],
        out_specs=[row(width), fixed],
        out_shape=[jax.ShapeDtypeStruct((rows, width), F32), jax.ShapeDtypeStruct((1, width), F32)],
        compiler_params=pltpu.CompilerParams(vmem_limit_bytes=VMEM_LIMIT),
        cost_estimate=pl.CostEstimate(flops=6 * rows * width * width, bytes_accessed=20 * 10**6, transcendentals=0),
        name="finish",
    )(tokens, grad_resid, gain, *parts, *weights)


def to_peers(blocks, moves):
    return [lax.ppermute(block, "dp", plane(*move)) for block, move in zip(blocks, moves)]


def rows_at(array, place, count):
    return lax.dynamic_slice_in_dim(array, place * count, count, 0)


def halves_summed(grads):
    core = lax.axis_index("dp") % 2
    half = grads.shape[0] // 2
    return rows_at(grads, core, half) + lax.ppermute(rows_at(grads, 1 - core, half), "dp", plane(0, 0, 1))


def halve_early(early_in, early_down, behind):
    early_in, early_down = halves_summed(early_in), halves_summed(early_down)
    early_in, early_down, behind = lax.optimization_barrier((early_in, early_down, behind))
    same_core = [[i for i in range(lax.axis_size("dp")) if i % 2 == c] for c in range(2)]
    early_in, early_down = lax.psum((early_in, early_down), "dp", axis_index_groups=same_core)
    return early_in, early_down, behind


def whole_of(done, got):
    first = lax.axis_index("dp") % 2 == 0
    return jnp.concatenate([jnp.where(first, done, got), jnp.where(first, got, done)], axis=0)


def join_early(*halves):
    return [whole_of(half, lax.ppermute(half, "dp", plane(0, 0, 1))) for half in halves]


def start_late(grads, behind):
    y = lax.axis_index("dp") // 8
    half = halves_summed(grads)
    quarter = half.shape[0] // 4
    blocks = [rows_at(half, (y + d) % 4, quarter) for d in range(4)]
    return lax.optimization_barrier((blocks, behind))


def reduce_late(blocks, small):
    at = lax.axis_index("dp")
    z, y = (at // 2) % 4, at // 8
    in_y = [(d, 0) for d in (1, 2, 3)]
    in_z = [(0, d) for d in (1, 2, 3)]
    got = to_peers(blocks[1:], in_y)
    mine = blocks[0] + got[0] + got[1] + got[2]
    part = mine.shape[0] // 4
    got = to_peers([rows_at(mine, (z + d) % 4, part) for d in (1, 2, 3)], in_z)
    done = rows_at(mine, z, part) + got[0] + got[1] + got[2]

    def spread(block, small, moves, place):
        sent = jnp.concatenate([block, small], axis=0)
        got = to_peers([sent] * 3, moves)
        count = block.shape[0]
        small = small + got[0][count:] + got[1][count:] + got[2][count:]
        blocks = [block] + [g[:count] for g in got]
        order = [lax.rem(place - j + 4, 4) for j in range(4)]
        whole = jnp.concatenate([lax.select_n(order[j], *blocks) for j in range(4)], axis=0)
        return whole, small

    done, small = spread(done, small, in_z, z)
    done, small = spread(done, small, in_y, y)
    sent = jnp.concatenate([done, small], axis=0)
    got = lax.ppermute(sent, "dp", plane(0, 0, 1))
    count = done.shape[0]
    return whole_of(done, got[:count]), small + got[count:]


def body(
    tokens,
    cotangent,
    seq_len,
    seq_slot,
    attn_gain,
    w_query,
    w_key,
    w_value,
    w_attn_out,
    mlp_gain,
    w_in,
    w_gate,
    w_down,
):
    rows, width = tokens.shape
    heads_cols = w_query.shape[1]
    per_group = 2
    slots = lax.axis_index("dp") * per_group + jnp.arange(per_group, dtype=jnp.int32)
    lengths = jnp.sum(jnp.where(seq_slot[None, :] == slots[:, None], seq_len[None, :], 0), axis=1)
    end0, end1 = lengths[0], lengths[0] + lengths[1]

    def segment_of(index):
        return (index >= end0).astype(jnp.int32) + (index >= end1).astype(jnp.int32)

    index = lax.broadcasted_iota(jnp.int32, (rows, PAIR), 0)
    position = index - jnp.where(index >= end1, end1, jnp.where(index >= end0, end0, 0))
    lane = lax.broadcasted_iota(jnp.int32, (rows, PAIR), 1)
    width_half = HEAD_DIM // 2
    frequency = 10000.0 ** (-(jnp.arange(width_half, dtype=F32) * 2.0 / HEAD_DIM))
    frequency = jnp.tile(frequency, PAIR // width_half)
    phase = position.astype(F32) * frequency[None, :]
    cos = jnp.cos(phase)
    sin = jnp.where(lane % HEAD_DIM < width_half, -1.0, 1.0) * jnp.sin(phase)
    shape = (rows // QB, KB, QB)
    block_at = lax.broadcasted_iota(jnp.int32, shape, 0) * QB
    row_at = block_at + lax.broadcasted_iota(jnp.int32, shape, 2)
    col_at = block_at + lax.broadcasted_iota(jnp.int32, shape, 1) - HALF
    allowed = (
        (segment_of(row_at) == segment_of(col_at))
        & (jnp.abs(row_at - col_at) <= HALF)
        & (col_at >= 0)
        & (col_at < rows)
    )
    bias = jnp.where(allowed, 0.0, -1e30).astype(F32)
    live = (jnp.arange(rows, dtype=jnp.int32) < end1).astype(F32)

    weights_mlp = gather_mlp(w_in, w_gate, w_down, w_attn_out)
    weights0, rest, (cos, sin, cos_t, sin_t, bias) = gather_attn(
        w_query, w_key, w_value, (cos, sin, cos.T, sin.T, bias)
    )
    gain1 = attn_gain[None, :]
    normed1, *qkv0 = project_qkv(tokens, gain1, weights0, cos, sin)
    mix0, prob0 = attend(*qkv0, bias)
    weights1, mix0 = rest(mix0)
    weights_attn = (weights0, weights1)
    qkv1 = project_qkv(normed1, None, weights_attn[1], cos, sin)
    mix1, prob1 = attend(*qkv1, bias)
    (
        mixed_out,
        grad_resid,
        grad_resid_low,
        grad_mix,
        normed2,
        hidden,
        grad_up_gate,
        grad_out_low,
        gain2_sum,
    ) = mlp(weights_mlp, tokens, mix0, mix1, cotangent, live[:, None], mlp_gain[None, :])
    early_in = inner_rows(normed2, grad_up_gate)
    early_down = jnp.concatenate(
        [inner_rows(hidden, grad_out_low), inner_rows(mix0[:, :heads_cols], grad_resid_low)], axis=0
    )
    early_in, early_down, grad_mix = halve_early(early_in, early_down, grad_mix)
    split = mix0.shape[1]
    tables = (cos, sin, cos_t, sin_t)
    back0 = attend_back(*qkv0, grad_mix[:, :split], prob0, *tables)
    own_grads = jnp.concatenate([g[:, :heads_cols] for g in back0], axis=1)
    late = inner_rows(normed1, own_grads)
    late, next_in = start_late(late, grad_mix[:, split:])
    back1 = attend_back(*qkv1, next_in, prob1, *tables)
    grad_tokens, gain1_sum = finish(tokens, grad_resid, gain1, [*back0, *back1], weights_attn)
    lanes = own_grads.shape[1]
    small = jnp.concatenate([gain1_sum[0], gain2_sum[0]])
    small = jnp.pad(small, (0, 8 * lanes - small.shape[0])).reshape(8, lanes)
    late, small = reduce_late(late, small)
    small = small.reshape(-1)
    early_in, early_down = join_early(early_in, early_down)
    ff_cols = w_in.shape[1]
    return (
        mixed_out,
        grad_tokens,
        small[:width],
        late[:, :heads_cols],
        late[:, heads_cols : 2 * heads_cols],
        late[:, 2 * heads_cols :],
        early_down[ff_cols:],
        small[width : 2 * width],
        early_in[:, :ff_cols],
        early_in[:, ff_cols:],
        early_down[:ff_cols],
    )


def solution(mesh):
    rows, cols, all_of = P("dp", None), P(None, "tensor"), P()
    tall = P("tensor", None)
    return jax.shard_map(
        body,
        mesh=mesh,
        in_specs=(rows, rows, all_of, all_of, all_of, cols, cols, cols, tall, all_of, cols, cols, tall),
        out_specs=(rows, rows, all_of, cols, cols, cols, tall, all_of, cols, cols, tall),
        check_vma=False,
    )
```

```python
import jax
import jax.numpy as jnp
from jax import lax
from jax.experimental import pallas as pl
from jax.experimental.pallas import tpu as pltpu
from jax.sharding import PartitionSpec as P

HEAD_DIM = 64
HALF = 64
QB = 128
KB = QB + 2 * HALF
PAIR = 2 * HEAD_DIM
STAGED = 4
STAGED_BACK = 4
F32 = jnp.float32
BF16 = jnp.bfloat16
VMEM_LIMIT = 48 * 1024 * 1024


def dot(a, b):
    return jnp.dot(a, b, preferred_element_type=F32)


def inner_rows(left, right):
    return lax.dot_general(left, right, (((0,), (0,)), ((), ())), preferred_element_type=F32)


def outer_cols(left, right):
    return lax.dot_general(left, right, (((1,), (1,)), ((), ())), preferred_element_type=F32)


def normed(values, gain):
    centre = jnp.mean(values, axis=-1, keepdims=True)
    centred = values - centre
    spread = jnp.mean(centred * centred, axis=-1, keepdims=True)
    return centred * lax.rsqrt(spread + 1e-05) * gain


def norm_back(values, gain, grad):
    centre = jnp.mean(values, axis=-1, keepdims=True)
    centred = values - centre
    spread = jnp.mean(centred * centred, axis=-1, keepdims=True)
    inv = lax.rsqrt(spread + 1e-05)
    unit = centred * inv
    scaled = grad * gain
    first = jnp.mean(scaled, axis=-1, keepdims=True)
    second = jnp.mean(scaled * unit, axis=-1, keepdims=True)
    return inv * (scaled - first - unit * second), grad * unit


def swap_halves(v):
    lane = lax.broadcasted_iota(jnp.int32, v.shape, 1)
    low_half = lax.rem(lane, HEAD_DIM) < HEAD_DIM // 2
    return jnp.where(low_half, pltpu.roll(v, PAIR - HEAD_DIM // 2, 1), pltpu.roll(v, HEAD_DIM // 2, 1))


def rope(v, cos, sin):
    return v * cos + swap_halves(v) * sin


def write_qkv(n, w_ref, cos_ref, sin_ref, q_ref, k_ref, v_ref):
    count = w_ref.shape[1] // 3

    def weight(part):
        return jnp.concatenate([w_ref[r, part * count : (part + 1) * count, :] for r in range(w_ref.shape[0])], axis=0)

    cos, sin = cos_ref[...], sin_ref[...]
    q = outer_cols(n, weight(0))
    k = outer_cols(n, weight(1))
    for j in range(q.shape[1] // PAIR):
        cols = slice(j * PAIR, (j + 1) * PAIR)
        q_ref[:, cols] = (rope(q[:, cols], cos, sin) * (1.0 / HEAD_DIM**0.5)).astype(BF16)
        k_ref[:, cols] = rope(k[:, cols], cos, sin).astype(BF16)
    v_ref[...] = outer_cols(n, weight(2)).astype(BF16)


def norm_qkv_kernel(x_ref, gain_ref, w_ref, cos_ref, sin_ref, n_ref, q_ref, k_ref, v_ref):
    n = normed(x_ref[...].astype(F32), gain_ref[...]).astype(BF16)
    n_ref[...] = n
    write_qkv(n, w_ref, cos_ref, sin_ref, q_ref, k_ref, v_ref)


def only_qkv_kernel(n_ref, w_ref, cos_ref, sin_ref, q_ref, k_ref, v_ref):
    write_qkv(n_ref[...], w_ref, cos_ref, sin_ref, q_ref, k_ref, v_ref)


def project_qkv(rows_in, gain, pack, cos, sin):
    rows, width = rows_in.shape
    cols = pack.shape[0] * pack.shape[1] // 3
    block = 256
    row_spec = pl.BlockSpec((block, width), lambda i: (i, 0))
    out_spec = pl.BlockSpec((block, cols), lambda i: (i, 0))
    gain_spec = pl.BlockSpec((1, width), lambda i: (0, 0))
    w_spec = pl.BlockSpec(pack.shape, lambda i: (0, 0, 0))
    tab_spec = pl.BlockSpec((block, PAIR), lambda i: (i, 0))
    first = gain is not None
    return pl.pallas_call(
        norm_qkv_kernel if first else only_qkv_kernel,
        grid=(rows // block,),
        in_specs=[row_spec] + [gain_spec] * first + [w_spec, tab_spec, tab_spec],
        out_specs=[row_spec] * first + [out_spec] * 3,
        out_shape=[jax.ShapeDtypeStruct((rows, width), BF16)] * first + [jax.ShapeDtypeStruct((rows, cols), BF16)] * 3,
        compiler_params=pltpu.CompilerParams(vmem_limit_bytes=VMEM_LIMIT),
        cost_estimate=pl.CostEstimate(
            flops=8 * rows * width * cols, bytes_accessed=8 * rows * width + 6 * width * cols, transcendentals=0
        ),
        name="norm_qkv" if first else "qkv",
    )(*([rows_in] + [gain] * first + [pack, cos, sin]))


def pad_rows(dst, src):
    rows = src.shape[0]
    edge = jnp.zeros((HALF, PAIR), dst.dtype)
    dst[0:HALF, :] = edge
    dst[HALF : HALF + rows, :] = src
    dst[HALF + rows : rows + 2 * HALF, :] = edge


def split_lanes(src, first, second):
    lane = lax.broadcasted_iota(jnp.int32, src.shape, 1)
    zero = jnp.zeros_like(src)
    first[...] = jnp.where(lane < HEAD_DIM, src, zero)
    second[...] = jnp.where(lane < HEAD_DIM, zero, src)


def query_rows(i):
    return slice(i * QB, (i + 1) * QB)


def key_rows(i):
    return slice(i * QB, i * QB + KB)


def head_rows(h):
    return slice(h * HEAD_DIM, (h + 1) * HEAD_DIM)


def attend_kernel(q_ref, k_ref, v_ref, bias_ref, o_ref, p_ref, pad, k0, k1, vt):
    rows = q_ref.shape[0]
    pad_rows(pad, v_ref[...])
    vt[...] = pad[...].T
    pad_rows(pad, k_ref[...])
    split_lanes(pad[...], k0, k1)
    for start in range(0, rows // QB, STAGED):
        blocks = range(start, start + STAGED)
        units = [(i, h) for i in blocks for h in range(2)]
        q_t = {i: q_ref[query_rows(i), :].T for i in blocks}
        scores = [dot((k0, k1)[h][key_rows(i), :], q_t[i]) + bias_ref[i] for i, h in units]
        tops = [jnp.max(s, axis=0, keepdims=True) for s in scores]
        expos = [jnp.exp(s - top) for s, top in zip(scores, tops)]
        shares = [1.0 / jnp.sum(e, axis=0, keepdims=True) for e in expos]
        probs = [(e * share).astype(BF16) for e, share in zip(expos, shares)]
        outs = [dot(vt[head_rows(h), key_rows(i)], p) for (i, h), p in zip(units, probs)]
        for (i, h), p in zip(units, probs):
            p_ref[0, i, :, h * QB : (h + 1) * QB] = p
        for n, i in enumerate(blocks):
            o_ref[query_rows(i), :] = jnp.concatenate(outs[2 * n : 2 * n + 2], axis=0).astype(BF16).T


def attend(q, k, v, bias):
    rows, width = q.shape
    pairs, blocks = width // PAIR, rows // QB
    spec = pl.BlockSpec((rows, PAIR), lambda j: (0, j))
    padded = rows + 2 * HALF
    return pl.pallas_call(
        attend_kernel,
        grid=(pairs,),
        in_specs=[spec, spec, spec, pl.BlockSpec((blocks, KB, QB), lambda j: (0, 0, 0))],
        out_specs=[spec, pl.BlockSpec((1, blocks, KB, 2 * QB), lambda j: (j, 0, 0, 0))],
        out_shape=[
            jax.ShapeDtypeStruct((rows, width), BF16),
            jax.ShapeDtypeStruct((pairs, blocks, KB, 2 * QB), BF16),
        ],
        scratch_shapes=[pltpu.VMEM((padded, PAIR), BF16)] * 3 + [pltpu.VMEM((PAIR, padded), BF16)],
        compiler_params=pltpu.CompilerParams(vmem_limit_bytes=VMEM_LIMIT),
        cost_estimate=pl.CostEstimate(flops=2 * 10**9 * pairs, bytes_accessed=2 * rows * width * 8, transcendentals=0),
        name="attend",
    )(q, k, v, bias)


def swap_rows(v):
    quarter = HEAD_DIM // 2
    part = [v[i * quarter : (i + 1) * quarter, :] for i in range(4)]
    return jnp.concatenate([part[1], part[0], part[3], part[2]], axis=0)


def both_heads(v):
    lane = lax.broadcasted_iota(jnp.int32, v.shape, 1)
    zero = jnp.zeros_like(v)
    return jnp.concatenate([jnp.where(lane < HEAD_DIM, v, zero), jnp.where(lane < HEAD_DIM, zero, v)], axis=0)


def attend_back_kernel(
    q_ref, k_ref, v_ref, g_ref, p_ref, cos_ref, sin_ref, cos_t, sin_t, gq_ref, gk_ref, gv_ref, pad, v0, v1, kt, gk, gv
):
    rows = q_ref.shape[0]
    scale = 1.0 / HEAD_DIM**0.5
    pad_rows(pad, k_ref[...])
    kt[...] = pad[...].T
    pad_rows(pad, v_ref[...])
    split_lanes(pad[...], v0, v1)
    gk[...] = jnp.zeros_like(gk)
    gv[...] = jnp.zeros_like(gv)
    for start in range(0, rows // QB, STAGED_BACK):
        blocks = range(start, start + STAGED_BACK)
        units = [(i, h) for i in blocks for h in range(2)]
        g_t = {i: g_ref[query_rows(i), :].T for i in blocks}
        gps = [dot((v0, v1)[h][key_rows(i), :], g_t[i]) for i, h in units]
        probs = [p_ref[0, i, :, h * QB : (h + 1) * QB].astype(F32) for i, h in units]
        sums = [jnp.sum(p * gp, axis=0, keepdims=True) for p, gp in zip(probs, gps)]
        grads = [(p * (gp - total)).astype(BF16) for p, gp, total in zip(probs, gps, sums)]
        outs = [dot(kt[head_rows(h), key_rows(i)], gs) for (i, h), gs in zip(units, grads)]
        gks = [
            dot(jnp.concatenate(grads[2 * n : 2 * n + 2], axis=1), both_heads(q_ref[query_rows(i), :]))
            for n, i in enumerate(blocks)
        ]
        gvs = [dot(p_ref[0, i], both_heads(g_ref[query_rows(i), :])) for i in blocks]
        for n, i in enumerate(blocks):
            at = query_rows(i)
            gk[key_rows(i), :] += gks[n]
            gv[key_rows(i), :] += gvs[n]
            gq = jnp.concatenate(outs[2 * n : 2 * n + 2], axis=0) * scale
            gq_ref[at, :] = (gq * cos_t[:, at] - swap_rows(gq) * sin_t[:, at]).astype(BF16).T
    gk_ref[...] = rope(gk[HALF : HALF + rows, :], cos_ref[...], -sin_ref[...]).astype(BF16)
    gv_ref[...] = gv[HALF : HALF + rows, :].astype(BF16)


def attend_back(q, k, v, g, prob, cos, sin, cos_t, sin_t):
    rows, width = q.shape
    pairs, blocks = width // PAIR, rows // QB
    spec = pl.BlockSpec((rows, PAIR), lambda j: (0, j))
    tab_spec = pl.BlockSpec((rows, PAIR), lambda j: (0, 0))
    tab_t_spec = pl.BlockSpec((PAIR, rows), lambda j: (0, 0))
    padded = rows + 2 * HALF
    return pl.pallas_call(
        attend_back_kernel,
        grid=(pairs,),
        in_specs=[spec] * 4
        + [pl.BlockSpec((1, blocks, KB, 2 * QB), lambda j: (j, 0, 0, 0)), tab_spec, tab_spec, tab_t_spec, tab_t_spec],
        out_specs=[spec] * 3,
        out_shape=[jax.ShapeDtypeStruct((rows, width), BF16)] * 3,
        scratch_shapes=[pltpu.VMEM((padded, PAIR), BF16)] * 3
        + [pltpu.VMEM((PAIR, padded), BF16)]
        + [pltpu.VMEM((padded, PAIR), F32)] * 2,
        compiler_params=pltpu.CompilerParams(vmem_limit_bytes=VMEM_LIMIT),
        cost_estimate=pl.CostEstimate(flops=8 * 10**9, bytes_accessed=10**7, transcendentals=0),
        name="attend_back",
    )(q, k, v, g, prob, cos, sin, cos_t, sin_t)


def ring(step):
    size = lax.axis_size("tensor")
    return [(i, (i + step) % size) for i in range(size)]


def plane(dy, dz, dc=0):
    size = lax.axis_size("dp")
    out = []
    for i in range(size):
        y, z, c = i // 8, (i // 2) % 4, i % 2
        out.append((i, (((y + dy) % 4) * 4 + (z + dz) % 4) * 2 + (c + dc) % 2))
    return out


def place_pair_kernel(core_ref, own_ref, mine_ref, other_ref, out_ref):
    half = mine_ref.shape[1]
    out_ref[0] = own_ref[...]
    core = core_ref[0]
    out_ref[1, :, pl.ds(pl.multiple_of(core * half, half), half)] = mine_ref[...].astype(BF16)
    out_ref[1, :, pl.ds(pl.multiple_of((1 - core) * half, half), half)] = other_ref[...].astype(BF16)


def place_rest_kernel(core_ref, mine_ref, other_ref, head_ref, tail_ref, other_head_ref, other_tail_ref, out_ref):
    rows, half = mine_ref.shape
    core = core_ref[0]
    mine_at = pl.ds(pl.multiple_of(core * half, half), half)
    other_at = pl.ds(pl.multiple_of((1 - core) * half, half), half)
    out_ref[0, :, mine_at] = mine_ref[...].astype(BF16)
    out_ref[0, :, other_at] = other_ref[...].astype(BF16)
    out_ref[1, 0 : rows // 2, mine_at] = head_ref[...].astype(BF16)
    out_ref[1, rows // 2 : rows, mine_at] = tail_ref[...].astype(BF16)
    out_ref[1, 0 : rows // 2, other_at] = other_head_ref[...].astype(BF16)
    out_ref[1, rows // 2 : rows, other_at] = other_tail_ref[...].astype(BF16)


def place(kernel, core, rows, lanes, args, name):
    whole = pl.BlockSpec(memory_space=pltpu.VMEM)
    return pl.pallas_call(
        kernel,
        in_specs=[pl.BlockSpec(memory_space=pltpu.SMEM)] + [whole] * len(args),
        out_specs=whole,
        out_shape=jax.ShapeDtypeStruct((2, rows, lanes), BF16),
        compiler_params=pltpu.CompilerParams(vmem_limit_bytes=VMEM_LIMIT),
        name=name,
    )(core[None].astype(jnp.int32), *args)


def gather_attn(w_query, w_key, w_value, meanwhile):
    core = lax.axis_index("dp") % 2
    own = jnp.concatenate([w_query.T, w_key.T, w_value.T], axis=0)
    rows, lanes = own.shape
    half = lanes // 2
    mine = lax.dynamic_slice_in_dim(own, core * half, half, 1).astype(F32)
    swap = plane(0, 0, 1)
    after = lax.ppermute(mine, "tensor", ring(-1))
    before = lax.ppermute(mine, "tensor", ring(1))
    after, before, meanwhile = lax.optimization_barrier((after, before, meanwhile))
    head = lax.ppermute(after[: rows // 2], "tensor", ring(-1))
    tail = lax.ppermute(before[rows // 2 :], "tensor", ring(1))
    other_after = lax.ppermute(after, "dp", swap)
    other_before = lax.ppermute(before, "dp", swap)
    first = place(place_pair_kernel, core, rows, lanes, (own, after, other_after), "place_pair")

    def rest(behind):
        late_head, late_tail, behind = lax.optimization_barrier((head, tail, behind))
        other_head = lax.ppermute(late_head, "dp", swap)
        other_tail = lax.ppermute(late_tail, "dp", swap)
        args = (before, other_before, late_head, late_tail, other_head, other_tail)
        return place(place_rest_kernel, core, rows, lanes, args, "place_rest"), behind

    return first, rest, meanwhile


def gather_mlp(w_in, w_gate, w_down, w_attn_out):
    at = lax.axis_index("dp")
    core, z, y = at % 2, (at // 2) % 4, at // 8
    half = w_down.shape[1] // 2
    count = w_down.shape[0] // 4
    short = w_attn_out.shape[0] // 4
    tall_in = lax.dynamic_slice(w_in, (core * half, z * count), (half, count)).T
    tall_gate = lax.dynamic_slice(w_gate, (core * half, z * count), (half, count)).T
    down = lax.dynamic_slice(w_down, (z * count, core * half), (count, half))
    out = lax.dynamic_slice(w_attn_out, (z * short, core * half), (short, half))
    out = jnp.pad(out, ((0, count - short), (0, 0)))
    piece = jnp.where(y == 0, tall_in, jnp.where(y == 1, tall_gate, jnp.where(y == 2, down, out))).astype(F32)
    whole = lax.all_gather(piece, ("dp", "tensor"), axis=0, tiled=False)
    return whole.reshape(4, 4, 2, 4, count, half)


def mlp_kernel(
    at_ref,
    w_ref,
    x_ref,
    mix0_ref,
    mix1_ref,
    cot_ref,
    live_ref,
    gain_ref,
    out_ref,
    resid_ref,
    low_ref,
    mixg_ref,
    n_ref,
    hid_ref,
    gug_ref,
    go_ref,
    gain_out_ref,
    up_w,
    gt_w,
    dn_w,
    o_w,
):
    step = pl.program_id(0)
    quarters, halves, count, half = w_ref.shape[1], w_ref.shape[2], w_ref.shape[4], w_ref.shape[5]
    loads = 4

    def load(dst, rows):
        for r in range(4):
            rank = lax.rem(at_ref[0] + (r ^ (r >> 1)), 4)
            at = slice(r * quarters * rows, (r + 1) * quarters * rows)
            for c in range(halves):
                block = jnp.concatenate([w_ref[0, z, c, rank, 0:rows, :] for z in range(quarters)], axis=0)
                dst[at, c * half : (c + 1) * half] = block.astype(BF16)

    for kind, (dst, rows) in enumerate(((up_w, count), (gt_w, count), (dn_w, count), (o_w, o_w.shape[0] // 16))):

        @pl.when(step == kind)
        def _(dst=dst, rows=rows):
            load(dst, rows)

    @pl.when(step >= loads)
    def _():
        split = mix0_ref.shape[1]
        gain = gain_ref[...]
        resid = x_ref[...].astype(F32) + dot(mix0_ref[...], o_w[0:split, :]) + dot(mix1_ref[...], o_w[split:, :])
        centre = jnp.mean(resid, axis=-1, keepdims=True)
        centred = resid - centre
        inv = lax.rsqrt(jnp.mean(centred * centred, axis=-1, keepdims=True) + 1e-05)
        unit = centred * inv
        n = (unit * gain).astype(BF16)
        n_ref[...] = n
        up = outer_cols(n, up_w[...])
        gate = outer_cols(n, gt_w[...])
        go = cot_ref[...].astype(F32) * live_ref[...]
        go_low = go.astype(BF16)
        go_ref[...] = go_low
        gh = outer_cols(go_low, dn_w[...])
        bell = jnp.exp(up * up * -0.5)
        t = 1.0 / (1.0 + (0.3275911 * 0.7071067811865476) * jnp.abs(up))
        poly = t * (
            0.5 * 0.254829592
            + t * (0.5 * -0.284496736 + t * (0.5 * 1.421413741 + t * (0.5 * -1.453152027 + t * (0.5 * 1.061405429))))
        )
        tail = poly * bell
        cdf = jnp.where(up >= 0.0, 1.0 - tail, tail)
        act = up * cdf
        slope = cdf + up * bell * 0.3989422804014327
        hid = (act * gate).astype(BF16)
        gup = (gh * gate * slope).astype(BF16)
        ggt = (gh * act).astype(BF16)
        own = hid_ref.shape[1]
        hid_ref[...] = hid[:, :own]
        gug_ref[...] = jnp.concatenate([gup[:, :own], ggt[:, :own]], axis=1)
        out_ref[...] = (resid + dot(hid, dn_w[...])).astype(BF16)
        gn = dot(gup, up_w[...]) + dot(ggt, gt_w[...])
        scaled = gn * gain
        first = jnp.mean(scaled, axis=-1, keepdims=True)
        second = jnp.mean(scaled * unit, axis=-1, keepdims=True)
        grad = go + inv * (scaled - first - unit * second)
        resid_ref[...] = grad
        low = grad.astype(BF16)
        low_ref[...] = low
        mixg_ref[...] = outer_cols(low, o_w[...]).astype(BF16)
        terms = jnp.sum(gn * unit, axis=0, keepdims=True)

        @pl.when(step == loads)
        def _():
            gain_out_ref[...] = terms

        @pl.when(step > loads)
        def _():
            gain_out_ref[...] += terms


def mlp(weights, tokens, mix0, mix1, cotangent, live, gain):
    rows, width = tokens.shape
    block, loads = 256, 4
    quarters, halves, count, half = weights.shape[1], weights.shape[2], weights.shape[4], weights.shape[5]
    own = quarters * count
    ff = 4 * own

    def at_row(i, _):
        return (jnp.maximum(i - loads, 0), 0)

    def at_weight(i, at):
        return (jnp.minimum(i, loads - 1), 0, 0, 0, 0, 0)

    def row(cols):
        return pl.BlockSpec((block, cols), at_row)

    def fixed(i, _):
        return (0, 0)

    def shape(cols, kind):
        return jax.ShapeDtypeStruct((rows, cols), kind)

    split = mix0.shape[1]
    return pl.pallas_call(
        mlp_kernel,
        grid_spec=pltpu.PrefetchScalarGridSpec(
            num_scalar_prefetch=1,
            grid=(loads + rows // block,),
            in_specs=[
                pl.BlockSpec((1, quarters, halves, 4, count, half), at_weight),
                row(width),
                row(split),
                row(width - split),
                row(width),
                row(1),
                pl.BlockSpec((1, width), fixed),
            ],
            out_specs=[
                row(width),
                row(width),
                row(width),
                row(width),
                row(width),
                row(own),
                row(2 * own),
                row(width),
                pl.BlockSpec((1, width), fixed),
            ],
            scratch_shapes=[
                pltpu.VMEM((ff, width), BF16),
                pltpu.VMEM((ff, width), BF16),
                pltpu.VMEM((ff, width), BF16),
                pltpu.VMEM((width, width), BF16),
            ],
        ),
        out_shape=[
            shape(width, BF16),
            shape(width, F32),
            shape(width, BF16),
            shape(width, BF16),
            shape(width, BF16),
            shape(own, BF16),
            shape(2 * own, BF16),
            shape(width, BF16),
            jax.ShapeDtypeStruct((1, width), F32),
        ],
        compiler_params=pltpu.CompilerParams(vmem_limit_bytes=VMEM_LIMIT),
        cost_estimate=pl.CostEstimate(flops=12 * rows * width * ff, bytes_accessed=40 * 10**6, transcendentals=0),
        name="mlp",
    )(lax.axis_index("tensor")[None].astype(jnp.int32), weights, tokens, mix0, mix1, cotangent, live, gain)


def finish_kernel(x_ref, grad_ref, gain_ref, *refs):
    parts, weights, (out_ref, gain_out_ref) = refs[:6], refs[6:8], refs[8:]
    total = None
    for half in range(2):
        w_ref = weights[half]
        count = w_ref.shape[1] // 3
        for part in range(3):
            w = jnp.concatenate([w_ref[r, part * count : (part + 1) * count, :] for r in range(w_ref.shape[0])], axis=0)
            term = dot(parts[half * 3 + part][...], w)
            total = term if total is None else total + term
    back, terms = norm_back(x_ref[...].astype(F32), gain_ref[...], total)
    out_ref[...] = grad_ref[...] + back
    terms = jnp.sum(terms, axis=0, keepdims=True)

    @pl.when(pl.program_id(0) == 0)
    def _():
        gain_out_ref[...] = terms

    @pl.when(pl.program_id(0) > 0)
    def _():
        gain_out_ref[...] += terms


def finish(tokens, grad_resid, gain, parts, weights):
    rows, width = tokens.shape
    block = 256

    def row(cols):
        return pl.BlockSpec((block, cols), lambda i: (i, 0))

    fixed = pl.BlockSpec((1, width), lambda i: (0, 0))
    return pl.pallas_call(
        finish_kernel,
        grid=(rows // block,),
        in_specs=[row(width), row(width), fixed]
        + [row(p.shape[1]) for p in parts]
        + [pl.BlockSpec(w.shape, lambda i: (0, 0, 0)) for w in weights],
        out_specs=[row(width), fixed],
        out_shape=[jax.ShapeDtypeStruct((rows, width), F32), jax.ShapeDtypeStruct((1, width), F32)],
        compiler_params=pltpu.CompilerParams(vmem_limit_bytes=VMEM_LIMIT),
        cost_estimate=pl.CostEstimate(flops=8 * 10**9, bytes_accessed=10**7, transcendentals=0),
        name="finish",
    )(tokens, grad_resid, gain, *parts, *weights)


def rows_at(array, place, count):
    return lax.dynamic_slice_in_dim(array, place * count, count, 0)


def halves_summed(pairs):
    core = lax.axis_index("dp") % 2

    def half(at):
        lanes = pairs[0][1].shape[1] // 2
        terms = [inner_rows(a, lax.dynamic_slice_in_dim(b, at * lanes, lanes, 1)) for a, b in pairs]
        return jnp.concatenate(terms, axis=0) if len(terms) > 1 else terms[0]

    return half(core) + lax.ppermute(half(1 - core), "dp", plane(0, 0, 1))


def whole_of(done):
    got = lax.ppermute(done, "dp", plane(0, 0, 1))
    first = lax.axis_index("dp") % 2 == 0
    return jnp.concatenate([jnp.where(first, done, got), jnp.where(first, got, done)], axis=1)


def ring_place(axis):
    at = lax.axis_index("dp")
    return at // 8 if axis == "y" else (at // 2) % 4


def ring_move(axis, d):
    return plane(d, 0) if axis == "y" else plane(0, d)


def split_ring(half, axis):
    quarter = half.shape[0] // 4
    place = ring_place(axis)
    return [rows_at(half, (place + d) % 4, quarter) for d in range(4)]


def sum_ring(blocks, axis):
    total = blocks[0]
    for d in (1, 2, 3):
        total = total + lax.ppermute(blocks[d], "dp", ring_move(axis, d))
    return total


def in_order(blocks, axis):
    place = ring_place(axis)
    return jnp.concatenate([lax.select_n(lax.rem(place - j + 4, 4), *blocks) for j in range(4)], axis=0)


def far_by_half(blocks, axis):
    half = blocks[2].shape[0] // 16 * 8
    head = lax.ppermute(blocks[2][:half], "dp", ring_move(axis, 1))
    tail = lax.ppermute(blocks[2][half:], "dp", ring_move(axis, -1))
    after = jnp.concatenate([blocks[1][:half] + head, blocks[1][half:]], axis=0)
    before = jnp.concatenate([blocks[3][:half], blocks[3][half:] + tail], axis=0)
    return blocks[0], after, before


def sum_neighbours(parts, axis):
    own, after, before = parts
    return own + lax.ppermute(after, "dp", ring_move(axis, 1)) + lax.ppermute(before, "dp", ring_move(axis, -1))


def spread_ring(block, axis):
    return [block] + [lax.ppermute(block, "dp", ring_move(axis, d)) for d in (1, 2, 3)]


def spread_ring_twice(block, axis):
    half = block.shape[0] // 16 * 8
    before = lax.ppermute(block, "dp", ring_move(axis, 1))
    after = lax.ppermute(block, "dp", ring_move(axis, -1))
    head = lax.ppermute(before[:half], "dp", ring_move(axis, 1))
    tail = lax.ppermute(after[half:], "dp", ring_move(axis, -1))
    return [block, before, jnp.concatenate([head, tail], axis=0), after]


def body(
    tokens,
    cotangent,
    seq_len,
    seq_slot,
    attn_gain,
    w_query,
    w_key,
    w_value,
    w_attn_out,
    mlp_gain,
    w_in,
    w_gate,
    w_down,
):
    rows, width = tokens.shape
    heads_cols = w_query.shape[1]
    per_group = 2
    slots = lax.axis_index("dp") * per_group + jnp.arange(per_group, dtype=jnp.int32)
    lengths = jnp.sum(jnp.where(seq_slot[None, :] == slots[:, None], seq_len[None, :], 0), axis=1)
    end0, end1 = lengths[0], lengths[0] + lengths[1]

    def segment_of(index):
        return (index >= end0).astype(jnp.int32) + (index >= end1).astype(jnp.int32)

    index = lax.broadcasted_iota(jnp.int32, (rows, PAIR), 0)
    position = index - jnp.where(index >= end1, end1, jnp.where(index >= end0, end0, 0))
    lane = lax.broadcasted_iota(jnp.int32, (rows, PAIR), 1)
    width_half = HEAD_DIM // 2
    frequency = 10000.0 ** (-(jnp.arange(width_half, dtype=F32) * 2.0 / HEAD_DIM))
    frequency = jnp.tile(frequency, PAIR // width_half)
    phase = position.astype(F32) * frequency[None, :]
    cos = jnp.cos(phase)
    sin = jnp.where(lane % HEAD_DIM < width_half, -1.0, 1.0) * jnp.sin(phase)
    shape = (rows // QB, KB, QB)
    block_at = lax.broadcasted_iota(jnp.int32, shape, 0) * QB
    row_at = block_at + lax.broadcasted_iota(jnp.int32, shape, 2)
    col_at = block_at + lax.broadcasted_iota(jnp.int32, shape, 1) - HALF
    allowed = (
        (segment_of(row_at) == segment_of(col_at))
        & (jnp.abs(row_at - col_at) <= HALF)
        & (col_at >= 0)
        & (col_at < rows)
    )
    bias = jnp.where(allowed, 0.0, -1e30).astype(F32)
    live = (jnp.arange(rows, dtype=jnp.int32) < end1).astype(F32)

    weights_mlp = gather_mlp(w_in, w_gate, w_down, w_attn_out)
    weights0, rest, (cos, sin, cos_t, sin_t, bias) = gather_attn(
        w_query, w_key, w_value, (cos, sin, cos.T, sin.T, bias)
    )
    gain1 = attn_gain[None, :]
    normed1, *qkv0 = project_qkv(tokens, gain1, weights0, cos, sin)
    mix0, prob0 = attend(*qkv0, bias)
    weights1, mix0 = rest(mix0)
    weights_attn = (weights0, weights1)
    qkv1 = project_qkv(normed1, None, weights_attn[1], cos, sin)
    mix1, prob1 = attend(*qkv1, bias)
    (
        mixed_out,
        grad_resid,
        grad_resid_low,
        grad_mix,
        normed2,
        hidden,
        grad_up_gate,
        grad_out_low,
        gain2_sum,
    ) = mlp(weights_mlp, tokens, mix0, mix1, cotangent, live[:, None], mlp_gain[None, :])
    ff_cols = w_in.shape[1]
    spare = jnp.zeros((rows, -(3 * ff_cols + heads_cols) % 128), BF16)
    early = halves_summed(
        [
            (grad_up_gate, normed2),
            (hidden, grad_out_low),
            (jnp.concatenate([mix0[:, :heads_cols], spare], axis=1), grad_resid_low),
        ]
    )
    early = split_ring(early, "y")
    early, grad_mix = lax.optimization_barrier((early, grad_mix))
    split = mix0.shape[1]
    tables = (cos, sin, cos_t, sin_t)
    back0 = attend_back(*qkv0, grad_mix[:, :split], prob0, *tables)
    spare = jnp.zeros((rows, -(3 * heads_cols) % 128), BF16)
    early, back0 = lax.optimization_barrier((far_by_half(early, "y"), back0))
    own_grads = jnp.concatenate([g[:, :heads_cols] for g in back0] + [spare], axis=1)
    late = split_ring(halves_summed([(own_grads, normed1)]), "z")
    early, late, next_in = lax.optimization_barrier((early, late, grad_mix[:, split:]))
    back1 = attend_back(*qkv1, next_in, prob1, *tables)
    late, back1 = lax.optimization_barrier((far_by_half(late, "z"), back1))
    grad_tokens, gain1_sum = finish(tokens, grad_resid, gain1, [*back0, *back1], weights_attn)
    early = split_ring(sum_neighbours(early, "y"), "z")
    late = split_ring(sum_neighbours(late, "z"), "y")
    early, late = lax.optimization_barrier((early, late))
    early, late = lax.optimization_barrier((sum_ring(early, "z"), sum_ring(late, "y")))
    lanes = width // 2
    small = jnp.concatenate([gain1_sum[0], gain2_sum[0]])
    small = jnp.pad(small, (0, 8 * lanes - small.shape[0])).reshape(8, lanes)
    got_early = spread_ring(early, "z")
    got_late = spread_ring(jnp.concatenate([late, small], axis=0), "y")
    count = late.shape[0]
    small = sum(g[count:] for g in got_late)
    early = in_order(got_early, "z")
    late = in_order([g[:count] for g in got_late], "y")
    early, late, small = lax.optimization_barrier((early, late, small))
    got_late = spread_ring(jnp.concatenate([late, small], axis=0), "z")
    got_early = spread_ring_twice(early, "y")
    count = late.shape[0]
    small = sum(g[count:] for g in got_late)
    late = in_order([g[:count] for g in got_late], "z")
    early = in_order(got_early, "y")
    count = late.shape[0]
    late = whole_of(jnp.concatenate([late, small], axis=0))
    small = (late[count:, :lanes] + late[count:, lanes:]).reshape(-1)
    early = whole_of(early)
    return (
        mixed_out,
        grad_tokens,
        small[:width],
        late[:heads_cols].T,
        late[heads_cols : 2 * heads_cols].T,
        late[2 * heads_cols : 3 * heads_cols].T,
        early[3 * ff_cols : 3 * ff_cols + heads_cols],
        small[width : 2 * width],
        early[:ff_cols].T,
        early[ff_cols : 2 * ff_cols].T,
        early[2 * ff_cols : 3 * ff_cols],
    )


def solution(mesh):
    rows, cols, all_of = P("dp", None), P(None, "tensor"), P()
    tall = P("tensor", None)
    return jax.shard_map(
        body,
        mesh=mesh,
        in_specs=(rows, rows, all_of, all_of, all_of, cols, cols, cols, tall, all_of, cols, cols, tall),
        out_specs=(rows, rows, all_of, cols, cols, cols, tall, all_of, cols, cols, tall),
        check_vma=False,
    )
```

```python
import jax
import jax.numpy as jnp
from jax import lax
from jax.experimental import pallas as pl
from jax.experimental.pallas import tpu as pltpu
from jax.sharding import PartitionSpec as P

HEAD_DIM = 64
HALF = 64
QB = 128
KB = QB + 2 * HALF
PAIR = 2 * HEAD_DIM
STAGED = 4
STAGED_BACK = 4
F32 = jnp.float32
BF16 = jnp.bfloat16
VMEM_LIMIT = 48 * 1024 * 1024


def dot(a, b):
    return jnp.dot(a, b, preferred_element_type=F32)


def inner_rows(left, right):
    return lax.dot_general(left, right, (((0,), (0,)), ((), ())), preferred_element_type=F32)


def outer_cols(left, right):
    return lax.dot_general(left, right, (((1,), (1,)), ((), ())), preferred_element_type=F32)


def normed(values, gain):
    centre = jnp.mean(values, axis=-1, keepdims=True)
    centred = values - centre
    spread = jnp.mean(centred * centred, axis=-1, keepdims=True)
    return centred * lax.rsqrt(spread + 1e-05) * gain


def norm_back(values, gain, grad):
    centre = jnp.mean(values, axis=-1, keepdims=True)
    centred = values - centre
    spread = jnp.mean(centred * centred, axis=-1, keepdims=True)
    inv = lax.rsqrt(spread + 1e-05)
    unit = centred * inv
    scaled = grad * gain
    first = jnp.mean(scaled, axis=-1, keepdims=True)
    second = jnp.mean(scaled * unit, axis=-1, keepdims=True)
    return inv * (scaled - first - unit * second), grad * unit


def swap_halves(v):
    lane = lax.broadcasted_iota(jnp.int32, v.shape, 1)
    low_half = lax.rem(lane, HEAD_DIM) < HEAD_DIM // 2
    return jnp.where(low_half, pltpu.roll(v, PAIR - HEAD_DIM // 2, 1), pltpu.roll(v, HEAD_DIM // 2, 1))


def rope(v, cos, sin):
    return v * cos + swap_halves(v) * sin


def write_qkv(n, w_ref, cos_ref, sin_ref, q_ref, k_ref, v_ref):
    count = w_ref.shape[1] // 3

    def weight(part):
        return jnp.concatenate([w_ref[r, part * count : (part + 1) * count, :] for r in range(w_ref.shape[0])], axis=0)

    cos, sin = cos_ref[...], sin_ref[...]
    q = outer_cols(n, weight(0))
    k = outer_cols(n, weight(1))
    for j in range(q.shape[1] // PAIR):
        cols = slice(j * PAIR, (j + 1) * PAIR)
        q_ref[:, cols] = (rope(q[:, cols], cos, sin) * (1.0 / HEAD_DIM**0.5)).astype(BF16)
        k_ref[:, cols] = rope(k[:, cols], cos, sin).astype(BF16)
    v_ref[...] = outer_cols(n, weight(2)).astype(BF16)


def norm_qkv_kernel(x_ref, gain_ref, w_ref, cos_ref, sin_ref, n_ref, q_ref, k_ref, v_ref):
    n = normed(x_ref[...].astype(F32), gain_ref[...]).astype(BF16)
    n_ref[...] = n
    write_qkv(n, w_ref, cos_ref, sin_ref, q_ref, k_ref, v_ref)


def only_qkv_kernel(n_ref, w_ref, cos_ref, sin_ref, q_ref, k_ref, v_ref):
    write_qkv(n_ref[...], w_ref, cos_ref, sin_ref, q_ref, k_ref, v_ref)


def project_qkv(rows_in, gain, pack, cos, sin):
    rows, width = rows_in.shape
    cols = pack.shape[0] * pack.shape[1] // 3
    block = 256
    row_spec = pl.BlockSpec((block, width), lambda i: (i, 0))
    out_spec = pl.BlockSpec((block, cols), lambda i: (i, 0))
    gain_spec = pl.BlockSpec((1, width), lambda i: (0, 0))
    w_spec = pl.BlockSpec(pack.shape, lambda i: (0, 0, 0))
    tab_spec = pl.BlockSpec((block, PAIR), lambda i: (i, 0))
    first = gain is not None
    return pl.pallas_call(
        norm_qkv_kernel if first else only_qkv_kernel,
        grid=(rows // block,),
        in_specs=[row_spec] + [gain_spec] * first + [w_spec, tab_spec, tab_spec],
        out_specs=[row_spec] * first + [out_spec] * 3,
        out_shape=[jax.ShapeDtypeStruct((rows, width), BF16)] * first + [jax.ShapeDtypeStruct((rows, cols), BF16)] * 3,
        compiler_params=pltpu.CompilerParams(vmem_limit_bytes=VMEM_LIMIT),
        cost_estimate=pl.CostEstimate(
            flops=8 * rows * width * cols, bytes_accessed=8 * rows * width + 6 * width * cols, transcendentals=0
        ),
        name="norm_qkv" if first else "qkv",
    )(*([rows_in] + [gain] * first + [pack, cos, sin]))


def pad_rows(dst, src):
    rows = src.shape[0]
    edge = jnp.zeros((HALF, PAIR), dst.dtype)
    dst[0:HALF, :] = edge
    dst[HALF : HALF + rows, :] = src
    dst[HALF + rows : rows + 2 * HALF, :] = edge


def split_lanes(src, first, second):
    lane = lax.broadcasted_iota(jnp.int32, src.shape, 1)
    zero = jnp.zeros_like(src)
    first[...] = jnp.where(lane < HEAD_DIM, src, zero)
    second[...] = jnp.where(lane < HEAD_DIM, zero, src)


def query_rows(i):
    return slice(i * QB, (i + 1) * QB)


def key_rows(i):
    return slice(i * QB, i * QB + KB)


def head_rows(h):
    return slice(h * HEAD_DIM, (h + 1) * HEAD_DIM)


def attend_kernel(q_ref, k_ref, v_ref, bias_ref, o_ref, p_ref, pad, k0, k1, vt):
    rows = q_ref.shape[0]
    pad_rows(pad, v_ref[...])
    vt[...] = pad[...].T
    pad_rows(pad, k_ref[...])
    split_lanes(pad[...], k0, k1)
    for start in range(0, rows // QB, STAGED):
        blocks = range(start, start + STAGED)
        units = [(i, h) for i in blocks for h in range(2)]
        q_t = {i: q_ref[query_rows(i), :].T for i in blocks}
        scores = [dot((k0, k1)[h][key_rows(i), :], q_t[i]) + bias_ref[i] for i, h in units]
        tops = [jnp.max(s, axis=0, keepdims=True) for s in scores]
        expos = [jnp.exp(s - top) for s, top in zip(scores, tops)]
        shares = [1.0 / jnp.sum(e, axis=0, keepdims=True) for e in expos]
        probs = [(e * share).astype(BF16) for e, share in zip(expos, shares)]
        outs = [dot(vt[head_rows(h), key_rows(i)], p) for (i, h), p in zip(units, probs)]
        for (i, h), p in zip(units, probs):
            p_ref[0, i, :, h * QB : (h + 1) * QB] = p
        for n, i in enumerate(blocks):
            o_ref[query_rows(i), :] = jnp.concatenate(outs[2 * n : 2 * n + 2], axis=0).astype(BF16).T


def attend(q, k, v, bias):
    rows, width = q.shape
    pairs, blocks = width // PAIR, rows // QB
    spec = pl.BlockSpec((rows, PAIR), lambda j: (0, j))
    padded = rows + 2 * HALF
    return pl.pallas_call(
        attend_kernel,
        grid=(pairs,),
        in_specs=[spec, spec, spec, pl.BlockSpec((blocks, KB, QB), lambda j: (0, 0, 0))],
        out_specs=[spec, pl.BlockSpec((1, blocks, KB, 2 * QB), lambda j: (j, 0, 0, 0))],
        out_shape=[
            jax.ShapeDtypeStruct((rows, width), BF16),
            jax.ShapeDtypeStruct((pairs, blocks, KB, 2 * QB), BF16),
        ],
        scratch_shapes=[pltpu.VMEM((padded, PAIR), BF16)] * 3 + [pltpu.VMEM((PAIR, padded), BF16)],
        compiler_params=pltpu.CompilerParams(vmem_limit_bytes=VMEM_LIMIT),
        cost_estimate=pl.CostEstimate(flops=2 * 10**9 * pairs, bytes_accessed=2 * rows * width * 8, transcendentals=0),
        name="attend",
    )(q, k, v, bias)


def swap_rows(v):
    quarter = HEAD_DIM // 2
    part = [v[i * quarter : (i + 1) * quarter, :] for i in range(4)]
    return jnp.concatenate([part[1], part[0], part[3], part[2]], axis=0)


def both_heads(v):
    lane = lax.broadcasted_iota(jnp.int32, v.shape, 1)
    zero = jnp.zeros_like(v)
    return jnp.concatenate([jnp.where(lane < HEAD_DIM, v, zero), jnp.where(lane < HEAD_DIM, zero, v)], axis=0)


def attend_back_kernel(
    q_ref, k_ref, v_ref, g_ref, p_ref, cos_ref, sin_ref, cos_t, sin_t, gq_ref, gk_ref, gv_ref, pad, v0, v1, kt, gk, gv
):
    rows = q_ref.shape[0]
    scale = 1.0 / HEAD_DIM**0.5
    pad_rows(pad, k_ref[...])
    kt[...] = pad[...].T
    pad_rows(pad, v_ref[...])
    split_lanes(pad[...], v0, v1)
    gk[...] = jnp.zeros_like(gk)
    gv[...] = jnp.zeros_like(gv)
    for start in range(0, rows // QB, STAGED_BACK):
        blocks = range(start, start + STAGED_BACK)
        units = [(i, h) for i in blocks for h in range(2)]
        g_t = {i: g_ref[query_rows(i), :].T for i in blocks}
        gps = [dot((v0, v1)[h][key_rows(i), :], g_t[i]) for i, h in units]
        probs = [p_ref[0, i, :, h * QB : (h + 1) * QB].astype(F32) for i, h in units]
        sums = [jnp.sum(p * gp, axis=0, keepdims=True) for p, gp in zip(probs, gps)]
        grads = [(p * (gp - total)).astype(BF16) for p, gp, total in zip(probs, gps, sums)]
        outs = [dot(kt[head_rows(h), key_rows(i)], gs) for (i, h), gs in zip(units, grads)]
        gks = [
            dot(jnp.concatenate(grads[2 * n : 2 * n + 2], axis=1), both_heads(q_ref[query_rows(i), :]))
            for n, i in enumerate(blocks)
        ]
        gvs = [dot(p_ref[0, i], both_heads(g_ref[query_rows(i), :])) for i in blocks]
        for n, i in enumerate(blocks):
            at = query_rows(i)
            gk[key_rows(i), :] += gks[n]
            gv[key_rows(i), :] += gvs[n]
            gq = jnp.concatenate(outs[2 * n : 2 * n + 2], axis=0) * scale
            gq_ref[at, :] = (gq * cos_t[:, at] - swap_rows(gq) * sin_t[:, at]).astype(BF16).T
    gk_ref[...] = rope(gk[HALF : HALF + rows, :], cos_ref[...], -sin_ref[...]).astype(BF16)
    gv_ref[...] = gv[HALF : HALF + rows, :].astype(BF16)


def attend_back(q, k, v, g, prob, cos, sin, cos_t, sin_t):
    rows, width = q.shape
    pairs, blocks = width // PAIR, rows // QB
    spec = pl.BlockSpec((rows, PAIR), lambda j: (0, j))
    tab_spec = pl.BlockSpec((rows, PAIR), lambda j: (0, 0))
    tab_t_spec = pl.BlockSpec((PAIR, rows), lambda j: (0, 0))
    padded = rows + 2 * HALF
    return pl.pallas_call(
        attend_back_kernel,
        grid=(pairs,),
        in_specs=[spec] * 4
        + [pl.BlockSpec((1, blocks, KB, 2 * QB), lambda j: (j, 0, 0, 0)), tab_spec, tab_spec, tab_t_spec, tab_t_spec],
        out_specs=[spec] * 3,
        out_shape=[jax.ShapeDtypeStruct((rows, width), BF16)] * 3,
        scratch_shapes=[pltpu.VMEM((padded, PAIR), BF16)] * 3
        + [pltpu.VMEM((PAIR, padded), BF16)]
        + [pltpu.VMEM((padded, PAIR), F32)] * 2,
        compiler_params=pltpu.CompilerParams(vmem_limit_bytes=VMEM_LIMIT),
        cost_estimate=pl.CostEstimate(flops=8 * 10**9, bytes_accessed=10**7, transcendentals=0),
        name="attend_back",
    )(q, k, v, g, prob, cos, sin, cos_t, sin_t)


def ring(step):
    size = lax.axis_size("tensor")
    return [(i, (i + step) % size) for i in range(size)]


def plane(dy, dz, dc=0):
    size = lax.axis_size("dp")
    out = []
    for i in range(size):
        y, z, c = i // 8, (i // 2) % 4, i % 2
        out.append((i, (((y + dy) % 4) * 4 + (z + dz) % 4) * 2 + (c + dc) % 2))
    return out


def place_pair_kernel(core_ref, own_ref, mine_ref, other_ref, out_ref):
    half = mine_ref.shape[1]
    out_ref[0] = own_ref[...]
    core = core_ref[0]
    out_ref[1, :, pl.ds(pl.multiple_of(core * half, half), half)] = mine_ref[...].astype(BF16)
    out_ref[1, :, pl.ds(pl.multiple_of((1 - core) * half, half), half)] = other_ref[...].astype(BF16)


def place_rest_kernel(core_ref, mine_ref, other_ref, head_ref, tail_ref, other_head_ref, other_tail_ref, out_ref):
    rows, half = mine_ref.shape
    core = core_ref[0]
    mine_at = pl.ds(pl.multiple_of(core * half, half), half)
    other_at = pl.ds(pl.multiple_of((1 - core) * half, half), half)
    out_ref[0, :, mine_at] = mine_ref[...].astype(BF16)
    out_ref[0, :, other_at] = other_ref[...].astype(BF16)
    out_ref[1, 0 : rows // 2, mine_at] = head_ref[...].astype(BF16)
    out_ref[1, rows // 2 : rows, mine_at] = tail_ref[...].astype(BF16)
    out_ref[1, 0 : rows // 2, other_at] = other_head_ref[...].astype(BF16)
    out_ref[1, rows // 2 : rows, other_at] = other_tail_ref[...].astype(BF16)


def place(kernel, core, rows, lanes, args, name):
    whole = pl.BlockSpec(memory_space=pltpu.VMEM)
    return pl.pallas_call(
        kernel,
        in_specs=[pl.BlockSpec(memory_space=pltpu.SMEM)] + [whole] * len(args),
        out_specs=whole,
        out_shape=jax.ShapeDtypeStruct((2, rows, lanes), BF16),
        compiler_params=pltpu.CompilerParams(vmem_limit_bytes=VMEM_LIMIT),
        name=name,
    )(core[None].astype(jnp.int32), *args)


def gather_attn(w_query, w_key, w_value, meanwhile):
    core = lax.axis_index("dp") % 2
    own = jnp.concatenate([w_query.T, w_key.T, w_value.T], axis=0)
    rows, lanes = own.shape
    half = lanes // 2
    mine = lax.dynamic_slice_in_dim(own, core * half, half, 1).astype(F32)
    swap = plane(0, 0, 1)
    after = lax.ppermute(mine, "tensor", ring(-1))
    before = lax.ppermute(mine, "tensor", ring(1))
    after, before, meanwhile = lax.optimization_barrier((after, before, meanwhile))
    head = lax.ppermute(after[: rows // 2], "tensor", ring(-1))
    tail = lax.ppermute(before[rows // 2 :], "tensor", ring(1))
    other_after = lax.ppermute(after, "dp", swap)
    other_before = lax.ppermute(before, "dp", swap)
    first = place(place_pair_kernel, core, rows, lanes, (own, after, other_after), "place_pair")

    def rest(behind):
        late_head, late_tail, behind = lax.optimization_barrier((head, tail, behind))
        other_head = lax.ppermute(late_head, "dp", swap)
        other_tail = lax.ppermute(late_tail, "dp", swap)
        args = (before, other_before, late_head, late_tail, other_head, other_tail)
        return place(place_rest_kernel, core, rows, lanes, args, "place_rest"), behind

    return first, rest, meanwhile


def gather_mlp(w_in, w_gate, w_down, w_attn_out):
    at = lax.axis_index("dp")
    core, z, y = at % 2, (at // 2) % 4, at // 8
    half = w_down.shape[1] // 2
    count = w_down.shape[0] // 4
    short = w_attn_out.shape[0] // 4
    tall_in = lax.dynamic_slice(w_in, (core * half, z * count), (half, count)).T
    tall_gate = lax.dynamic_slice(w_gate, (core * half, z * count), (half, count)).T
    down = lax.dynamic_slice(w_down, (z * count, core * half), (count, half))
    out = lax.dynamic_slice(w_attn_out, (z * short, core * half), (short, half))
    out = jnp.pad(out, ((0, count - short), (0, 0)))
    piece = jnp.where(y == 0, tall_in, jnp.where(y == 1, tall_gate, jnp.where(y == 2, down, out))).astype(F32)
    whole = lax.all_gather(piece, ("dp", "tensor"), axis=0, tiled=False)
    return whole.reshape(4, 4, 2, 4, count, half)


def mlp_kernel(
    at_ref,
    w_ref,
    x_ref,
    mix0_ref,
    mix1_ref,
    cot_ref,
    live_ref,
    gain_ref,
    out_ref,
    resid_ref,
    low_ref,
    mixg_ref,
    n_ref,
    hid_ref,
    gug_ref,
    go_ref,
    gain_out_ref,
    up_w,
    gt_w,
    dn_w,
    o_w,
):
    step = pl.program_id(0)
    quarters, halves, count, half = w_ref.shape[1], w_ref.shape[2], w_ref.shape[4], w_ref.shape[5]
    loads = 4

    def load(dst, rows):
        for r in range(4):
            rank = lax.rem(at_ref[0] + (r ^ (r >> 1)), 4)
            at = slice(r * quarters * rows, (r + 1) * quarters * rows)
            for c in range(halves):
                block = jnp.concatenate([w_ref[0, z, c, rank, 0:rows, :] for z in range(quarters)], axis=0)
                dst[at, c * half : (c + 1) * half] = block.astype(BF16)

    for kind, (dst, rows) in enumerate(((up_w, count), (gt_w, count), (dn_w, count), (o_w, o_w.shape[0] // 16))):

        @pl.when(step == kind)
        def _(dst=dst, rows=rows):
            load(dst, rows)

    @pl.when(step >= loads)
    def _():
        split = mix0_ref.shape[1]
        gain = gain_ref[...]
        resid = x_ref[...].astype(F32) + dot(mix0_ref[...], o_w[0:split, :]) + dot(mix1_ref[...], o_w[split:, :])
        centre = jnp.mean(resid, axis=-1, keepdims=True)
        centred = resid - centre
        inv = lax.rsqrt(jnp.mean(centred * centred, axis=-1, keepdims=True) + 1e-05)
        unit = centred * inv
        n = (unit * gain).astype(BF16)
        n_ref[...] = n
        up = outer_cols(n, up_w[...])
        gate = outer_cols(n, gt_w[...])
        go = cot_ref[...].astype(F32) * live_ref[...]
        go_low = go.astype(BF16)
        go_ref[...] = go_low
        gh = outer_cols(go_low, dn_w[...])
        bell = jnp.exp(up * up * -0.5)
        t = 1.0 / (1.0 + (0.3275911 * 0.7071067811865476) * jnp.abs(up))
        poly = t * (
            0.5 * 0.254829592
            + t * (0.5 * -0.284496736 + t * (0.5 * 1.421413741 + t * (0.5 * -1.453152027 + t * (0.5 * 1.061405429))))
        )
        tail = poly * bell
        cdf = jnp.where(up >= 0.0, 1.0 - tail, tail)
        act = up * cdf
        slope = cdf + up * bell * 0.3989422804014327
        hid = (act * gate).astype(BF16)
        gup = (gh * gate * slope).astype(BF16)
        ggt = (gh * act).astype(BF16)
        own = hid_ref.shape[1]
        hid_ref[...] = hid[:, :own]
        gug_ref[...] = jnp.concatenate([gup[:, :own], ggt[:, :own]], axis=1)
        out_ref[...] = (resid + dot(hid, dn_w[...])).astype(BF16)
        gn = dot(gup, up_w[...]) + dot(ggt, gt_w[...])
        scaled = gn * gain
        first = jnp.mean(scaled, axis=-1, keepdims=True)
        second = jnp.mean(scaled * unit, axis=-1, keepdims=True)
        grad = go + inv * (scaled - first - unit * second)
        resid_ref[...] = grad
        low = grad.astype(BF16)
        low_ref[...] = low
        mixg_ref[...] = outer_cols(low, o_w[...]).astype(BF16)
        terms = jnp.sum(gn * unit, axis=0, keepdims=True)

        @pl.when(step == loads)
        def _():
            gain_out_ref[...] = terms

        @pl.when(step > loads)
        def _():
            gain_out_ref[...] += terms


def mlp(weights, tokens, mix0, mix1, cotangent, live, gain):
    rows, width = tokens.shape
    block, loads = 256, 4
    quarters, halves, count, half = weights.shape[1], weights.shape[2], weights.shape[4], weights.shape[5]
    own = quarters * count
    ff = 4 * own

    def at_row(i, _):
        return (jnp.maximum(i - loads, 0), 0)

    def at_weight(i, at):
        return (jnp.minimum(i, loads - 1), 0, 0, 0, 0, 0)

    def row(cols):
        return pl.BlockSpec((block, cols), at_row)

    def fixed(i, _):
        return (0, 0)

    def shape(cols, kind):
        return jax.ShapeDtypeStruct((rows, cols), kind)

    split = mix0.shape[1]
    return pl.pallas_call(
        mlp_kernel,
        grid_spec=pltpu.PrefetchScalarGridSpec(
            num_scalar_prefetch=1,
            grid=(loads + rows // block,),
            in_specs=[
                pl.BlockSpec((1, quarters, halves, 4, count, half), at_weight),
                row(width),
                row(split),
                row(width - split),
                row(width),
                row(1),
                pl.BlockSpec((1, width), fixed),
            ],
            out_specs=[
                row(width),
                row(width),
                row(width),
                row(width),
                row(width),
                row(own),
                row(2 * own),
                row(width),
                pl.BlockSpec((1, width), fixed),
            ],
            scratch_shapes=[
                pltpu.VMEM((ff, width), BF16),
                pltpu.VMEM((ff, width), BF16),
                pltpu.VMEM((ff, width), BF16),
                pltpu.VMEM((width, width), BF16),
            ],
        ),
        out_shape=[
            shape(width, BF16),
            shape(width, F32),
            shape(width, BF16),
            shape(width, BF16),
            shape(width, BF16),
            shape(own, BF16),
            shape(2 * own, BF16),
            shape(width, BF16),
            jax.ShapeDtypeStruct((1, width), F32),
        ],
        compiler_params=pltpu.CompilerParams(vmem_limit_bytes=VMEM_LIMIT),
        cost_estimate=pl.CostEstimate(flops=12 * rows * width * ff, bytes_accessed=40 * 10**6, transcendentals=0),
        name="mlp",
    )(lax.axis_index("tensor")[None].astype(jnp.int32), weights, tokens, mix0, mix1, cotangent, live, gain)


def finish_kernel(x_ref, grad_ref, gain_ref, *refs):
    parts, weights, (out_ref, gain_out_ref) = refs[:6], refs[6:8], refs[8:]
    total = None
    for half in range(2):
        w_ref = weights[half]
        count = w_ref.shape[1] // 3
        for part in range(3):
            w = jnp.concatenate([w_ref[r, part * count : (part + 1) * count, :] for r in range(w_ref.shape[0])], axis=0)
            term = dot(parts[half * 3 + part][...], w)
            total = term if total is None else total + term
    back, terms = norm_back(x_ref[...].astype(F32), gain_ref[...], total)
    out_ref[...] = grad_ref[...] + back
    terms = jnp.sum(terms, axis=0, keepdims=True)

    @pl.when(pl.program_id(0) == 0)
    def _():
        gain_out_ref[...] = terms

    @pl.when(pl.program_id(0) > 0)
    def _():
        gain_out_ref[...] += terms


def finish(tokens, grad_resid, gain, parts, weights):
    rows, width = tokens.shape
    block = 256

    def row(cols):
        return pl.BlockSpec((block, cols), lambda i: (i, 0))

    fixed = pl.BlockSpec((1, width), lambda i: (0, 0))
    return pl.pallas_call(
        finish_kernel,
        grid=(rows // block,),
        in_specs=[row(width), row(width), fixed]
        + [row(p.shape[1]) for p in parts]
        + [pl.BlockSpec(w.shape, lambda i: (0, 0, 0)) for w in weights],
        out_specs=[row(width), fixed],
        out_shape=[jax.ShapeDtypeStruct((rows, width), F32), jax.ShapeDtypeStruct((1, width), F32)],
        compiler_params=pltpu.CompilerParams(vmem_limit_bytes=VMEM_LIMIT),
        cost_estimate=pl.CostEstimate(flops=8 * 10**9, bytes_accessed=10**7, transcendentals=0),
        name="finish",
    )(tokens, grad_resid, gain, *parts, *weights)


def rows_at(array, place, count):
    return lax.dynamic_slice_in_dim(array, place * count, count, 0)


def halves_summed(pairs):
    core = lax.axis_index("dp") % 2

    def half(at):
        lanes = pairs[0][1].shape[1] // 2
        terms = [inner_rows(a, lax.dynamic_slice_in_dim(b, at * lanes, lanes, 1)) for a, b in pairs]
        return jnp.concatenate(terms, axis=0) if len(terms) > 1 else terms[0]

    return half(core) + lax.ppermute(half(1 - core), "dp", plane(0, 0, 1))


def whole_of(done):
    got = lax.ppermute(done, "dp", plane(0, 0, 1))
    first = lax.axis_index("dp") % 2 == 0
    return jnp.concatenate([jnp.where(first, done, got), jnp.where(first, got, done)], axis=1)


def ring_place(axis):
    at = lax.axis_index("dp")
    return at // 8 if axis == "y" else (at // 2) % 4


def ring_move(axis, d):
    return plane(d, 0) if axis == "y" else plane(0, d)


def split_ring(half, axis):
    quarter = half.shape[0] // 4
    place = ring_place(axis)
    return [rows_at(half, (place + d) % 4, quarter) for d in range(4)]


def sum_ring(blocks, axis):
    total = blocks[0]
    for d in (1, 2, 3):
        total = total + lax.ppermute(blocks[d], "dp", ring_move(axis, d))
    return total


def in_order(blocks, axis):
    place = ring_place(axis)
    return jnp.concatenate([lax.select_n(lax.rem(place - j + 4, 4), *blocks) for j in range(4)], axis=0)


def far_by_half(blocks, axis):
    half = blocks[2].shape[0] // 16 * 8
    head = lax.ppermute(blocks[2][:half], "dp", ring_move(axis, 1))
    tail = lax.ppermute(blocks[2][half:], "dp", ring_move(axis, -1))
    after = jnp.concatenate([blocks[1][:half] + head, blocks[1][half:]], axis=0)
    before = jnp.concatenate([blocks[3][:half], blocks[3][half:] + tail], axis=0)
    return blocks[0], after, before


def sum_neighbours(parts, axis):
    own, after, before = parts
    return own + lax.ppermute(after, "dp", ring_move(axis, 1)) + lax.ppermute(before, "dp", ring_move(axis, -1))


def spread_ring(block, axis):
    return [block] + [lax.ppermute(block, "dp", ring_move(axis, d)) for d in (1, 2, 3)]


def far_by_half(blocks, axis):
    half = blocks[2].shape[0] // 16 * 8
    head = lax.ppermute(blocks[2][:half], "dp", ring_move(axis, 1))
    tail = lax.ppermute(blocks[2][half:], "dp", ring_move(axis, -1))
    after = jnp.concatenate([blocks[1][:half] + head, blocks[1][half:]], axis=0)
    before = jnp.concatenate([blocks[3][:half], blocks[3][half:] + tail], axis=0)
    return blocks[0], after, before


def sum_neighbours(parts, axis):
    own, after, before = parts
    return own + lax.ppermute(after, "dp", ring_move(axis, 1)) + lax.ppermute(before, "dp", ring_move(axis, -1))


def spread_ring(block, axis):
    return [block] + [lax.ppermute(block, "dp", ring_move(axis, d)) for d in (1, 2, 3)]


def spread_ring_twice(block, axis):
    half = block.shape[0] // 16 * 8
    before = lax.ppermute(block, "dp", ring_move(axis, 1))
    after = lax.ppermute(block, "dp", ring_move(axis, -1))
    head = lax.ppermute(before[:half], "dp", ring_move(axis, 1))
    tail = lax.ppermute(after[half:], "dp", ring_move(axis, -1))
    return [block, before, jnp.concatenate([head, tail], axis=0), after]


def body(
    tokens,
    cotangent,
    seq_len,
    seq_slot,
    attn_gain,
    w_query,
    w_key,
    w_value,
    w_attn_out,
    mlp_gain,
    w_in,
    w_gate,
    w_down,
):
    rows, width = tokens.shape
    heads_cols = w_query.shape[1]
    per_group = 2
    slots = lax.axis_index("dp") * per_group + jnp.arange(per_group, dtype=jnp.int32)
    lengths = jnp.sum(jnp.where(seq_slot[None, :] == slots[:, None], seq_len[None, :], 0), axis=1)
    end0, end1 = lengths[0], lengths[0] + lengths[1]

    def segment_of(index):
        return (index >= end0).astype(jnp.int32) + (index >= end1).astype(jnp.int32)

    index = lax.broadcasted_iota(jnp.int32, (rows, PAIR), 0)
    position = index - jnp.where(index >= end1, end1, jnp.where(index >= end0, end0, 0))
    lane = lax.broadcasted_iota(jnp.int32, (rows, PAIR), 1)
    width_half = HEAD_DIM // 2
    frequency = 10000.0 ** (-(jnp.arange(width_half, dtype=F32) * 2.0 / HEAD_DIM))
    frequency = jnp.tile(frequency, PAIR // width_half)
    phase = position.astype(F32) * frequency[None, :]
    cos = jnp.cos(phase)
    sin = jnp.where(lane % HEAD_DIM < width_half, -1.0, 1.0) * jnp.sin(phase)
    shape = (rows // QB, KB, QB)
    block_at = lax.broadcasted_iota(jnp.int32, shape, 0) * QB
    row_at = block_at + lax.broadcasted_iota(jnp.int32, shape, 2)
    col_at = block_at + lax.broadcasted_iota(jnp.int32, shape, 1) - HALF
    allowed = (
        (segment_of(row_at) == segment_of(col_at))
        & (jnp.abs(row_at - col_at) <= HALF)
        & (col_at >= 0)
        & (col_at < rows)
    )
    bias = jnp.where(allowed, 0.0, -1e30).astype(F32)
    live = (jnp.arange(rows, dtype=jnp.int32) < end1).astype(F32)

    weights_mlp = gather_mlp(w_in, w_gate, w_down, w_attn_out)
    weights0, rest, (cos, sin, cos_t, sin_t, bias) = gather_attn(
        w_query, w_key, w_value, (cos, sin, cos.T, sin.T, bias)
    )
    gain1 = attn_gain[None, :]
    normed1, *qkv0 = project_qkv(tokens, gain1, weights0, cos, sin)
    mix0, prob0 = attend(*qkv0, bias)
    weights1, mix0 = rest(mix0)
    weights_attn = (weights0, weights1)
    qkv1 = project_qkv(normed1, None, weights_attn[1], cos, sin)
    mix1, prob1 = attend(*qkv1, bias)
    (
        mixed_out,
        grad_resid,
        grad_resid_low,
        grad_mix,
        normed2,
        hidden,
        grad_up_gate,
        grad_out_low,
        gain2_sum,
    ) = mlp(weights_mlp, tokens, mix0, mix1, cotangent, live[:, None], mlp_gain[None, :])
    ff_cols = w_in.shape[1]
    spare = jnp.zeros((rows, -(3 * ff_cols + heads_cols) % 128), BF16)
    early = halves_summed(
        [
            (grad_up_gate, normed2),
            (hidden, grad_out_low),
            (jnp.concatenate([mix0[:, :heads_cols], spare], axis=1), grad_resid_low),
        ]
    )
    early = split_ring(early, "y")
    early, grad_mix = lax.optimization_barrier((early, grad_mix))
    split = mix0.shape[1]
    tables = (cos, sin, cos_t, sin_t)
    back0 = attend_back(*qkv0, grad_mix[:, :split], prob0, *tables)
    spare = jnp.zeros((rows, -(3 * heads_cols) % 128), BF16)
    early, back0 = lax.optimization_barrier((far_by_half(early, "y"), back0))
    own_grads = jnp.concatenate([g[:, :heads_cols] for g in back0] + [spare], axis=1)
    late = split_ring(halves_summed([(own_grads, normed1)]), "z")
    early = split_ring(sum_neighbours(early, "y"), "z")
    early, late, next_in = lax.optimization_barrier((early, late, grad_mix[:, split:]))
    back1 = attend_back(*qkv1, next_in, prob1, *tables)
    early, late, back1 = lax.optimization_barrier((sum_ring(early, "z"), far_by_half(late, "z"), back1))
    grad_tokens, gain1_sum = finish(tokens, grad_resid, gain1, [*back0, *back1], weights_attn)
    early = in_order(spread_ring(early, "z"), "z")
    late = split_ring(sum_neighbours(late, "z"), "y")
    lanes = width // 2
    small = jnp.concatenate([gain1_sum[0], gain2_sum[0]])
    small = jnp.pad(small, (0, 8 * lanes - small.shape[0])).reshape(8, lanes)
    early, late, small = lax.optimization_barrier((early, late, small))
    late = sum_ring(late, "y")
    before, after = [lax.ppermute(early, "dp", ring_move("y", d)) for d in (1, -1)]
    late, before, after = lax.optimization_barrier((late, before, after))
    got_late = spread_ring(jnp.concatenate([late, small], axis=0), "y")
    half = early.shape[0] // 16 * 8
    head = lax.ppermute(before[:half], "dp", ring_move("y", 1))
    tail = lax.ppermute(after[half:], "dp", ring_move("y", -1))
    count = late.shape[0]
    small = sum(g[count:] for g in got_late)
    late = in_order([g[:count] for g in got_late], "y")
    early = in_order([early, before, jnp.concatenate([head, tail], axis=0), after], "y")
    early, late, small = lax.optimization_barrier((early, late, small))
    got_late = spread_ring(jnp.concatenate([late, small], axis=0), "z")
    early = whole_of(early)
    count = late.shape[0]
    small = sum(g[count:] for g in got_late)
    late = in_order([g[:count] for g in got_late], "z")
    count = late.shape[0]
    late = whole_of(jnp.concatenate([late, small], axis=0))
    small = (late[count:, :lanes] + late[count:, lanes:]).reshape(-1)
    return (
        mixed_out,
        grad_tokens,
        small[:width],
        late[:heads_cols].T,
        late[heads_cols : 2 * heads_cols].T,
        late[2 * heads_cols : 3 * heads_cols].T,
        early[3 * ff_cols : 3 * ff_cols + heads_cols],
        small[width : 2 * width],
        early[:ff_cols].T,
        early[ff_cols : 2 * ff_cols].T,
        early[2 * ff_cols : 3 * ff_cols],
    )


def solution(mesh):
    rows, cols, all_of = P("dp", None), P(None, "tensor"), P()
    tall = P("tensor", None)
    return jax.shard_map(
        body,
        mesh=mesh,
        in_specs=(rows, rows, all_of, all_of, all_of, cols, cols, cols, tall, all_of, cols, cols, tall),
        out_specs=(rows, rows, all_of, cols, cols, cols, tall, all_of, cols, cols, tall),
        check_vma=False,
    )
```

```python
import jax
import jax.numpy as jnp
from jax import lax
from jax.experimental import pallas as pl
from jax.experimental.pallas import tpu as pltpu
from jax.sharding import PartitionSpec as P

HEAD_DIM = 64
HALF = 64
QB = 128
KB = QB + 2 * HALF
PAIR = 2 * HEAD_DIM
STAGED = 4
STAGED_BACK = 4
F32 = jnp.float32
BF16 = jnp.bfloat16
VMEM_LIMIT = 48 * 1024 * 1024


def dot(a, b):
    return jnp.dot(a, b, preferred_element_type=F32)


def inner_rows(left, right):
    return lax.dot_general(left, right, (((0,), (0,)), ((), ())), preferred_element_type=F32)


def outer_cols(left, right):
    return lax.dot_general(left, right, (((1,), (1,)), ((), ())), preferred_element_type=F32)


def normed(values, gain):
    centre = jnp.mean(values, axis=-1, keepdims=True)
    centred = values - centre
    spread = jnp.mean(centred * centred, axis=-1, keepdims=True)
    return centred * lax.rsqrt(spread + 1e-05) * gain


def norm_back(values, gain, grad):
    centre = jnp.mean(values, axis=-1, keepdims=True)
    centred = values - centre
    spread = jnp.mean(centred * centred, axis=-1, keepdims=True)
    inv = lax.rsqrt(spread + 1e-05)
    unit = centred * inv
    scaled = grad * gain
    first = jnp.mean(scaled, axis=-1, keepdims=True)
    second = jnp.mean(scaled * unit, axis=-1, keepdims=True)
    return inv * (scaled - first - unit * second), grad * unit


def swap_halves(v):
    lane = lax.broadcasted_iota(jnp.int32, v.shape, 1)
    low_half = lax.rem(lane, HEAD_DIM) < HEAD_DIM // 2
    return jnp.where(low_half, pltpu.roll(v, PAIR - HEAD_DIM // 2, 1), pltpu.roll(v, HEAD_DIM // 2, 1))


def rope(v, cos, sin):
    return v * cos + swap_halves(v) * sin


def write_qkv(n, w_ref, cos_ref, sin_ref, q_ref, k_ref, v_ref):
    count = w_ref.shape[1] // 3

    def weight(part):
        return jnp.concatenate([w_ref[r, part * count : (part + 1) * count, :] for r in range(w_ref.shape[0])], axis=0)

    cos, sin = cos_ref[...], sin_ref[...]
    q = outer_cols(n, weight(0))
    k = outer_cols(n, weight(1))
    for j in range(q.shape[1] // PAIR):
        cols = slice(j * PAIR, (j + 1) * PAIR)
        q_ref[:, cols] = (rope(q[:, cols], cos, sin) * (1.0 / HEAD_DIM**0.5)).astype(BF16)
        k_ref[:, cols] = rope(k[:, cols], cos, sin).astype(BF16)
    v_ref[...] = outer_cols(n, weight(2)).astype(BF16)


def norm_qkv_kernel(x_ref, gain_ref, w_ref, cos_ref, sin_ref, n_ref, q_ref, k_ref, v_ref):
    n = normed(x_ref[...].astype(F32), gain_ref[...]).astype(BF16)
    n_ref[...] = n
    write_qkv(n, w_ref, cos_ref, sin_ref, q_ref, k_ref, v_ref)


def only_qkv_kernel(n_ref, w_ref, cos_ref, sin_ref, q_ref, k_ref, v_ref):
    write_qkv(n_ref[...], w_ref, cos_ref, sin_ref, q_ref, k_ref, v_ref)


def project_qkv(rows_in, gain, pack, cos, sin):
    rows, width = rows_in.shape
    cols = pack.shape[0] * pack.shape[1] // 3
    block = 256
    row_spec = pl.BlockSpec((block, width), lambda i: (i, 0))
    out_spec = pl.BlockSpec((block, cols), lambda i: (i, 0))
    gain_spec = pl.BlockSpec((1, width), lambda i: (0, 0))
    w_spec = pl.BlockSpec(pack.shape, lambda i: (0, 0, 0))
    tab_spec = pl.BlockSpec((block, PAIR), lambda i: (i, 0))
    first = gain is not None
    return pl.pallas_call(
        norm_qkv_kernel if first else only_qkv_kernel,
        grid=(rows // block,),
        in_specs=[row_spec] + [gain_spec] * first + [w_spec, tab_spec, tab_spec],
        out_specs=[row_spec] * first + [out_spec] * 3,
        out_shape=[jax.ShapeDtypeStruct((rows, width), BF16)] * first + [jax.ShapeDtypeStruct((rows, cols), BF16)] * 3,
        compiler_params=pltpu.CompilerParams(vmem_limit_bytes=VMEM_LIMIT),
        cost_estimate=pl.CostEstimate(
            flops=8 * rows * width * cols, bytes_accessed=8 * rows * width + 6 * width * cols, transcendentals=0
        ),
        name="norm_qkv" if first else "qkv",
    )(*([rows_in] + [gain] * first + [pack, cos, sin]))


def pad_rows(dst, src):
    rows = src.shape[0]
    edge = jnp.zeros((HALF, PAIR), dst.dtype)
    dst[0:HALF, :] = edge
    dst[HALF : HALF + rows, :] = src
    dst[HALF + rows : rows + 2 * HALF, :] = edge


def split_lanes(src, first, second):
    lane = lax.broadcasted_iota(jnp.int32, src.shape, 1)
    zero = jnp.zeros_like(src)
    first[...] = jnp.where(lane < HEAD_DIM, src, zero)
    second[...] = jnp.where(lane < HEAD_DIM, zero, src)


def query_rows(i):
    return slice(i * QB, (i + 1) * QB)


def key_rows(i):
    return slice(i * QB, i * QB + KB)


def head_rows(h):
    return slice(h * HEAD_DIM, (h + 1) * HEAD_DIM)


def attend_kernel(q_ref, k_ref, v_ref, bias_ref, o_ref, p_ref, pad, k0, k1, vt):
    rows = q_ref.shape[0]
    pad_rows(pad, v_ref[...])
    vt[...] = pad[...].T
    pad_rows(pad, k_ref[...])
    split_lanes(pad[...], k0, k1)
    for start in range(0, rows // QB, STAGED):
        blocks = range(start, start + STAGED)
        units = [(i, h) for i in blocks for h in range(2)]
        q_t = {i: q_ref[query_rows(i), :].T for i in blocks}
        scores = [dot((k0, k1)[h][key_rows(i), :], q_t[i]) + bias_ref[i] for i, h in units]
        tops = [jnp.max(s, axis=0, keepdims=True) for s in scores]
        expos = [jnp.exp(s - top) for s, top in zip(scores, tops)]
        shares = [1.0 / jnp.sum(e, axis=0, keepdims=True) for e in expos]
        probs = [(e * share).astype(BF16) for e, share in zip(expos, shares)]
        outs = [dot(vt[head_rows(h), key_rows(i)], p) for (i, h), p in zip(units, probs)]
        for (i, h), p in zip(units, probs):
            p_ref[0, i, :, h * QB : (h + 1) * QB] = p
        for n, i in enumerate(blocks):
            o_ref[query_rows(i), :] = jnp.concatenate(outs[2 * n : 2 * n + 2], axis=0).astype(BF16).T


def attend(q, k, v, bias):
    rows, width = q.shape
    pairs, blocks = width // PAIR, rows // QB
    spec = pl.BlockSpec((rows, PAIR), lambda j: (0, j))
    padded = rows + 2 * HALF
    return pl.pallas_call(
        attend_kernel,
        grid=(pairs,),
        in_specs=[spec, spec, spec, pl.BlockSpec((blocks, KB, QB), lambda j: (0, 0, 0))],
        out_specs=[spec, pl.BlockSpec((1, blocks, KB, 2 * QB), lambda j: (j, 0, 0, 0))],
        out_shape=[
            jax.ShapeDtypeStruct((rows, width), BF16),
            jax.ShapeDtypeStruct((pairs, blocks, KB, 2 * QB), BF16),
        ],
        scratch_shapes=[pltpu.VMEM((padded, PAIR), BF16)] * 3 + [pltpu.VMEM((PAIR, padded), BF16)],
        compiler_params=pltpu.CompilerParams(vmem_limit_bytes=VMEM_LIMIT),
        cost_estimate=pl.CostEstimate(flops=2 * 10**9 * pairs, bytes_accessed=2 * rows * width * 8, transcendentals=0),
        name="attend",
    )(q, k, v, bias)


def swap_rows(v):
    quarter = HEAD_DIM // 2
    part = [v[i * quarter : (i + 1) * quarter, :] for i in range(4)]
    return jnp.concatenate([part[1], part[0], part[3], part[2]], axis=0)


def both_heads(v):
    lane = lax.broadcasted_iota(jnp.int32, v.shape, 1)
    zero = jnp.zeros_like(v)
    return jnp.concatenate([jnp.where(lane < HEAD_DIM, v, zero), jnp.where(lane < HEAD_DIM, zero, v)], axis=0)


def attend_back_kernel(
    q_ref, k_ref, v_ref, g_ref, p_ref, cos_ref, sin_ref, cos_t, sin_t, gq_ref, gk_ref, gv_ref, pad, v0, v1, kt, gk, gv
):
    rows = q_ref.shape[0]
    scale = 1.0 / HEAD_DIM**0.5
    pad_rows(pad, k_ref[...])
    kt[...] = pad[...].T
    pad_rows(pad, v_ref[...])
    split_lanes(pad[...], v0, v1)
    gk[...] = jnp.zeros_like(gk)
    gv[...] = jnp.zeros_like(gv)
    for start in range(0, rows // QB, STAGED_BACK):
        blocks = range(start, start + STAGED_BACK)
        units = [(i, h) for i in blocks for h in range(2)]
        g_t = {i: g_ref[query_rows(i), :].T for i in blocks}
        gps = [dot((v0, v1)[h][key_rows(i), :], g_t[i]) for i, h in units]
        probs = [p_ref[0, i, :, h * QB : (h + 1) * QB].astype(F32) for i, h in units]
        sums = [jnp.sum(p * gp, axis=0, keepdims=True) for p, gp in zip(probs, gps)]
        grads = [(p * (gp - total)).astype(BF16) for p, gp, total in zip(probs, gps, sums)]
        outs = [dot(kt[head_rows(h), key_rows(i)], gs) for (i, h), gs in zip(units, grads)]
        gks = [
            dot(jnp.concatenate(grads[2 * n : 2 * n + 2], axis=1), both_heads(q_ref[query_rows(i), :]))
            for n, i in enumerate(blocks)
        ]
        gvs = [dot(p_ref[0, i], both_heads(g_ref[query_rows(i), :])) for i in blocks]
        for n, i in enumerate(blocks):
            at = query_rows(i)
            gk[key_rows(i), :] += gks[n]
            gv[key_rows(i), :] += gvs[n]
            gq = jnp.concatenate(outs[2 * n : 2 * n + 2], axis=0) * scale
            gq_ref[at, :] = (gq * cos_t[:, at] - swap_rows(gq) * sin_t[:, at]).astype(BF16).T
    gk_ref[...] = rope(gk[HALF : HALF + rows, :], cos_ref[...], -sin_ref[...]).astype(BF16)
    gv_ref[...] = gv[HALF : HALF + rows, :].astype(BF16)


def attend_back(q, k, v, g, prob, cos, sin, cos_t, sin_t):
    rows, width = q.shape
    pairs, blocks = width // PAIR, rows // QB
    spec = pl.BlockSpec((rows, PAIR), lambda j: (0, j))
    tab_spec = pl.BlockSpec((rows, PAIR), lambda j: (0, 0))
    tab_t_spec = pl.BlockSpec((PAIR, rows), lambda j: (0, 0))
    padded = rows + 2 * HALF
    return pl.pallas_call(
        attend_back_kernel,
        grid=(pairs,),
        in_specs=[spec] * 4
        + [pl.BlockSpec((1, blocks, KB, 2 * QB), lambda j: (j, 0, 0, 0)), tab_spec, tab_spec, tab_t_spec, tab_t_spec],
        out_specs=[spec] * 3,
        out_shape=[jax.ShapeDtypeStruct((rows, width), BF16)] * 3,
        scratch_shapes=[pltpu.VMEM((padded, PAIR), BF16)] * 3
        + [pltpu.VMEM((PAIR, padded), BF16)]
        + [pltpu.VMEM((padded, PAIR), F32)] * 2,
        compiler_params=pltpu.CompilerParams(vmem_limit_bytes=VMEM_LIMIT),
        cost_estimate=pl.CostEstimate(flops=8 * 10**9, bytes_accessed=10**7, transcendentals=0),
        name="attend_back",
    )(q, k, v, g, prob, cos, sin, cos_t, sin_t)


def ring(step):
    size = lax.axis_size("tensor")
    return [(i, (i + step) % size) for i in range(size)]


def plane(dy, dz, dc=0):
    size = lax.axis_size("dp")
    out = []
    for i in range(size):
        y, z, c = i // 8, (i // 2) % 4, i % 2
        out.append((i, (((y + dy) % 4) * 4 + (z + dz) % 4) * 2 + (c + dc) % 2))
    return out


def place_pair_kernel(core_ref, own_ref, mine_ref, other_ref, out_ref):
    half = mine_ref.shape[1]
    out_ref[0] = own_ref[...]
    core = core_ref[0]
    out_ref[1, :, pl.ds(pl.multiple_of(core * half, half), half)] = mine_ref[...].astype(BF16)
    out_ref[1, :, pl.ds(pl.multiple_of((1 - core) * half, half), half)] = other_ref[...].astype(BF16)


def place_rest_kernel(core_ref, mine_ref, other_ref, head_ref, tail_ref, other_head_ref, other_tail_ref, out_ref):
    rows, half = mine_ref.shape
    core = core_ref[0]
    mine_at = pl.ds(pl.multiple_of(core * half, half), half)
    other_at = pl.ds(pl.multiple_of((1 - core) * half, half), half)
    out_ref[0, :, mine_at] = mine_ref[...].astype(BF16)
    out_ref[0, :, other_at] = other_ref[...].astype(BF16)
    out_ref[1, 0 : rows // 2, mine_at] = head_ref[...].astype(BF16)
    out_ref[1, rows // 2 : rows, mine_at] = tail_ref[...].astype(BF16)
    out_ref[1, 0 : rows // 2, other_at] = other_head_ref[...].astype(BF16)
    out_ref[1, rows // 2 : rows, other_at] = other_tail_ref[...].astype(BF16)


def place(kernel, core, rows, lanes, args, name):
    whole = pl.BlockSpec(memory_space=pltpu.VMEM)
    return pl.pallas_call(
        kernel,
        in_specs=[pl.BlockSpec(memory_space=pltpu.SMEM)] + [whole] * len(args),
        out_specs=whole,
        out_shape=jax.ShapeDtypeStruct((2, rows, lanes), BF16),
        compiler_params=pltpu.CompilerParams(vmem_limit_bytes=VMEM_LIMIT),
        name=name,
    )(core[None].astype(jnp.int32), *args)


def gather_attn(w_query, w_key, w_value, meanwhile):
    core = lax.axis_index("dp") % 2
    own = jnp.concatenate([w_query.T, w_key.T, w_value.T], axis=0)
    rows, lanes = own.shape
    half = lanes // 2
    mine = lax.dynamic_slice_in_dim(own, core * half, half, 1).astype(F32)
    swap = plane(0, 0, 1)
    after = lax.ppermute(mine, "tensor", ring(-1))
    before = lax.ppermute(mine, "tensor", ring(1))
    after, before, meanwhile = lax.optimization_barrier((after, before, meanwhile))
    head = lax.ppermute(after[: rows // 2], "tensor", ring(-1))
    tail = lax.ppermute(before[rows // 2 :], "tensor", ring(1))
    other_after = lax.ppermute(after, "dp", swap)
    other_before = lax.ppermute(before, "dp", swap)
    first = place(place_pair_kernel, core, rows, lanes, (own, after, other_after), "place_pair")

    def rest(behind):
        late_head, late_tail, behind = lax.optimization_barrier((head, tail, behind))
        other_head = lax.ppermute(late_head, "dp", swap)
        other_tail = lax.ppermute(late_tail, "dp", swap)
        args = (before, other_before, late_head, late_tail, other_head, other_tail)
        return place(place_rest_kernel, core, rows, lanes, args, "place_rest"), behind

    return first, rest, meanwhile


def both_ways(block, axis, move):
    return lax.ppermute(block, axis, move(1)), lax.ppermute(block, axis, move(-1))


def far_of(back, on, axis, move):
    half = back.shape[0] // 16 * 8
    parts = [lax.ppermute(on[:half], axis, move(-1)), lax.ppermute(back[half:], axis, move(1))]
    return jnp.concatenate(parts, axis=0)


def mlp_piece(w_in, w_gate, w_down, w_attn_out):
    core, z, y = lax.axis_index("dp") % 2, ring_place("z"), ring_place("y")
    half = w_down.shape[1] // 2
    count, short = w_down.shape[0] // 4, w_attn_out.shape[0] // 4
    parts = [
        lax.dynamic_slice(w_in.T, (z * count, core * half), (count, half)),
        lax.dynamic_slice(w_gate.T, (z * count, core * half), (count, half)),
        lax.dynamic_slice(w_down, (y * count, core * half), (count, half)),
        lax.dynamic_slice(w_attn_out, (y * short, core * half), (short, half)),
    ]
    return jnp.concatenate(parts, axis=0).astype(F32)


def mlp_kernel(
    at_ref,
    z_mine,
    z_other,
    y_mine,
    y_other,
    own_in,
    own_gate,
    own_down,
    own_out,
    x_ref,
    mix0_ref,
    mix1_ref,
    cot_ref,
    live_ref,
    gain_ref,
    out_ref,
    resid_ref,
    low_ref,
    mixg_ref,
    n_ref,
    hid_ref,
    gug_ref,
    go_ref,
    gain_out_ref,
    up_w,
    gt_w,
    dn_w,
    o_w,
):
    step = pl.program_id(0)
    core, z, y = at_ref[0], at_ref[1], at_ref[2]
    half = z_mine.shape[3]
    loads = 3
    count, short = own_in.shape[0] // 4, own_out.shape[0] // 4

    @pl.when(step == 0)
    def _():
        for dst, own in ((up_w, own_in), (gt_w, own_gate), (dn_w, own_down), (o_w, own_out)):
            dst[0 : own.shape[0], :] = own[...]

    for slot in range(loads):

        @pl.when(step == slot)
        def _(slot=slot):
            for src, lanes, place, dst, first, rows in (
                (z_mine, core, z, up_w, 0, count),
                (z_other, 1 - core, z, up_w, 0, count),
                (z_mine, core, z, gt_w, count, count),
                (z_other, 1 - core, z, gt_w, count, count),
                (y_mine, core, y, dn_w, 0, count),
                (y_other, 1 - core, y, dn_w, 0, count),
                (y_mine, core, y, o_w, count, short),
                (y_other, 1 - core, y, o_w, count, short),
            ):
                quarters = [src[lax.rem(place - j + 4, 4), 0, first : first + rows, :] for j in range(4)]
                block = jnp.concatenate(quarters, axis=0).astype(BF16)
                start = (slot + 1) * 4 * rows
                dst[start : start + 4 * rows, pl.ds(pl.multiple_of(lanes * half, half), half)] = block

    @pl.when(step >= loads)
    def _():
        split = mix0_ref.shape[1]
        gain = gain_ref[...]
        resid = x_ref[...].astype(F32) + dot(mix0_ref[...], o_w[0:split, :]) + dot(mix1_ref[...], o_w[split:, :])
        centre = jnp.mean(resid, axis=-1, keepdims=True)
        centred = resid - centre
        inv = lax.rsqrt(jnp.mean(centred * centred, axis=-1, keepdims=True) + 1e-05)
        unit = centred * inv
        n = (unit * gain).astype(BF16)
        n_ref[...] = n
        up = outer_cols(n, up_w[...])
        gate = outer_cols(n, gt_w[...])
        go = cot_ref[...].astype(F32) * live_ref[...]
        go_low = go.astype(BF16)
        go_ref[...] = go_low
        gh = outer_cols(go_low, dn_w[...])
        bell = jnp.exp(up * up * -0.5)
        t = 1.0 / (1.0 + (0.3275911 * 0.7071067811865476) * jnp.abs(up))
        poly = t * (
            0.5 * 0.254829592
            + t * (0.5 * -0.284496736 + t * (0.5 * 1.421413741 + t * (0.5 * -1.453152027 + t * (0.5 * 1.061405429))))
        )
        tail = poly * bell
        cdf = jnp.where(up >= 0.0, 1.0 - tail, tail)
        act = up * cdf
        slope = cdf + up * bell * 0.3989422804014327
        hid = (act * gate).astype(BF16)
        gup = (gh * gate * slope).astype(BF16)
        ggt = (gh * act).astype(BF16)
        own = hid_ref.shape[1]
        hid_ref[...] = hid[:, :own]
        gug_ref[...] = jnp.concatenate([gup[:, :own], ggt[:, :own]], axis=1)
        out_ref[...] = (resid + dot(hid, dn_w[...])).astype(BF16)
        gn = dot(gup, up_w[...]) + dot(ggt, gt_w[...])
        scaled = gn * gain
        first = jnp.mean(scaled, axis=-1, keepdims=True)
        second = jnp.mean(scaled * unit, axis=-1, keepdims=True)
        grad = go + inv * (scaled - first - unit * second)
        resid_ref[...] = grad
        low = grad.astype(BF16)
        low_ref[...] = low
        mixg_ref[...] = outer_cols(low, o_w[...]).astype(BF16)
        terms = jnp.sum(gn * unit, axis=0, keepdims=True)

        @pl.when(step == loads)
        def _():
            gain_out_ref[...] = terms

        @pl.when(step > loads)
        def _():
            gain_out_ref[...] += terms


def mlp(gathered, own, tokens, mix0, mix1, cotangent, live, gain):
    rows, width = tokens.shape
    block, loads = 256, 3
    ff_own = own[0].shape[0]
    ff = 4 * ff_own
    place = jnp.stack([lax.axis_index("dp") % 2, ring_place("z"), ring_place("y")]).astype(jnp.int32)

    def at_row(i, _):
        return (jnp.maximum(i - loads, 0), 0)

    def from_ranks(array):
        return pl.BlockSpec((4, 1) + array.shape[2:], lambda i, _: (0, jnp.minimum(i, loads - 1), 0, 0))

    def whole(array):
        return pl.BlockSpec(array.shape, lambda i, _: (0, 0))

    def row(cols):
        return pl.BlockSpec((block, cols), at_row)

    def fixed(i, _):
        return (0, 0)

    def shape(cols, kind):
        return jax.ShapeDtypeStruct((rows, cols), kind)

    split = mix0.shape[1]
    return pl.pallas_call(
        mlp_kernel,
        grid_spec=pltpu.PrefetchScalarGridSpec(
            num_scalar_prefetch=1,
            grid=(loads + rows // block,),
            in_specs=[
                *[from_ranks(array) for array in gathered],
                *[whole(array) for array in own],
                row(width),
                row(split),
                row(width - split),
                row(width),
                row(1),
                pl.BlockSpec((1, width), fixed),
            ],
            out_specs=[
                row(width),
                row(width),
                row(width),
                row(width),
                row(width),
                row(ff_own),
                row(2 * ff_own),
                row(width),
                pl.BlockSpec((1, width), fixed),
            ],
            scratch_shapes=[
                pltpu.VMEM((ff, width), BF16),
                pltpu.VMEM((ff, width), BF16),
                pltpu.VMEM((ff, width), BF16),
                pltpu.VMEM((width, width), BF16),
            ],
        ),
        out_shape=[
            shape(width, BF16),
            shape(width, F32),
            shape(width, BF16),
            shape(width, BF16),
            shape(width, BF16),
            shape(ff_own, BF16),
            shape(2 * ff_own, BF16),
            shape(width, BF16),
            jax.ShapeDtypeStruct((1, width), F32),
        ],
        compiler_params=pltpu.CompilerParams(vmem_limit_bytes=VMEM_LIMIT),
        cost_estimate=pl.CostEstimate(flops=12 * rows * width * ff, bytes_accessed=40 * 10**6, transcendentals=0),
        name="mlp",
    )(place, *gathered, *own, tokens, mix0, mix1, cotangent, live, gain)


def finish_kernel(x_ref, grad_ref, gain_ref, *refs):
    parts, weights, (out_ref, gain_out_ref) = refs[:6], refs[6:8], refs[8:]
    total = None
    for half in range(2):
        w_ref = weights[half]
        count = w_ref.shape[1] // 3
        for part in range(3):
            w = jnp.concatenate([w_ref[r, part * count : (part + 1) * count, :] for r in range(w_ref.shape[0])], axis=0)
            term = dot(parts[half * 3 + part][...], w)
            total = term if total is None else total + term
    back, terms = norm_back(x_ref[...].astype(F32), gain_ref[...], total)
    out_ref[...] = grad_ref[...] + back
    terms = jnp.sum(terms, axis=0, keepdims=True)

    @pl.when(pl.program_id(0) == 0)
    def _():
        gain_out_ref[...] = terms

    @pl.when(pl.program_id(0) > 0)
    def _():
        gain_out_ref[...] += terms


def finish(tokens, grad_resid, gain, parts, weights):
    rows, width = tokens.shape
    block = 256

    def row(cols):
        return pl.BlockSpec((block, cols), lambda i: (i, 0))

    fixed = pl.BlockSpec((1, width), lambda i: (0, 0))
    return pl.pallas_call(
        finish_kernel,
        grid=(rows // block,),
        in_specs=[row(width), row(width), fixed]
        + [row(p.shape[1]) for p in parts]
        + [pl.BlockSpec(w.shape, lambda i: (0, 0, 0)) for w in weights],
        out_specs=[row(width), fixed],
        out_shape=[jax.ShapeDtypeStruct((rows, width), F32), jax.ShapeDtypeStruct((1, width), F32)],
        compiler_params=pltpu.CompilerParams(vmem_limit_bytes=VMEM_LIMIT),
        cost_estimate=pl.CostEstimate(flops=8 * 10**9, bytes_accessed=10**7, transcendentals=0),
        name="finish",
    )(tokens, grad_resid, gain, *parts, *weights)


def rows_at(array, place, count):
    return lax.dynamic_slice_in_dim(array, place * count, count, 0)


def halves_summed(pairs):
    core = lax.axis_index("dp") % 2

    def half(at):
        lanes = pairs[0][1].shape[1] // 2
        terms = [inner_rows(a, lax.dynamic_slice_in_dim(b, at * lanes, lanes, 1)) for a, b in pairs]
        return jnp.concatenate(terms, axis=0) if len(terms) > 1 else terms[0]

    return half(core) + lax.ppermute(half(1 - core), "dp", plane(0, 0, 1))


def whole_of(done):
    got = lax.ppermute(done, "dp", plane(0, 0, 1))
    first = lax.axis_index("dp") % 2 == 0
    return jnp.concatenate([jnp.where(first, done, got), jnp.where(first, got, done)], axis=1)


def ring_place(axis):
    at = lax.axis_index("dp")
    return at // 8 if axis == "y" else (at // 2) % 4


def ring_move(axis, d):
    return plane(d, 0) if axis == "y" else plane(0, d)


def split_ring(half, axis):
    quarter = half.shape[0] // 4
    place = ring_place(axis)
    return [rows_at(half, (place + d) % 4, quarter) for d in range(4)]


def sum_ring(blocks, axis):
    total = blocks[0]
    for d in (1, 2, 3):
        total = total + lax.ppermute(blocks[d], "dp", ring_move(axis, d))
    return total


def in_order(blocks, axis):
    place = ring_place(axis)
    return jnp.concatenate([lax.select_n(lax.rem(place - j + 4, 4), *blocks) for j in range(4)], axis=0)


def far_by_half(blocks, axis):
    half = blocks[2].shape[0] // 16 * 8
    head = lax.ppermute(blocks[2][:half], "dp", ring_move(axis, 1))
    tail = lax.ppermute(blocks[2][half:], "dp", ring_move(axis, -1))
    after = jnp.concatenate([blocks[1][:half] + head, blocks[1][half:]], axis=0)
    before = jnp.concatenate([blocks[3][:half], blocks[3][half:] + tail], axis=0)
    return blocks[0], after, before


def sum_neighbours(parts, axis):
    own, after, before = parts
    return own + lax.ppermute(after, "dp", ring_move(axis, 1)) + lax.ppermute(before, "dp", ring_move(axis, -1))


def spread_ring(block, axis):
    return [block] + [lax.ppermute(block, "dp", ring_move(axis, d)) for d in (1, 2, 3)]


def spread_ring_twice(block, axis):
    half = block.shape[0] // 16 * 8
    before = lax.ppermute(block, "dp", ring_move(axis, 1))
    after = lax.ppermute(block, "dp", ring_move(axis, -1))
    head = lax.ppermute(before[:half], "dp", ring_move(axis, 1))
    tail = lax.ppermute(after[half:], "dp", ring_move(axis, -1))
    return [block, before, jnp.concatenate([head, tail], axis=0), after]


def body(
    tokens,
    cotangent,
    seq_len,
    seq_slot,
    attn_gain,
    w_query,
    w_key,
    w_value,
    w_attn_out,
    mlp_gain,
    w_in,
    w_gate,
    w_down,
):
    rows, width = tokens.shape
    heads_cols = w_query.shape[1]
    per_group = 2
    slots = lax.axis_index("dp") * per_group + jnp.arange(per_group, dtype=jnp.int32)
    lengths = jnp.sum(jnp.where(seq_slot[None, :] == slots[:, None], seq_len[None, :], 0), axis=1)
    end0, end1 = lengths[0], lengths[0] + lengths[1]

    def segment_of(index):
        return (index >= end0).astype(jnp.int32) + (index >= end1).astype(jnp.int32)

    index = lax.broadcasted_iota(jnp.int32, (rows, PAIR), 0)
    position = index - jnp.where(index >= end1, end1, jnp.where(index >= end0, end0, 0))
    lane = lax.broadcasted_iota(jnp.int32, (rows, PAIR), 1)
    width_half = HEAD_DIM // 2
    frequency = 10000.0 ** (-(jnp.arange(width_half, dtype=F32) * 2.0 / HEAD_DIM))
    frequency = jnp.tile(frequency, PAIR // width_half)
    phase = position.astype(F32) * frequency[None, :]
    cos = jnp.cos(phase)
    sin = jnp.where(lane % HEAD_DIM < width_half, -1.0, 1.0) * jnp.sin(phase)
    shape = (rows // QB, KB, QB)
    block_at = lax.broadcasted_iota(jnp.int32, shape, 0) * QB
    row_at = block_at + lax.broadcasted_iota(jnp.int32, shape, 2)
    col_at = block_at + lax.broadcasted_iota(jnp.int32, shape, 1) - HALF
    allowed = (
        (segment_of(row_at) == segment_of(col_at))
        & (jnp.abs(row_at - col_at) <= HALF)
        & (col_at >= 0)
        & (col_at < rows)
    )
    bias = jnp.where(allowed, 0.0, -1e30).astype(F32)
    live = (jnp.arange(rows, dtype=jnp.int32) < end1).astype(F32)

    def along_z(d):
        return plane(0, d)

    def along_y(d):
        return plane(d, 0)

    piece = mlp_piece(w_in, w_gate, w_down, w_attn_out)
    piece_back, piece_on = both_ways(piece, "tensor", ring)
    piece_far = far_of(piece_back, piece_on, "tensor", ring)
    cut = 2 * (w_in.shape[1] // 4)
    by_z = jnp.concatenate([piece_on[:cut], piece_back[:cut], piece_far[:cut]], axis=0)
    by_y = jnp.concatenate([piece_on[cut:], piece_back[cut:], piece_far[cut:]], axis=0)
    weights0, rest, (cos, sin, cos_t, sin_t, bias, by_z, by_y) = gather_attn(
        w_query, w_key, w_value, (cos, sin, cos.T, sin.T, bias, by_z, by_y)
    )
    z_back, z_on = both_ways(by_z, "dp", along_z)
    y_back, y_on = both_ways(by_y, "dp", along_y)
    gain1 = attn_gain[None, :]
    normed1, *qkv0 = project_qkv(tokens, gain1, weights0, cos, sin)
    mix0, prob0 = attend(*qkv0, bias)
    z_back, z_on, y_back, y_on, mix0 = lax.optimization_barrier((z_back, z_on, y_back, y_on, mix0))
    weights1, mix0 = rest(mix0)
    z_far = far_of(z_back, z_on, "dp", along_z)
    y_far = far_of(y_back, y_on, "dp", along_y)
    weights_attn = (weights0, weights1)
    qkv1 = project_qkv(normed1, None, weights_attn[1], cos, sin)
    z_far, y_far, qkv1 = lax.optimization_barrier((z_far, y_far, qkv1))
    z_mine = jnp.concatenate([by_z, z_back, z_far, z_on], axis=0)
    y_mine = jnp.concatenate([by_y, y_back, y_far, y_on], axis=0)
    z_mine, y_mine, qkv1 = lax.optimization_barrier((z_mine, y_mine, qkv1))
    z_other = lax.ppermute(z_mine, "dp", plane(0, 0, 1))
    y_other = lax.ppermute(y_mine, "dp", plane(0, 0, 1))
    mix1, prob1 = attend(*qkv1, bias)
    gathered = [a.reshape(4, 3, -1, a.shape[1]) for a in (z_mine, z_other, y_mine, y_other)]
    own_mlp = [w_in.T, w_gate.T, w_down, w_attn_out]
    (
        mixed_out,
        grad_resid,
        grad_resid_low,
        grad_mix,
        normed2,
        hidden,
        grad_up_gate,
        grad_out_low,
        gain2_sum,
    ) = mlp(gathered, own_mlp, tokens, mix0, mix1, cotangent, live[:, None], mlp_gain[None, :])
    ff_cols = w_in.shape[1]
    spare = jnp.zeros((rows, -(3 * ff_cols + heads_cols) % 128), BF16)
    early = halves_summed(
        [
            (grad_up_gate, normed2),
            (hidden, grad_out_low),
            (jnp.concatenate([mix0[:, :heads_cols], spare], axis=1), grad_resid_low),
        ]
    )
    early = split_ring(early, "y")
    early, grad_mix = lax.optimization_barrier((early, grad_mix))
    split = mix0.shape[1]
    tables = (cos, sin, cos_t, sin_t)
    back0 = attend_back(*qkv0, grad_mix[:, :split], prob0, *tables)
    spare = jnp.zeros((rows, -(3 * heads_cols) % 128), BF16)
    early, back0 = lax.optimization_barrier((far_by_half(early, "y"), back0))
    own_grads = jnp.concatenate([g[:, :heads_cols] for g in back0] + [spare], axis=1)
    late = split_ring(halves_summed([(own_grads, normed1)]), "z")
    early, late, next_in = lax.optimization_barrier((early, late, grad_mix[:, split:]))
    back1 = attend_back(*qkv1, next_in, prob1, *tables)
    late, back1 = lax.optimization_barrier((far_by_half(late, "z"), back1))
    grad_tokens, gain1_sum = finish(tokens, grad_resid, gain1, [*back0, *back1], weights_attn)
    early = split_ring(sum_neighbours(early, "y"), "z")
    late = split_ring(sum_neighbours(late, "z"), "y")
    early, late = lax.optimization_barrier((early, late))
    early, late = lax.optimization_barrier((sum_ring(early, "z"), sum_ring(late, "y")))
    lanes = width // 2
    small = jnp.concatenate([gain1_sum[0], gain2_sum[0]])
    small = jnp.pad(small, (0, 8 * lanes - small.shape[0])).reshape(8, lanes)
    got_early = spread_ring(early, "z")
    got_late = spread_ring(jnp.concatenate([late, small], axis=0), "y")
    count = late.shape[0]
    small = sum(g[count:] for g in got_late)
    early = in_order(got_early, "z")
    late = in_order([g[:count] for g in got_late], "y")
    early, late, small = lax.optimization_barrier((early, late, small))
    got_late = spread_ring(jnp.concatenate([late, small], axis=0), "z")
    got_early = spread_ring_twice(early, "y")
    count = late.shape[0]
    small = sum(g[count:] for g in got_late)
    late = in_order([g[:count] for g in got_late], "z")
    early = in_order(got_early, "y")
    count = late.shape[0]
    late = whole_of(jnp.concatenate([late, small], axis=0))
    small = (late[count:, :lanes] + late[count:, lanes:]).reshape(-1)
    early = whole_of(early)
    return (
        mixed_out,
        grad_tokens,
        small[:width],
        late[:heads_cols].T,
        late[heads_cols : 2 * heads_cols].T,
        late[2 * heads_cols : 3 * heads_cols].T,
        early[3 * ff_cols : 3 * ff_cols + heads_cols],
        small[width : 2 * width],
        early[:ff_cols].T,
        early[ff_cols : 2 * ff_cols].T,
        early[2 * ff_cols : 3 * ff_cols],
    )


def solution(mesh):
    rows, cols, all_of = P("dp", None), P(None, "tensor"), P()
    tall = P("tensor", None)
    return jax.shard_map(
        body,
        mesh=mesh,
        in_specs=(rows, rows, all_of, all_of, all_of, cols, cols, cols, tall, all_of, cols, cols, tall),
        out_specs=(rows, rows, all_of, cols, cols, cols, tall, all_of, cols, cols, tall),
        check_vma=False,
    )
```

```python
import jax
import jax.numpy as jnp
from jax import lax
from jax.experimental import pallas as pl
from jax.experimental.pallas import tpu as pltpu
from jax.sharding import PartitionSpec as P

HEAD_DIM = 64
HALF = 64
QB = 128
KB = QB + 2 * HALF
PAIR = 2 * HEAD_DIM
STAGED = 4
STAGED_BACK = 4
F32 = jnp.float32
BF16 = jnp.bfloat16
VMEM_LIMIT = 48 * 1024 * 1024


def dot(a, b):
    return jnp.dot(a, b, preferred_element_type=F32)


def inner_rows(left, right):
    return lax.dot_general(left, right, (((0,), (0,)), ((), ())), preferred_element_type=F32)


def outer_cols(left, right):
    return lax.dot_general(left, right, (((1,), (1,)), ((), ())), preferred_element_type=F32)


def normed(values, gain):
    centre = jnp.mean(values, axis=-1, keepdims=True)
    centred = values - centre
    spread = jnp.mean(centred * centred, axis=-1, keepdims=True)
    return centred * lax.rsqrt(spread + 1e-05) * gain


def norm_back(values, gain, grad):
    centre = jnp.mean(values, axis=-1, keepdims=True)
    centred = values - centre
    spread = jnp.mean(centred * centred, axis=-1, keepdims=True)
    inv = lax.rsqrt(spread + 1e-05)
    unit = centred * inv
    scaled = grad * gain
    first = jnp.mean(scaled, axis=-1, keepdims=True)
    second = jnp.mean(scaled * unit, axis=-1, keepdims=True)
    return inv * (scaled - first - unit * second), grad * unit


def swap_halves(v):
    lane = lax.broadcasted_iota(jnp.int32, v.shape, 1)
    low_half = lax.rem(lane, HEAD_DIM) < HEAD_DIM // 2
    return jnp.where(low_half, pltpu.roll(v, PAIR - HEAD_DIM // 2, 1), pltpu.roll(v, HEAD_DIM // 2, 1))


def rope(v, cos, sin):
    return v * cos + swap_halves(v) * sin


def write_qkv(n, w_ref, cos_ref, sin_ref, q_ref, k_ref, v_ref):
    count = w_ref.shape[1] // 3

    def weight(part):
        return jnp.concatenate([w_ref[r, part * count : (part + 1) * count, :] for r in range(w_ref.shape[0])], axis=0)

    cos, sin = cos_ref[...], sin_ref[...]
    q = outer_cols(n, weight(0))
    k = outer_cols(n, weight(1))
    for j in range(q.shape[1] // PAIR):
        cols = slice(j * PAIR, (j + 1) * PAIR)
        q_ref[:, cols] = (rope(q[:, cols], cos, sin) * (1.0 / HEAD_DIM**0.5)).astype(BF16)
        k_ref[:, cols] = rope(k[:, cols], cos, sin).astype(BF16)
    v_ref[...] = outer_cols(n, weight(2)).astype(BF16)


def norm_qkv_kernel(x_ref, gain_ref, w_ref, cos_ref, sin_ref, n_ref, q_ref, k_ref, v_ref):
    n = normed(x_ref[...].astype(F32), gain_ref[...]).astype(BF16)
    n_ref[...] = n
    write_qkv(n, w_ref, cos_ref, sin_ref, q_ref, k_ref, v_ref)


def only_qkv_kernel(n_ref, w_ref, cos_ref, sin_ref, q_ref, k_ref, v_ref):
    write_qkv(n_ref[...], w_ref, cos_ref, sin_ref, q_ref, k_ref, v_ref)


def project_qkv(rows_in, gain, pack, cos, sin):
    rows, width = rows_in.shape
    cols = pack.shape[0] * pack.shape[1] // 3
    block = 256
    row_spec = pl.BlockSpec((block, width), lambda i: (i, 0))
    out_spec = pl.BlockSpec((block, cols), lambda i: (i, 0))
    gain_spec = pl.BlockSpec((1, width), lambda i: (0, 0))
    w_spec = pl.BlockSpec(pack.shape, lambda i: (0, 0, 0))
    tab_spec = pl.BlockSpec((block, PAIR), lambda i: (i, 0))
    first = gain is not None
    return pl.pallas_call(
        norm_qkv_kernel if first else only_qkv_kernel,
        grid=(rows // block,),
        in_specs=[row_spec] + [gain_spec] * first + [w_spec, tab_spec, tab_spec],
        out_specs=[row_spec] * first + [out_spec] * 3,
        out_shape=[jax.ShapeDtypeStruct((rows, width), BF16)] * first + [jax.ShapeDtypeStruct((rows, cols), BF16)] * 3,
        compiler_params=pltpu.CompilerParams(vmem_limit_bytes=VMEM_LIMIT),
        cost_estimate=pl.CostEstimate(
            flops=8 * rows * width * cols, bytes_accessed=8 * rows * width + 6 * width * cols, transcendentals=0
        ),
        name="norm_qkv" if first else "qkv",
    )(*([rows_in] + [gain] * first + [pack, cos, sin]))


def pad_rows(dst, src):
    rows = src.shape[0]
    edge = jnp.zeros((HALF, PAIR), dst.dtype)
    dst[0:HALF, :] = edge
    dst[HALF : HALF + rows, :] = src
    dst[HALF + rows : rows + 2 * HALF, :] = edge


def split_lanes(src, first, second):
    lane = lax.broadcasted_iota(jnp.int32, src.shape, 1)
    zero = jnp.zeros_like(src)
    first[...] = jnp.where(lane < HEAD_DIM, src, zero)
    second[...] = jnp.where(lane < HEAD_DIM, zero, src)


def query_rows(i):
    return slice(i * QB, (i + 1) * QB)


def key_rows(i):
    return slice(i * QB, i * QB + KB)


def head_rows(h):
    return slice(h * HEAD_DIM, (h + 1) * HEAD_DIM)


def attend_kernel(q_ref, k_ref, v_ref, bias_ref, o_ref, p_ref, pad, k0, k1, vt):
    rows = q_ref.shape[0]
    pad_rows(pad, v_ref[...])
    vt[...] = pad[...].T
    pad_rows(pad, k_ref[...])
    split_lanes(pad[...], k0, k1)
    for start in range(0, rows // QB, STAGED):
        blocks = range(start, start + STAGED)
        units = [(i, h) for i in blocks for h in range(2)]
        q_t = {i: q_ref[query_rows(i), :].T for i in blocks}
        scores = [dot((k0, k1)[h][key_rows(i), :], q_t[i]) + bias_ref[i] for i, h in units]
        tops = [jnp.max(s, axis=0, keepdims=True) for s in scores]
        expos = [jnp.exp(s - top) for s, top in zip(scores, tops)]
        shares = [1.0 / jnp.sum(e, axis=0, keepdims=True) for e in expos]
        probs = [(e * share).astype(BF16) for e, share in zip(expos, shares)]
        outs = [dot(vt[head_rows(h), key_rows(i)], p) for (i, h), p in zip(units, probs)]
        for (i, h), p in zip(units, probs):
            p_ref[0, i, :, h * QB : (h + 1) * QB] = p
        for n, i in enumerate(blocks):
            o_ref[query_rows(i), :] = jnp.concatenate(outs[2 * n : 2 * n + 2], axis=0).astype(BF16).T


def attend(q, k, v, bias):
    rows, width = q.shape
    pairs, blocks = width // PAIR, rows // QB
    spec = pl.BlockSpec((rows, PAIR), lambda j: (0, j))
    padded = rows + 2 * HALF
    return pl.pallas_call(
        attend_kernel,
        grid=(pairs,),
        in_specs=[spec, spec, spec, pl.BlockSpec((blocks, KB, QB), lambda j: (0, 0, 0))],
        out_specs=[spec, pl.BlockSpec((1, blocks, KB, 2 * QB), lambda j: (j, 0, 0, 0))],
        out_shape=[
            jax.ShapeDtypeStruct((rows, width), BF16),
            jax.ShapeDtypeStruct((pairs, blocks, KB, 2 * QB), BF16),
        ],
        scratch_shapes=[pltpu.VMEM((padded, PAIR), BF16)] * 3 + [pltpu.VMEM((PAIR, padded), BF16)],
        compiler_params=pltpu.CompilerParams(vmem_limit_bytes=VMEM_LIMIT),
        cost_estimate=pl.CostEstimate(flops=2 * 10**9 * pairs, bytes_accessed=2 * rows * width * 8, transcendentals=0),
        name="attend",
    )(q, k, v, bias)


def swap_rows(v):
    quarter = HEAD_DIM // 2
    part = [v[i * quarter : (i + 1) * quarter, :] for i in range(4)]
    return jnp.concatenate([part[1], part[0], part[3], part[2]], axis=0)


def both_heads(v):
    lane = lax.broadcasted_iota(jnp.int32, v.shape, 1)
    zero = jnp.zeros_like(v)
    return jnp.concatenate([jnp.where(lane < HEAD_DIM, v, zero), jnp.where(lane < HEAD_DIM, zero, v)], axis=0)


def attend_back_kernel(
    q_ref, k_ref, v_ref, g_ref, p_ref, cos_ref, sin_ref, cos_t, sin_t, gq_ref, gk_ref, gv_ref, pad, v0, v1, kt, gk, gv
):
    rows = q_ref.shape[0]
    scale = 1.0 / HEAD_DIM**0.5
    pad_rows(pad, k_ref[...])
    kt[...] = pad[...].T
    pad_rows(pad, v_ref[...])
    split_lanes(pad[...], v0, v1)
    gk[...] = jnp.zeros_like(gk)
    gv[...] = jnp.zeros_like(gv)
    for start in range(0, rows // QB, STAGED_BACK):
        blocks = range(start, start + STAGED_BACK)
        units = [(i, h) for i in blocks for h in range(2)]
        g_t = {i: g_ref[query_rows(i), :].T for i in blocks}
        gps = [dot((v0, v1)[h][key_rows(i), :], g_t[i]) for i, h in units]
        probs = [p_ref[0, i, :, h * QB : (h + 1) * QB].astype(F32) for i, h in units]
        sums = [jnp.sum(p * gp, axis=0, keepdims=True) for p, gp in zip(probs, gps)]
        grads = [(p * (gp - total)).astype(BF16) for p, gp, total in zip(probs, gps, sums)]
        outs = [dot(kt[head_rows(h), key_rows(i)], gs) for (i, h), gs in zip(units, grads)]
        gks = [
            dot(jnp.concatenate(grads[2 * n : 2 * n + 2], axis=1), both_heads(q_ref[query_rows(i), :]))
            for n, i in enumerate(blocks)
        ]
        gvs = [dot(p_ref[0, i], both_heads(g_ref[query_rows(i), :])) for i in blocks]
        for n, i in enumerate(blocks):
            at = query_rows(i)
            gk[key_rows(i), :] += gks[n]
            gv[key_rows(i), :] += gvs[n]
            gq = jnp.concatenate(outs[2 * n : 2 * n + 2], axis=0) * scale
            gq_ref[at, :] = (gq * cos_t[:, at] - swap_rows(gq) * sin_t[:, at]).astype(BF16).T
    gk_ref[...] = rope(gk[HALF : HALF + rows, :], cos_ref[...], -sin_ref[...]).astype(BF16)
    gv_ref[...] = gv[HALF : HALF + rows, :].astype(BF16)


def attend_back(q, k, v, g, prob, cos, sin, cos_t, sin_t):
    rows, width = q.shape
    pairs, blocks = width // PAIR, rows // QB
    spec = pl.BlockSpec((rows, PAIR), lambda j: (0, j))
    tab_spec = pl.BlockSpec((rows, PAIR), lambda j: (0, 0))
    tab_t_spec = pl.BlockSpec((PAIR, rows), lambda j: (0, 0))
    padded = rows + 2 * HALF
    return pl.pallas_call(
        attend_back_kernel,
        grid=(pairs,),
        in_specs=[spec] * 4
        + [pl.BlockSpec((1, blocks, KB, 2 * QB), lambda j: (j, 0, 0, 0)), tab_spec, tab_spec, tab_t_spec, tab_t_spec],
        out_specs=[spec] * 3,
        out_shape=[jax.ShapeDtypeStruct((rows, width), BF16)] * 3,
        scratch_shapes=[pltpu.VMEM((padded, PAIR), BF16)] * 3
        + [pltpu.VMEM((PAIR, padded), BF16)]
        + [pltpu.VMEM((padded, PAIR), F32)] * 2,
        compiler_params=pltpu.CompilerParams(vmem_limit_bytes=VMEM_LIMIT),
        cost_estimate=pl.CostEstimate(flops=8 * 10**9, bytes_accessed=10**7, transcendentals=0),
        name="attend_back",
    )(q, k, v, g, prob, cos, sin, cos_t, sin_t)


def ring(step):
    size = lax.axis_size("tensor")
    return [(i, (i + step) % size) for i in range(size)]


def plane(dy, dz, dc=0):
    size = lax.axis_size("dp")
    out = []
    for i in range(size):
        y, z, c = i // 8, (i // 2) % 4, i % 2
        out.append((i, (((y + dy) % 4) * 4 + (z + dz) % 4) * 2 + (c + dc) % 2))
    return out


def place_pair_kernel(core_ref, own_ref, mine_ref, other_ref, out_ref):
    half = mine_ref.shape[1]
    out_ref[0] = own_ref[...]
    core = core_ref[0]
    out_ref[1, :, pl.ds(pl.multiple_of(core * half, half), half)] = mine_ref[...].astype(BF16)
    out_ref[1, :, pl.ds(pl.multiple_of((1 - core) * half, half), half)] = other_ref[...].astype(BF16)


def place_rest_kernel(core_ref, mine_ref, other_ref, head_ref, tail_ref, other_head_ref, other_tail_ref, out_ref):
    rows, half = mine_ref.shape
    core = core_ref[0]
    mine_at = pl.ds(pl.multiple_of(core * half, half), half)
    other_at = pl.ds(pl.multiple_of((1 - core) * half, half), half)
    out_ref[0, :, mine_at] = mine_ref[...].astype(BF16)
    out_ref[0, :, other_at] = other_ref[...].astype(BF16)
    out_ref[1, 0 : rows // 2, mine_at] = head_ref[...].astype(BF16)
    out_ref[1, rows // 2 : rows, mine_at] = tail_ref[...].astype(BF16)
    out_ref[1, 0 : rows // 2, other_at] = other_head_ref[...].astype(BF16)
    out_ref[1, rows // 2 : rows, other_at] = other_tail_ref[...].astype(BF16)


def place(kernel, core, rows, lanes, args, name):
    whole = pl.BlockSpec(memory_space=pltpu.VMEM)
    return pl.pallas_call(
        kernel,
        in_specs=[pl.BlockSpec(memory_space=pltpu.SMEM)] + [whole] * len(args),
        out_specs=whole,
        out_shape=jax.ShapeDtypeStruct((2, rows, lanes), BF16),
        compiler_params=pltpu.CompilerParams(vmem_limit_bytes=VMEM_LIMIT),
        name=name,
    )(core[None].astype(jnp.int32), *args)


def gather_attn(w_query, w_key, w_value, meanwhile):
    core = lax.axis_index("dp") % 2
    own = jnp.concatenate([w_query.T, w_key.T, w_value.T], axis=0)
    rows, lanes = own.shape
    half = lanes // 2
    mine = lax.dynamic_slice_in_dim(own, core * half, half, 1).astype(F32)
    swap = plane(0, 0, 1)
    after = lax.ppermute(mine, "tensor", ring(-1))
    before = lax.ppermute(mine, "tensor", ring(1))
    after, before, meanwhile = lax.optimization_barrier((after, before, meanwhile))
    head = lax.ppermute(after[: rows // 2], "tensor", ring(-1))
    tail = lax.ppermute(before[rows // 2 :], "tensor", ring(1))
    other_after = lax.ppermute(after, "dp", swap)
    other_before = lax.ppermute(before, "dp", swap)
    first = place(place_pair_kernel, core, rows, lanes, (own, after, other_after), "place_pair")

    def rest(behind):
        late_head, late_tail, behind = lax.optimization_barrier((head, tail, behind))
        other_head = lax.ppermute(late_head, "dp", swap)
        other_tail = lax.ppermute(late_tail, "dp", swap)
        args = (before, other_before, late_head, late_tail, other_head, other_tail)
        return place(place_rest_kernel, core, rows, lanes, args, "place_rest"), behind

    return first, rest, meanwhile


def both_ways(block, axis, move):
    return lax.ppermute(block, axis, move(1)), lax.ppermute(block, axis, move(-1))


def far_of(back, on, axis, move):
    half = back.shape[0] // 16 * 8
    parts = [lax.ppermute(on[:half], axis, move(-1)), lax.ppermute(back[half:], axis, move(1))]
    return jnp.concatenate(parts, axis=0)


def mlp_piece(w_in, w_gate, w_down, w_attn_out):
    core, z, y = lax.axis_index("dp") % 2, ring_place("z"), ring_place("y")
    half = w_down.shape[1] // 2
    count, short = w_down.shape[0] // 4, w_attn_out.shape[0] // 4
    parts = [
        lax.dynamic_slice(w_in.T, (z * count, core * half), (count, half)),
        lax.dynamic_slice(w_gate.T, (z * count, core * half), (count, half)),
        lax.dynamic_slice(w_down, (y * count, core * half), (count, half)),
        lax.dynamic_slice(w_attn_out, (y * short, core * half), (short, half)),
    ]
    return jnp.concatenate(parts, axis=0).astype(F32)


def mlp_kernel(
    at_ref,
    z_mine,
    z_other,
    y_mine,
    y_other,
    own_in,
    own_gate,
    own_down,
    own_out,
    x_ref,
    mix0_ref,
    mix1_ref,
    cot_ref,
    live_ref,
    gain_ref,
    out_ref,
    resid_ref,
    low_ref,
    mixg_ref,
    n_ref,
    hid_ref,
    gug_ref,
    go_ref,
    gain_out_ref,
    up_w,
    gt_w,
    dn_w,
    o_w,
):
    step = pl.program_id(0)
    core, z, y = at_ref[0], at_ref[1], at_ref[2]
    half = z_mine.shape[3]
    loads = 3
    count, short = own_in.shape[0] // 4, own_out.shape[0] // 4

    @pl.when(step == 0)
    def _():
        for dst, own in ((up_w, own_in), (gt_w, own_gate), (dn_w, own_down), (o_w, own_out)):
            dst[0 : own.shape[0], :] = own[...]

    for slot in range(loads):

        @pl.when(step == slot)
        def _(slot=slot):
            for src, lanes, place, dst, first, rows in (
                (z_mine, core, z, up_w, 0, count),
                (z_other, 1 - core, z, up_w, 0, count),
                (z_mine, core, z, gt_w, count, count),
                (z_other, 1 - core, z, gt_w, count, count),
                (y_mine, core, y, dn_w, 0, count),
                (y_other, 1 - core, y, dn_w, 0, count),
                (y_mine, core, y, o_w, count, short),
                (y_other, 1 - core, y, o_w, count, short),
            ):
                quarters = [src[lax.rem(place - j + 4, 4), 0, first : first + rows, :] for j in range(4)]
                block = jnp.concatenate(quarters, axis=0).astype(BF16)
                start = (slot + 1) * 4 * rows
                dst[start : start + 4 * rows, pl.ds(pl.multiple_of(lanes * half, half), half)] = block

    @pl.when(step >= loads)
    def _():
        split = mix0_ref.shape[1]
        gain = gain_ref[...]
        resid = x_ref[...].astype(F32) + dot(mix0_ref[...], o_w[0:split, :]) + dot(mix1_ref[...], o_w[split:, :])
        centre = jnp.mean(resid, axis=-1, keepdims=True)
        centred = resid - centre
        inv = lax.rsqrt(jnp.mean(centred * centred, axis=-1, keepdims=True) + 1e-05)
        unit = centred * inv
        n = (unit * gain).astype(BF16)
        n_ref[...] = n
        up = outer_cols(n, up_w[...])
        gate = outer_cols(n, gt_w[...])
        go = cot_ref[...].astype(F32) * live_ref[...]
        go_low = go.astype(BF16)
        go_ref[...] = go_low
        gh = outer_cols(go_low, dn_w[...])
        bell = jnp.exp(up * up * -0.5)
        t = 1.0 / (1.0 + (0.3275911 * 0.7071067811865476) * jnp.abs(up))
        poly = t * (
            0.5 * 0.254829592
            + t * (0.5 * -0.284496736 + t * (0.5 * 1.421413741 + t * (0.5 * -1.453152027 + t * (0.5 * 1.061405429))))
        )
        tail = poly * bell
        cdf = jnp.where(up >= 0.0, 1.0 - tail, tail)
        act = up * cdf
        slope = cdf + up * bell * 0.3989422804014327
        hid = (act * gate).astype(BF16)
        gup = (gh * gate * slope).astype(BF16)
        ggt = (gh * act).astype(BF16)
        own = hid_ref.shape[1]
        hid_ref[...] = hid[:, :own]
        gug_ref[...] = jnp.concatenate([gup[:, :own], ggt[:, :own]], axis=1)
        out_ref[...] = (resid + dot(hid, dn_w[...])).astype(BF16)
        gn = dot(gup, up_w[...]) + dot(ggt, gt_w[...])
        scaled = gn * gain
        first = jnp.mean(scaled, axis=-1, keepdims=True)
        second = jnp.mean(scaled * unit, axis=-1, keepdims=True)
        grad = go + inv * (scaled - first - unit * second)
        resid_ref[...] = grad
        low = grad.astype(BF16)
        low_ref[...] = low
        mixg_ref[...] = outer_cols(low, o_w[...]).astype(BF16)
        terms = jnp.sum(gn * unit, axis=0, keepdims=True)

        @pl.when(step == loads)
        def _():
            gain_out_ref[...] = terms

        @pl.when(step > loads)
        def _():
            gain_out_ref[...] += terms


def mlp(gathered, own, tokens, mix0, mix1, cotangent, live, gain):
    rows, width = tokens.shape
    block, loads = 256, 3
    ff_own = own[0].shape[0]
    ff = 4 * ff_own
    place = jnp.stack([lax.axis_index("dp") % 2, ring_place("z"), ring_place("y")]).astype(jnp.int32)

    def at_row(i, _):
        return (jnp.maximum(i - loads, 0), 0)

    def from_ranks(array):
        return pl.BlockSpec((4, 1) + array.shape[2:], lambda i, _: (0, jnp.minimum(i, loads - 1), 0, 0))

    def whole(array):
        return pl.BlockSpec(array.shape, lambda i, _: (0, 0))

    def row(cols):
        return pl.BlockSpec((block, cols), at_row)

    def fixed(i, _):
        return (0, 0)

    def shape(cols, kind):
        return jax.ShapeDtypeStruct((rows, cols), kind)

    split = mix0.shape[1]
    return pl.pallas_call(
        mlp_kernel,
        grid_spec=pltpu.PrefetchScalarGridSpec(
            num_scalar_prefetch=1,
            grid=(loads + rows // block,),
            in_specs=[
                *[from_ranks(array) for array in gathered],
                *[whole(array) for array in own],
                row(width),
                row(split),
                row(width - split),
                row(width),
                row(1),
                pl.BlockSpec((1, width), fixed),
            ],
            out_specs=[
                row(width),
                row(width),
                row(width),
                row(width),
                row(width),
                row(ff_own),
                row(2 * ff_own),
                row(width),
                pl.BlockSpec((1, width), fixed),
            ],
            scratch_shapes=[
                pltpu.VMEM((ff, width), BF16),
                pltpu.VMEM((ff, width), BF16),
                pltpu.VMEM((ff, width), BF16),
                pltpu.VMEM((width, width), BF16),
            ],
        ),
        out_shape=[
            shape(width, BF16),
            shape(width, F32),
            shape(width, BF16),
            shape(width, BF16),
            shape(width, BF16),
            shape(ff_own, BF16),
            shape(2 * ff_own, BF16),
            shape(width, BF16),
            jax.ShapeDtypeStruct((1, width), F32),
        ],
        compiler_params=pltpu.CompilerParams(vmem_limit_bytes=VMEM_LIMIT),
        cost_estimate=pl.CostEstimate(flops=12 * rows * width * ff, bytes_accessed=40 * 10**6, transcendentals=0),
        name="mlp",
    )(place, *gathered, *own, tokens, mix0, mix1, cotangent, live, gain)


def finish_kernel(x_ref, grad_ref, gain_ref, *refs):
    parts, weights, (out_ref, gain_out_ref) = refs[:6], refs[6:8], refs[8:]
    total = None
    for half in range(2):
        w_ref = weights[half]
        count = w_ref.shape[1] // 3
        for part in range(3):
            w = jnp.concatenate([w_ref[r, part * count : (part + 1) * count, :] for r in range(w_ref.shape[0])], axis=0)
            term = dot(parts[half * 3 + part][...], w)
            total = term if total is None else total + term
    back, terms = norm_back(x_ref[...].astype(F32), gain_ref[...], total)
    out_ref[...] = grad_ref[...] + back
    terms = jnp.sum(terms, axis=0, keepdims=True)

    @pl.when(pl.program_id(0) == 0)
    def _():
        gain_out_ref[...] = terms

    @pl.when(pl.program_id(0) > 0)
    def _():
        gain_out_ref[...] += terms


def finish(tokens, grad_resid, gain, parts, weights):
    rows, width = tokens.shape
    block = 256

    def row(cols):
        return pl.BlockSpec((block, cols), lambda i: (i, 0))

    fixed = pl.BlockSpec((1, width), lambda i: (0, 0))
    return pl.pallas_call(
        finish_kernel,
        grid=(rows // block,),
        in_specs=[row(width), row(width), fixed]
        + [row(p.shape[1]) for p in parts]
        + [pl.BlockSpec(w.shape, lambda i: (0, 0, 0)) for w in weights],
        out_specs=[row(width), fixed],
        out_shape=[jax.ShapeDtypeStruct((rows, width), F32), jax.ShapeDtypeStruct((1, width), F32)],
        compiler_params=pltpu.CompilerParams(vmem_limit_bytes=VMEM_LIMIT),
        cost_estimate=pl.CostEstimate(flops=8 * 10**9, bytes_accessed=10**7, transcendentals=0),
        name="finish",
    )(tokens, grad_resid, gain, *parts, *weights)


def rows_at(array, place, count):
    return lax.dynamic_slice_in_dim(array, place * count, count, 0)


def halves_summed(pairs):
    core = lax.axis_index("dp") % 2

    def half(at):
        lanes = pairs[0][1].shape[1] // 2
        terms = [inner_rows(a, lax.dynamic_slice_in_dim(b, at * lanes, lanes, 1)) for a, b in pairs]
        return jnp.concatenate(terms, axis=0) if len(terms) > 1 else terms[0]

    return half(core) + lax.ppermute(half(1 - core), "dp", plane(0, 0, 1))


def whole_of(done):
    got = lax.ppermute(done, "dp", plane(0, 0, 1))
    first = lax.axis_index("dp") % 2 == 0
    return jnp.concatenate([jnp.where(first, done, got), jnp.where(first, got, done)], axis=1)


def ring_place(axis):
    at = lax.axis_index("dp")
    return at // 8 if axis == "y" else (at // 2) % 4


def ring_move(axis, d):
    return plane(d, 0) if axis == "y" else plane(0, d)


def split_ring(half, axis):
    quarter = half.shape[0] // 4
    place = ring_place(axis)
    return [rows_at(half, (place + d) % 4, quarter) for d in range(4)]


def sum_ring(blocks, axis):
    total = blocks[0]
    for d in (1, 2, 3):
        total = total + lax.ppermute(blocks[d], "dp", ring_move(axis, d))
    return total


def in_order(blocks, axis):
    place = ring_place(axis)
    return jnp.concatenate([lax.select_n(lax.rem(place - j + 4, 4), *blocks) for j in range(4)], axis=0)


def far_by_half(blocks, axis):
    half = blocks[2].shape[0] // 16 * 8
    head = lax.ppermute(blocks[2][:half], "dp", ring_move(axis, 1))
    tail = lax.ppermute(blocks[2][half:], "dp", ring_move(axis, -1))
    after = jnp.concatenate([blocks[1][:half] + head, blocks[1][half:]], axis=0)
    before = jnp.concatenate([blocks[3][:half], blocks[3][half:] + tail], axis=0)
    return blocks[0], after, before


def sum_neighbours(parts, axis):
    own, after, before = parts
    return own + lax.ppermute(after, "dp", ring_move(axis, 1)) + lax.ppermute(before, "dp", ring_move(axis, -1))


def spread_ring(block, axis):
    return [block] + [lax.ppermute(block, "dp", ring_move(axis, d)) for d in (1, 2, 3)]


def spread_ring_twice(block, axis):
    half = block.shape[0] // 16 * 8
    before = lax.ppermute(block, "dp", ring_move(axis, 1))
    after = lax.ppermute(block, "dp", ring_move(axis, -1))
    head = lax.ppermute(before[:half], "dp", ring_move(axis, 1))
    tail = lax.ppermute(after[half:], "dp", ring_move(axis, -1))
    return [block, before, jnp.concatenate([head, tail], axis=0), after]


def body(
    tokens,
    cotangent,
    seq_len,
    seq_slot,
    attn_gain,
    w_query,
    w_key,
    w_value,
    w_attn_out,
    mlp_gain,
    w_in,
    w_gate,
    w_down,
):
    rows, width = tokens.shape
    heads_cols = w_query.shape[1]
    per_group = 2
    slots = lax.axis_index("dp") * per_group + jnp.arange(per_group, dtype=jnp.int32)
    lengths = jnp.sum(jnp.where(seq_slot[None, :] == slots[:, None], seq_len[None, :], 0), axis=1)
    end0, end1 = lengths[0], lengths[0] + lengths[1]

    def segment_of(index):
        return (index >= end0).astype(jnp.int32) + (index >= end1).astype(jnp.int32)

    index = lax.broadcasted_iota(jnp.int32, (rows, PAIR), 0)
    position = index - jnp.where(index >= end1, end1, jnp.where(index >= end0, end0, 0))
    lane = lax.broadcasted_iota(jnp.int32, (rows, PAIR), 1)
    width_half = HEAD_DIM // 2
    frequency = 10000.0 ** (-(jnp.arange(width_half, dtype=F32) * 2.0 / HEAD_DIM))
    frequency = jnp.tile(frequency, PAIR // width_half)
    phase = position.astype(F32) * frequency[None, :]
    cos = jnp.cos(phase)
    sin = jnp.where(lane % HEAD_DIM < width_half, -1.0, 1.0) * jnp.sin(phase)
    shape = (rows // QB, KB, QB)
    block_at = lax.broadcasted_iota(jnp.int32, shape, 0) * QB
    row_at = block_at + lax.broadcasted_iota(jnp.int32, shape, 2)
    col_at = block_at + lax.broadcasted_iota(jnp.int32, shape, 1) - HALF
    allowed = (
        (segment_of(row_at) == segment_of(col_at))
        & (jnp.abs(row_at - col_at) <= HALF)
        & (col_at >= 0)
        & (col_at < rows)
    )
    bias = jnp.where(allowed, 0.0, -1e30).astype(F32)
    live = (jnp.arange(rows, dtype=jnp.int32) < end1).astype(F32)

    def along_z(d):
        return plane(0, d)

    def along_y(d):
        return plane(d, 0)

    piece = mlp_piece(w_in, w_gate, w_down, w_attn_out)
    piece_back, piece_on = both_ways(piece, "tensor", ring)
    piece_far = far_of(piece_back, piece_on, "tensor", ring)
    cut = 2 * (w_in.shape[1] // 4)
    by_z = jnp.concatenate([piece_on[:cut], piece_back[:cut], piece_far[:cut]], axis=0)
    by_y = jnp.concatenate([piece_on[cut:], piece_back[cut:], piece_far[cut:]], axis=0)
    weights0, rest, (cos, sin, cos_t, sin_t, bias, by_z, by_y) = gather_attn(
        w_query, w_key, w_value, (cos, sin, cos.T, sin.T, bias, by_z, by_y)
    )
    z_back, z_on = both_ways(by_z, "dp", along_z)
    y_back, y_on = both_ways(by_y, "dp", along_y)
    gain1 = attn_gain[None, :]
    normed1, *qkv0 = project_qkv(tokens, gain1, weights0, cos, sin)
    mix0, prob0 = attend(*qkv0, bias)
    z_back, z_on, y_back, y_on, mix0 = lax.optimization_barrier((z_back, z_on, y_back, y_on, mix0))
    weights1, mix0 = rest(mix0)
    weights1, z_back, z_on, y_back, y_on = lax.optimization_barrier((weights1, z_back, z_on, y_back, y_on))
    z_far = far_of(z_back, z_on, "dp", along_z)
    y_far = far_of(y_back, y_on, "dp", along_y)
    weights_attn = (weights0, weights1)
    qkv1 = project_qkv(normed1, None, weights_attn[1], cos, sin)
    z_far, y_far, qkv1 = lax.optimization_barrier((z_far, y_far, qkv1))
    z_mine = jnp.concatenate([by_z, z_back, z_far, z_on], axis=0)
    y_mine = jnp.concatenate([by_y, y_back, y_far, y_on], axis=0)
    z_mine, y_mine, qkv1 = lax.optimization_barrier((z_mine, y_mine, qkv1))
    z_other = lax.ppermute(z_mine, "dp", plane(0, 0, 1))
    y_other = lax.ppermute(y_mine, "dp", plane(0, 0, 1))
    mix1, prob1 = attend(*qkv1, bias)
    gathered = [a.reshape(4, 3, -1, a.shape[1]) for a in (z_mine, z_other, y_mine, y_other)]
    own_mlp = [w_in.T, w_gate.T, w_down, w_attn_out]
    (
        mixed_out,
        grad_resid,
        grad_resid_low,
        grad_mix,
        normed2,
        hidden,
        grad_up_gate,
        grad_out_low,
        gain2_sum,
    ) = mlp(gathered, own_mlp, tokens, mix0, mix1, cotangent, live[:, None], mlp_gain[None, :])
    ff_cols = w_in.shape[1]
    spare = jnp.zeros((rows, -(3 * ff_cols + heads_cols) % 128), BF16)
    early = halves_summed(
        [
            (grad_up_gate, normed2),
            (hidden, grad_out_low),
            (jnp.concatenate([mix0[:, :heads_cols], spare], axis=1), grad_resid_low),
        ]
    )
    early = split_ring(early, "y")
    early, grad_mix = lax.optimization_barrier((early, grad_mix))
    split = mix0.shape[1]
    tables = (cos, sin, cos_t, sin_t)
    back0 = attend_back(*qkv0, grad_mix[:, :split], prob0, *tables)
    spare = jnp.zeros((rows, -(3 * heads_cols) % 128), BF16)
    early, back0 = lax.optimization_barrier((far_by_half(early, "y"), back0))
    own_grads = jnp.concatenate([g[:, :heads_cols] for g in back0] + [spare], axis=1)
    late = split_ring(halves_summed([(own_grads, normed1)]), "z")
    early, late, next_in = lax.optimization_barrier((early, late, grad_mix[:, split:]))
    back1 = attend_back(*qkv1, next_in, prob1, *tables)
    late, back1 = lax.optimization_barrier((far_by_half(late, "z"), back1))
    grad_tokens, gain1_sum = finish(tokens, grad_resid, gain1, [*back0, *back1], weights_attn)
    early = split_ring(sum_neighbours(early, "y"), "z")
    late = split_ring(sum_neighbours(late, "z"), "y")
    early, late = lax.optimization_barrier((early, late))
    early, late = lax.optimization_barrier((sum_ring(early, "z"), sum_ring(late, "y")))
    lanes = width // 2
    small = jnp.concatenate([gain1_sum[0], gain2_sum[0]])
    small = jnp.pad(small, (0, 8 * lanes - small.shape[0])).reshape(8, lanes)
    got_early = spread_ring(early, "z")
    got_late = spread_ring(jnp.concatenate([late, small], axis=0), "y")
    count = late.shape[0]
    small = sum(g[count:] for g in got_late)
    early = in_order(got_early, "z")
    late = in_order([g[:count] for g in got_late], "y")
    early, late, small = lax.optimization_barrier((early, late, small))
    got_late = spread_ring(jnp.concatenate([late, small], axis=0), "z")
    got_early = spread_ring_twice(early, "y")
    count = late.shape[0]
    small = sum(g[count:] for g in got_late)
    late = in_order([g[:count] for g in got_late], "z")
    early = in_order(got_early, "y")
    count = late.shape[0]
    late = whole_of(jnp.concatenate([late, small], axis=0))
    small = (late[count:, :lanes] + late[count:, lanes:]).reshape(-1)
    early = whole_of(early)
    return (
        mixed_out,
        grad_tokens,
        small[:width],
        late[:heads_cols].T,
        late[heads_cols : 2 * heads_cols].T,
        late[2 * heads_cols : 3 * heads_cols].T,
        early[3 * ff_cols : 3 * ff_cols + heads_cols],
        small[width : 2 * width],
        early[:ff_cols].T,
        early[ff_cols : 2 * ff_cols].T,
        early[2 * ff_cols : 3 * ff_cols],
    )


def solution(mesh):
    rows, cols, all_of = P("dp", None), P(None, "tensor"), P()
    tall = P("tensor", None)
    return jax.shard_map(
        body,
        mesh=mesh,
        in_specs=(rows, rows, all_of, all_of, all_of, cols, cols, cols, tall, all_of, cols, cols, tall),
        out_specs=(rows, rows, all_of, cols, cols, cols, tall, all_of, cols, cols, tall),
        check_vma=False,
    )
```
